32 devices in a mesh: dom: 2 (over y), expert: 4 (over z), dp: 2 (over x), sub: 2 (over core).
Axes of the slice: x: 2, y: 2, z: 4, core: 2. Of those that a mesh axis runs over, the one named last changes fastest.
Arguments:
- tokens: bfloat16 [1024, 2048], P(('dom', 'expert', 'dp'), 'sub'), parts along dimension 0, may hold values from -6 to 6
- out_grad: bfloat16 [1024, 2048], P(('dom', 'expert', 'dp'), 'sub'), parts along dimension 0, may hold values from -6 to 6
- gates: float32 [1024, 8], P(('dom', 'expert', 'dp')), parts along dimension 0, may hold values from 0.1 to 1
- expert_ids: int32 [1024, 8], P(('dom', 'expert', 'dp')), parts along dimension 0, may hold values from 0 to 63, as said below
- slots: int32 [1024, 8], P(('dom', 'expert', 'dp')), parts along dimension 0, may hold values from 0 to 9, as said below
- gate_weight: bfloat16 [64, 2048, 768], P('expert', 'dp', 'sub'), may hold values from -0.125 to 0.125
- up_weight: bfloat16 [64, 2048, 768], P('expert', 'dp', 'sub'), may hold values from -0.125 to 0.125
- down_weight: bfloat16 [64, 768, 2048], P('expert', 'sub', 'dp'), may hold values from -0.21875 to 0.21875
Outputs:
- scores: float32 [128, 768], P(('dom', 'expert'), 'sub'), parts along dimension 0
- input_grad: bfloat16 [1024, 2048], P(('dom', 'expert', 'dp'), 'sub'), parts along dimension 0
The draws below stay inside these ranges and needn't reach their ends.
There are 2 independent parts, one for each index of `dom`. The reference program is written for one: setup_inputs(seed, part) draws one part's arguments, and reference() takes and returns one part's arrays. A program takes and returns all parts, laid end to end along the dimension named above; an argument that names none is the same for every part. Nothing has to cross between parts.
Inputs may be any that keep to these rules, and one draw needn't show every extreme that they name: `expert_ids`: A row names 8 different experts; in each aligned block of 64 rows (the rows of one index pair of expert and dp) no expert is named by more than 10 rows, every expert is named, and some expert is named by exactly 10 rows in every block. Within one aligned block of 64 rows, the routes to one expert have different slots.
All inputs are finite; a program needn't handle non-finite values.
Results may differ from the reference program's by a relative error of at most 0.0085.
Values may be sent and summed in bfloat16 or wider, within the bound.
No kernel may reach another device: no remote copies, remote signals or barrier semaphores. Data moves between devices by JAX's collectives and lax.ppermute only.
A program may use at most 256 MiB of HBM per device.

```python
import math
import jax
import jax.numpy as jnp
from jax import lax

D = 2048
FF = 768
LOCAL_EXPERTS = 64
TOPK = 8
TOK_DEV = 64
CAP = 10
TOKENS = 512
N_SUB = 2


def route_table(key):
    block_count = TOKENS // TOK_DEV
    subkeys = jax.random.split(key, 5)
    average = TOK_DEV * TOPK // LOCAL_EXPERTS
    heaviest_expert = jax.random.randint(subkeys[0], (), 0, LOCAL_EXPERTS)
    favored_experts = jax.random.randint(subkeys[1], (LOCAL_EXPERTS,), 0, 4)
    random_noise = jax.random.randint(subkeys[2], (block_count, LOCAL_EXPERTS), 0, 3)
    expert_total = jnp.arange(LOCAL_EXPERTS, dtype=jnp.int32)
    extra_boost = 100 * (expert_total == heaviest_expert).astype(jnp.int32)
    expert_order = (favored_experts[None, :] + random_noise + extra_boost[None, :]) * LOCAL_EXPERTS + expert_total[None, :]
    ordering = jnp.argsort(-expert_order, axis=1, stable=True)
    standing = jnp.argsort(ordering, axis=1, stable=True)
    quarter = LOCAL_EXPERTS // 4
    per_expert = jnp.where(standing < quarter, average + 2, jnp.where(standing >= 3 * quarter, average - 2, average))
    starts = jnp.cumsum(per_expert, axis=1) - per_expert
    position = jnp.arange(TOK_DEV * TOPK, dtype=jnp.int32)
    holders = jnp.sum((starts[:, None, :] <= position[None, :, None]).astype(jnp.int32), axis=2) - 1
    offset = position[None, :] - jnp.take_along_axis(starts, holders, axis=1)
    rotate = jax.random.randint(subkeys[3], (block_count, LOCAL_EXPERTS), 0, CAP)
    placed = (offset + jnp.take_along_axis(rotate, holders, axis=1)) % CAP
    holders = holders.reshape(block_count, TOPK, TOK_DEV).transpose(0, 2, 1)
    placed = placed.reshape(block_count, TOPK, TOK_DEV).transpose(0, 2, 1)
    shuffle = jax.vmap(lambda sub_key: jax.random.permutation(sub_key, TOK_DEV))(jax.random.split(subkeys[4], block_count))
    holders = jnp.take_along_axis(holders, shuffle[:, :, None], axis=1)
    placed = jnp.take_along_axis(placed, shuffle[:, :, None], axis=1)
    return (holders.reshape(TOKENS, TOPK).astype(jnp.int32), placed.reshape(TOKENS, TOPK).astype(jnp.int32))


def draw_expert_ids(key, part):
    holders, placed = route_table(key)
    return holders


def draw_slots(key, part):
    holders, placed = route_table(key)
    return placed


def block_scale(own_key, dims, pieces, low, largest):
    level, own = 1.0, jax.random.fold_in(own_key, 6)
    for dim, parts in pieces:
        heights = jnp.exp(jax.random.uniform(jax.random.fold_in(own, dim), (parts,), jnp.float32, low / len(pieces), largest / len(pieces)))
        level = level * jnp.repeat(heights, dims[dim] // parts).reshape([-1 if axis == dim else 1 for axis in range(len(dims))])
    return level


def bell_draw(rng, extent, spread, bound, cuts=(), kind=jnp.bfloat16):
    array = jax.random.normal(rng, extent, jnp.float32) * spread
    if len(cuts) > 0:
        array = block_scale(rng, extent, cuts, -0.22, 0.18) * array
    return jnp.clip(array, min=-bound, max=bound).astype(kind)


def setup_inputs(seed: int = 0, part: int = 0) -> dict:
    seeds = jax.random.split(jax.random.key(seed), 9)
    part_keys = jax.random.split(jax.random.fold_in(seeds[8], part), 9)
    return {
        "tokens": bell_draw(part_keys[0], (TOKENS, D), 1.0, 6.0, ((0, 8), (1, 2))),
        "out_grad": bell_draw(part_keys[1], (TOKENS, D), 1.0, 6.0, ((0, 8), (1, 2))),
        "gates": jnp.clip(jnp.exp(math.log(1.0) - 2.3025851 * jax.random.uniform(part_keys[2], (TOKENS, TOPK), jnp.float32) ** block_scale(part_keys[2], (TOKENS, TOPK), ((0, 8),), -0.2, 0.2)), 0.1, 1.0),
        "expert_ids": draw_expert_ids(jax.random.fold_in(jax.random.fold_in(seeds[8], part), 71), part),
        "slots": draw_slots(jax.random.fold_in(jax.random.fold_in(seeds[8], part), 71), part),
        "gate_weight": bell_draw(seeds[5], (LOCAL_EXPERTS, D, FF), D ** -0.5, 0.125, ((0, 4), (1, 2), (2, 2))),
        "up_weight": bell_draw(seeds[6], (LOCAL_EXPERTS, D, FF), D ** -0.5, 0.125, ((0, 4), (1, 2), (2, 2))),
        "down_weight": bell_draw(seeds[7], (LOCAL_EXPERTS, FF, D), FF ** -0.5, 0.21875, ((0, 4), (1, 2), (2, 2))),
    }


def reference(tokens, out_grad, gates, expert_ids, slots, gate_weight, up_weight, down_weight):
    block_count = TOKENS // TOK_DEV
    row_count = block_count * CAP
    half_width = FF // N_SUB
    routes = jnp.arange(TOKENS * TOPK, dtype=jnp.int32)
    owners = routes // TOPK
    placed = (owners // TOK_DEV) * CAP + slots.reshape(-1)
    flat_ids = expert_ids.reshape(-1)
    flat_gates = gates.reshape(-1)

    def one_expert(totals, expert):
        chosen = flat_ids == expert
        picked = jnp.nonzero(chosen, size=row_count, fill_value=0)[0].astype(jnp.int32)
        filled = jnp.arange(row_count, dtype=jnp.int32) < jnp.sum(chosen.astype(jnp.int32))
        senders = owners[picked]
        target = jnp.where(filled, placed[picked], row_count)
        x_block = jnp.zeros((row_count, D), jnp.bfloat16).at[target].add(tokens[senders], mode="drop")
        scaled = (flat_gates[picked][:, None] * out_grad[senders].astype(jnp.float32)).astype(jnp.bfloat16)
        grad_block = jnp.zeros((row_count, D), jnp.bfloat16).at[target].add(scaled, mode="drop")
        gate_mat = gate_weight[expert]
        up_mat = up_weight[expert]
        down_mat = down_weight[expert]
        gate_pre = jnp.dot(x_block, gate_mat, preferred_element_type=jnp.float32)
        up_pre = jnp.dot(x_block, up_mat, preferred_element_type=jnp.float32)
        hidden_grad = jnp.dot(grad_block, down_mat.T, preferred_element_type=jnp.float32)
        gating = jax.nn.sigmoid(gate_pre)
        activated = gate_pre * gating
        hidden = activated * up_pre
        channel = jnp.sum(hidden * hidden_grad, axis=0)
        gate_grad = (hidden_grad * up_pre * gating * (1.0 + gate_pre * (1.0 - gating))).astype(jnp.bfloat16)
        up_grad = (hidden_grad * activated).astype(jnp.bfloat16)
        row_grad = jnp.zeros((row_count, D), jnp.float32)
        for block_index in range(N_SUB):
            lower = block_index * half_width
            upper = lower + half_width
            piece_out = jnp.dot(gate_grad[:, lower:upper], gate_mat[:, lower:upper].T, preferred_element_type=jnp.float32)
            piece_out = piece_out + jnp.dot(up_grad[:, lower:upper], up_mat[:, lower:upper].T, preferred_element_type=jnp.float32)
            rounded = lax.optimization_barrier(piece_out.astype(jnp.bfloat16))
            row_grad = row_grad + rounded.astype(jnp.float32)
        contrib = row_grad[jnp.minimum(target, row_count - 1)]
        contrib = jnp.where(filled[:, None], contrib, jnp.float32(0.0))
        totals = totals.at[senders].add(contrib)
        return totals, channel

    start = jnp.zeros((TOKENS, D), jnp.float32)
    totals, channels = lax.scan(one_expert, start, jnp.arange(LOCAL_EXPERTS, dtype=jnp.int32))
    scores = channels * channels * (LOCAL_EXPERTS / (TOKENS * TOPK))
    return scores, totals.astype(jnp.bfloat16)
```

```python
import functools

import jax
import jax.numpy as jnp
from jax import lax
from jax.experimental import pallas as pl
from jax.experimental.pallas import tpu as pltpu
from jax.sharding import PartitionSpec as P

LOCAL_EXPERTS = 64
TOPK = 8
CAP = 10
F32 = jnp.float32
BF16 = jnp.bfloat16
NT = (((1,), (1,)), ((), ()))
TN = (((0,), (0,)), ((), ()))
PARAMS = dict(vmem_limit_bytes=48 * 1024 * 1024)


def gathered(tokens, out_grad, gates, expert_ids, slots, gate_weight, up_weight, down_weight):
    expert_count = lax.axis_size("expert")
    group_count = lax.axis_size("dp")
    local_count = gate_weight.shape[0]
    tok_rows = tokens.shape[0]
    half_width = tokens.shape[1]
    slot_count = local_count * expert_count * CAP
    target_dev = expert_ids // local_count
    local_expert = expert_ids % local_count
    slot_rows = ((local_expert * expert_count + target_dev) * CAP + slots).reshape(-1)
    scaled = (gates[:, :, None] * out_grad[:, None, :].astype(F32)).astype(BF16)
    scaled = scaled.reshape(tok_rows * TOPK, half_width)
    repeated = jnp.repeat(tokens, TOPK, axis=0)

    def route(rows):
        send = jnp.zeros((slot_count, half_width), BF16).at[slot_rows].add(rows)
        send = send.reshape(local_count, expert_count, CAP, half_width)
        recv = lax.all_to_all(send, "expert", split_axis=1, concat_axis=1, tiled=True)
        full = lax.all_gather(recv, "sub", axis=3, tiled=True)
        return full.reshape(local_count, expert_count * CAP, full.shape[3])

    x_full, grad_full = route(repeated), route(scaled)
    gate_full = lax.all_gather(gate_weight, "dp", axis=1, tiled=True)
    up_full = lax.all_gather(up_weight, "dp", axis=1, tiled=True)
    down_full = lax.all_gather(down_weight, "dp", axis=2, tiled=True)
    gate_pre = jnp.einsum("erd,edf->erf", x_full, gate_full, preferred_element_type=F32)
    up_pre = jnp.einsum("erd,edf->erf", x_full, up_full, preferred_element_type=F32)
    hidden_grad = jnp.einsum("erd,efd->erf", grad_full, down_full, preferred_element_type=F32)
    gating = jax.nn.sigmoid(gate_pre)
    activated = gate_pre * gating
    channel = lax.psum(jnp.sum(activated * up_pre * hidden_grad, axis=1), "dp")
    scale = LOCAL_EXPERTS / (tok_rows * expert_count * group_count * TOPK)
    scores = channel * channel * scale
    gate_grad = (hidden_grad * up_pre * gating * (1.0 + gate_pre * (1.0 - gating))).astype(BF16)
    up_grad = (hidden_grad * activated).astype(BF16)
    parts = jnp.einsum("erf,edf->erd", gate_grad, gate_full, preferred_element_type=F32)
    parts = parts + jnp.einsum("erf,edf->erd", up_grad, up_full, preferred_element_type=F32)
    summed = lax.psum_scatter(parts.astype(BF16), "sub", scatter_dimension=2, tiled=True)
    summed = summed.reshape(local_count, expert_count, CAP, half_width)
    returned = lax.all_to_all(summed, "expert", split_axis=1, concat_axis=1, tiled=True)
    picked = returned.reshape(slot_count, half_width)[slot_rows].astype(F32)
    token_grad = jnp.sum(picked.reshape(tok_rows, TOPK, half_width), axis=1)
    return (scores, token_grad.astype(BF16))


def one_hot(rows, place):
    index = lax.broadcasted_iota(jnp.int32, (rows, place.shape[1]), 0).astype(F32)
    return jnp.where(index == place, 1.0, 0.0)


def fill(tok_ref, own_refs, other_refs, side, tok):
    for d, (own, other) in enumerate(zip(own_refs, other_refs)):
        tok_ref[pl.ds(2 * d * tok + side * tok, tok), :] = own[...]
        tok_ref[pl.ds(2 * d * tok + (1 - side) * tok, tok), :] = other[...]


def dispatch(rows, experts, group, place_ref, tok_ref, hot_ref, out_ref, level_ref=None):
    def body(g, carry):
        levels = []
        for j in range(group):
            e = g * group + j
            hot = one_hot(rows, place_ref[pl.ds(e, 1), :])
            hot_ref[pl.ds(j * rows, rows), :] = hot.astype(BF16)
            if level_ref is not None:
                levels.append(jnp.sum(hot * level_ref[pl.ds(e, 1), :], axis=1, keepdims=True))
        got = jnp.dot(hot_ref[...], tok_ref[...], preferred_element_type=F32)
        if level_ref is not None:
            got = got * jnp.concatenate(levels, axis=0)
        out_ref[pl.ds(pl.multiple_of(g * group * rows, group * rows), group * rows), :] = got.astype(BF16)
        return carry

    lax.fori_loop(0, experts // group, body, 0)


def places(zs, tok, cap, experts, meta_refs, place_ref, level_ref, first):
    lane = lax.broadcasted_iota(jnp.int32, (TOPK, 2 * tok), 1)
    rows, codes, levels = [], [], []
    for d in range(zs):
        code = meta_refs[d][0:TOPK, :]
        expert = jnp.floor((code + 0.5) * (1.0 / cap))
        block = 2 * d + (lane >= tok).astype(jnp.int32)
        rows.append(code - expert * cap + block.astype(F32) * cap)
        codes.append(expert)
        levels.append(meta_refs[d][TOPK : 2 * TOPK, :])
    row, expert, level = (jnp.concatenate(v, axis=1) for v in (rows, codes, levels))
    for e in range(experts):
        hit = expert == (first + e).astype(F32)
        place_ref[e : e + 1, :] = jnp.max(jnp.where(hit, row, -1.0), axis=0, keepdims=True)
        level_ref[e : e + 1, :] = jnp.sum(jnp.where(hit, level, 0.0), axis=0, keepdims=True)


def x_kernel(cfg, s_ref, *refs):
    zs, tok, experts, rows, group = cfg
    own, other, meta = refs[:zs], refs[zs : 2 * zs], refs[2 * zs : 3 * zs]
    gate_ref, up_ref, au_ref, xin_ref, place_ref, level_ref, tok_ref, hot_ref = refs[3 * zs :]
    j = pl.program_id(0)

    @pl.when(j == 0)
    def _():
        places(zs, tok, CAP, experts, meta, place_ref, level_ref, s_ref[2])
        fill(tok_ref, own, other, s_ref[1], tok)
        dispatch(rows, experts, group, place_ref, tok_ref, hot_ref, xin_ref)

    e = s_ref[0] + j
    x = xin_ref[pl.ds(pl.multiple_of(e * rows, rows), rows), :]
    au_ref[0, 0:rows, :] = jnp.dot(x, gate_ref[0], preferred_element_type=F32).astype(BF16)
    au_ref[0, rows:, :] = jnp.dot(x, up_ref[0], preferred_element_type=F32).astype(BF16)


def x2_kernel(rows, s_ref, x_ref, gate_ref, up_ref, au_ref):
    x = x_ref[...]
    au_ref[0, 0:rows, :] = jnp.dot(x, gate_ref[0], preferred_element_type=F32).astype(BF16)
    au_ref[0, rows:, :] = jnp.dot(x, up_ref[0], preferred_element_type=F32).astype(BF16)


def y_kernel(cfg, s_ref, *refs):
    zs, tok, experts, rows, group = cfg
    own, other = refs[:zs], refs[zs : 2 * zs]
    place_ref, level_ref, down_ref, dh_ref, yin_ref, tok_ref, hot_ref = refs[2 * zs :]
    j = pl.program_id(0)

    @pl.when(j == 0)
    def _():
        fill(tok_ref, own, other, s_ref[1], tok)
        dispatch(rows, experts, group, place_ref, tok_ref, hot_ref, yin_ref, level_ref)

    e = s_ref[0] + j
    y = yin_ref[pl.ds(pl.multiple_of(e * rows, rows), rows), :]
    dh_ref[0] = lax.dot_general(y, down_ref[0], NT, preferred_element_type=F32).astype(BF16)


def combine(rows, count, first, place_ref, part_ref, hot_ref):
    for j in range(count):
        hot_ref[j * rows : (j + 1) * rows, :] = one_hot(rows, place_ref[pl.ds(first + j, 1), :]).astype(BF16)
    return lax.dot_general(hot_ref[...], part_ref[...], TN, preferred_element_type=F32)


def mine_kernel(rows, count, scale, has_acc, s_ref, *refs):
    x_ref, y_ref, au_ref, dhr_ref, gate_ref, up_ref, down_ref, place_ref = refs[:8]
    acc_in = refs[8] if has_acc else None
    d_ref, score_ref, acc_ref, part_ref, hot_ref = refs[8 + has_acc :]
    j = pl.program_id(0)
    x, y = x_ref[...], y_ref[...]
    gate, up = gate_ref[0], up_ref[0]
    a = jnp.dot(x, gate, preferred_element_type=F32) + au_ref[0, 0:rows, :].astype(F32)
    u = jnp.dot(x, up, preferred_element_type=F32) + au_ref[0, rows:, :].astype(F32)
    dh = lax.dot_general(y, down_ref[0], NT, preferred_element_type=F32) + dhr_ref[0].astype(F32)
    sig = jax.nn.sigmoid(a)
    act = a * sig
    channel = jnp.sum(act * u * dh, axis=0, keepdims=True)
    score_ref[0] = channel * channel * scale
    da = (dh * u * sig * (1.0 + a * (1.0 - sig))).astype(BF16)
    du = (dh * act).astype(BF16)
    d_ref[0, 0:rows, :] = da
    d_ref[0, rows:, :] = du
    part = lax.dot_general(da, gate, NT, preferred_element_type=F32)
    part = part + lax.dot_general(du, up, NT, preferred_element_type=F32)
    part_ref[pl.ds(pl.multiple_of(j * rows, rows), rows), :] = part.astype(BF16)

    @pl.when(j == count - 1)
    def _():
        total = combine(rows, count, s_ref[0], place_ref, part_ref, hot_ref)
        acc_ref[...] = total + acc_in[...] if has_acc else total


def other_kernel(cfg, last, s_ref, *refs):
    rows, count, zs, tok = cfg
    d_ref, gate_ref, up_ref, place_ref, acc_in = refs[:5]
    j = pl.program_id(0)
    part_ref, hot_ref = refs[-2:]
    part = lax.dot_general(d_ref[0, 0:rows, :], gate_ref[0], NT, preferred_element_type=F32)
    part = part + lax.dot_general(d_ref[0, rows:, :], up_ref[0], NT, preferred_element_type=F32)
    part_ref[pl.ds(pl.multiple_of(j * rows, rows), rows), :] = part.astype(BF16)

    @pl.when(j == count - 1)
    def _():
        total = combine(rows, count, s_ref[0], place_ref, part_ref, hot_ref) + acc_in[...]
        if not last:
            refs[5][...] = total
        else:
            keep_ref, send_ref, acc = refs[5], refs[6], refs[7]
            acc[...] = total
            side = s_ref[1]
            for d in range(zs):
                keep_ref[d] = acc[pl.ds(2 * d * tok + side * tok, tok), :]
                send_ref[d] = acc[pl.ds(2 * d * tok + (1 - side) * tok, tok), :].astype(BF16)


def stationary(tokens, out_grad, gates, expert_ids, slots, gate_weight, up_weight, down_weight):
    zs = lax.axis_size("expert")
    tok, width = tokens.shape
    experts, _, ff = gate_weight.shape
    rows = 2 * zs * CAP
    all_tok = 2 * zs * tok
    half = experts // 2
    chunks = 2 if half % 2 == 0 else 1
    count = half // chunks
    group = count
    p, s, z = lax.axis_index("dp"), lax.axis_index("sub"), lax.axis_index("expert")
    mine0, other0 = half * p, half * (1 - p)

    def swap(v):
        return lax.ppermute(v, ("dp", "sub"), [(0, 0), (1, 2), (2, 1), (3, 3)])

    def flip(v, axis):
        return lax.ppermute(v, axis, [(0, 1), (1, 0)])

    def shift(v, d):
        return lax.ppermute(v, "expert", [(i, (i + d) % zs) for i in range(zs)])

    meta = jnp.concatenate([(expert_ids * CAP + slots).astype(F32).T, gates.T], axis=0)
    meta_other = flip(meta, "dp")
    pair = jnp.concatenate(
        [jnp.where(p == 0, meta, meta_other), jnp.where(p == 0, meta_other, meta)], axis=1
    )
    metas = [pair] + [shift(pair, d) for d in range(1, zs)]

    def spread(v):
        v = swap(v)
        own = [v] + [shift(v, d) for d in range(1, zs)]
        return own, [flip(w, "sub") for w in own]

    x_own, x_other = spread(tokens)
    y_own, y_other = spread(out_grad)

    def info(first):
        return jnp.stack([first, s, z * experts]).astype(jnp.int32)

    def whole(shape):
        return pl.BlockSpec(shape, lambda j, m: (0,) * len(shape))

    def per(shape):
        return pl.BlockSpec((1,) + shape, lambda j, m: (j,) + (0,) * len(shape))

    def pick(shape):
        return pl.BlockSpec((1,) + shape, lambda j, m: (m[0] + j,) + (0,) * len(shape))

    def sds(shape, dtype):
        return jax.ShapeDtypeStruct(shape, dtype)

    rows_spec = pl.BlockSpec((rows, width), lambda j, m: (m[0] + j, 0))
    up_spec, down_spec = pick((width, ff)), pick((ff, width))
    blocks = [whole((tok, width))] * zs

    def call(body, first, ins, args, outs, out_specs, scratch, steps, cost):
        return pl.pallas_call(
            body,
            out_shape=outs,
            grid_spec=pltpu.PrefetchScalarGridSpec(
                num_scalar_prefetch=1, grid=(steps,), in_specs=ins, out_specs=out_specs, scratch_shapes=scratch
            ),
            compiler_params=pltpu.CompilerParams(**PARAMS),
            cost_estimate=pl.CostEstimate(flops=cost[0], bytes_accessed=cost[1], transcendentals=0),
        )(info(first), *args)

    wbytes = width * ff * 2
    flop = 2 * rows * width * ff
    dflop = 2 * experts * rows * all_tok * width
    cfg = (zs, tok, experts, rows, group)
    hot = pltpu.VMEM((group * rows, all_tok), BF16)
    tok_scratch = pltpu.VMEM((all_tok, width), BF16)
    au0, xin, place, level = call(
        functools.partial(x_kernel, cfg),
        other0,
        blocks * 2 + [whole((2 * TOPK, 2 * tok))] * zs + [up_spec, up_spec],
        (*x_own, *x_other, *metas, gate_weight, up_weight),
        [
            sds((count, 2 * rows, ff), BF16),
            sds((experts * rows, width), BF16),
            sds((experts, all_tok), F32),
            sds((experts, all_tok), F32),
        ],
        [per((2 * rows, ff)), whole((experts * rows, width)), whole((experts, all_tok)), whole((experts, all_tok))],
        [tok_scratch, hot],
        count,
        (2 * count * flop + dflop, 2 * count * wbytes),
    )
    au_send = [au0]
    for c in range(1, chunks):
        au_send.append(
            call(
                functools.partial(x2_kernel, rows),
                other0 + c * count,
                [rows_spec, up_spec, up_spec],
                (xin, gate_weight, up_weight),
                sds((count, 2 * rows, ff), BF16),
                per((2 * rows, ff)),
                [],
                count,
                (2 * count * flop, 2 * count * wbytes),
            )
        )
    au_recv = [flip(v, "dp") for v in au_send]
    dh_send, yin = call(
        functools.partial(y_kernel, cfg),
        other0,
        blocks * 2 + [whole((experts, all_tok))] * 2 + [down_spec],
        (*y_own, *y_other, place, level, down_weight),
        [sds((half, rows, ff), BF16), sds((experts * rows, width), BF16)],
        [per((rows, ff)), whole((experts * rows, width))],
        [tok_scratch, hot],
        half,
        (half * flop + dflop, half * wbytes),
    )
    dh_recv = [flip(dh_send[c * count : (c + 1) * count], "dp") for c in range(chunks)]
    scale = LOCAL_EXPERTS / (all_tok * TOPK)
    part_scratch = pltpu.VMEM((count * rows, width), BF16)
    place_spec = whole((experts, all_tok))
    acc_spec, acc_shape = whole((all_tok, width)), sds((all_tok, width), F32)
    acc = None
    back, scores = [], []
    for c in range(chunks):
        has_acc = acc is not None
        d, sc, acc = call(
            functools.partial(mine_kernel, rows, count, scale, has_acc),
            mine0 + c * count,
            [rows_spec, rows_spec, per((2 * rows, ff)), per((rows, ff)), up_spec, up_spec, down_spec, place_spec]
            + [acc_spec] * has_acc,
            (xin, yin, au_recv[c], dh_recv[c], gate_weight, up_weight, down_weight, place) + (acc,) * has_acc,
            [sds((count, 2 * rows, ff), BF16), sds((count, 1, ff), F32), acc_shape],
            [per((2 * rows, ff)), per((1, ff)), acc_spec],
            [part_scratch, hot],
            count,
            (5 * count * flop, 3 * count * wbytes),
        )
        back.append(flip(d, "dp"))
        scores.append(sc)
    for c in range(chunks):
        last = c == chunks - 1
        zshape = (zs, tok, width)
        res = call(
            functools.partial(other_kernel, (rows, count, zs, tok), last),
            other0 + c * count,
            [per((2 * rows, ff)), up_spec, up_spec, place_spec, acc_spec],
            (back[c], gate_weight, up_weight, place, acc),
            [sds(zshape, F32), sds(zshape, BF16)] if last else acc_shape,
            [whole(zshape), whole(zshape)] if last else acc_spec,
            ([pltpu.VMEM((all_tok, width), F32)] if last else []) + [part_scratch, hot],
            count,
            (2 * count * flop, 2 * count * wbytes),
        )
        if not last:
            acc = res
    keep, send = res
    summed = (keep + flip(send, "sub").astype(F32)).astype(BF16)
    total = summed[0].astype(F32)
    for d in range(1, zs):
        total = total + shift(summed[d], -d).astype(F32)
    token_grad = swap(total.astype(BF16))
    score = jnp.concatenate(scores, axis=0).reshape(half, ff)
    score_other = flip(score, "dp")
    scores = jnp.concatenate(
        [jnp.where(p == 0, score, score_other), jnp.where(p == 0, score_other, score)], axis=0
    )
    return (scores, token_grad)


def solution(mesh):
    in_specs = (
        P(("dom", "expert", "dp"), "sub"),
        P(("dom", "expert", "dp"), "sub"),
        P(("dom", "expert", "dp"), None),
        P(("dom", "expert", "dp"), None),
        P(("dom", "expert", "dp"), None),
        P("expert", "dp", "sub"),
        P("expert", "dp", "sub"),
        P("expert", "sub", "dp"),
    )
    out_specs = (P(("dom", "expert"), "sub"), P(("dom", "expert", "dp"), "sub"))
    pairs = mesh.shape["dp"] == 2 and mesh.shape["sub"] == 2
    split = (LOCAL_EXPERTS // mesh.shape["expert"]) % 2 == 0
    local = stationary if pairs and split else gathered
    return jax.shard_map(local, mesh=mesh, in_specs=in_specs, out_specs=out_specs, check_vma=False)
```

```python
import functools

import jax
import jax.numpy as jnp
from jax import lax
from jax.experimental import pallas as pl
from jax.experimental.pallas import tpu as pltpu
from jax.sharding import PartitionSpec as P

LOCAL_EXPERTS = 64
TOPK = 8
CAP = 10
F32 = jnp.float32
BF16 = jnp.bfloat16
NT = (((1,), (1,)), ((), ()))
TN = (((0,), (0,)), ((), ()))
VMEM_LIMIT = 40 * 1024 * 1024


def gathered(tokens, out_grad, gates, expert_ids, slots, gate_weight, up_weight, down_weight):
    expert_count = lax.axis_size("expert")
    group_count = lax.axis_size("dp")
    local_count = gate_weight.shape[0]
    tok_rows = tokens.shape[0]
    half_width = tokens.shape[1]
    slot_count = local_count * expert_count * CAP
    target_dev = expert_ids // local_count
    local_expert = expert_ids % local_count
    slot_rows = ((local_expert * expert_count + target_dev) * CAP + slots).reshape(-1)
    scaled = (gates[:, :, None] * out_grad[:, None, :].astype(F32)).astype(BF16)
    scaled = scaled.reshape(tok_rows * TOPK, half_width)
    repeated = jnp.repeat(tokens, TOPK, axis=0)

    def route(rows):
        send = jnp.zeros((slot_count, half_width), BF16).at[slot_rows].add(rows)
        send = send.reshape(local_count, expert_count, CAP, half_width)
        recv = lax.all_to_all(send, "expert", split_axis=1, concat_axis=1, tiled=True)
        full = lax.all_gather(recv, "sub", axis=3, tiled=True)
        return full.reshape(local_count, expert_count * CAP, full.shape[3])

    x_full, grad_full = route(repeated), route(scaled)
    gate_full = lax.all_gather(gate_weight, "dp", axis=1, tiled=True)
    up_full = lax.all_gather(up_weight, "dp", axis=1, tiled=True)
    down_full = lax.all_gather(down_weight, "dp", axis=2, tiled=True)
    gate_pre = jnp.einsum("erd,edf->erf", x_full, gate_full, preferred_element_type=F32)
    up_pre = jnp.einsum("erd,edf->erf", x_full, up_full, preferred_element_type=F32)
    hidden_grad = jnp.einsum("erd,efd->erf", grad_full, down_full, preferred_element_type=F32)
    gating = jax.nn.sigmoid(gate_pre)
    activated = gate_pre * gating
    channel = lax.psum(jnp.sum(activated * up_pre * hidden_grad, axis=1), "dp")
    scale = LOCAL_EXPERTS / (tok_rows * expert_count * group_count * TOPK)
    scores = channel * channel * scale
    gate_grad = (hidden_grad * up_pre * gating * (1.0 + gate_pre * (1.0 - gating))).astype(BF16)
    up_grad = (hidden_grad * activated).astype(BF16)
    parts = jnp.einsum("erf,edf->erd", gate_grad, gate_full, preferred_element_type=F32)
    parts = parts + jnp.einsum("erf,edf->erd", up_grad, up_full, preferred_element_type=F32)
    summed = lax.psum_scatter(parts.astype(BF16), "sub", scatter_dimension=2, tiled=True)
    summed = summed.reshape(local_count, expert_count, CAP, half_width)
    returned = lax.all_to_all(summed, "expert", split_axis=1, concat_axis=1, tiled=True)
    picked = returned.reshape(slot_count, half_width)[slot_rows].astype(F32)
    token_grad = jnp.sum(picked.reshape(tok_rows, TOPK, half_width), axis=1)
    return (scores, token_grad.astype(BF16))


ROUTE_ROWS = 16


def load(sources, first, count, buffers, sem):
    copies = []
    for j in range(count):
        line = []
        for n, (source, buffer) in enumerate(zip(sources, buffers)):
            copy = pltpu.make_async_copy(source.at[first + j], buffer.at[j], sem.at[j * len(sources) + n])
            copy.start()
            line.append(copy)
        copies.append(line)
    return copies


def ready(line):
    for copy in line:
        copy.wait()


def one_hot(rows, place):
    index = lax.broadcasted_iota(jnp.int32, (rows, place.shape[1]), 0).astype(F32)
    return jnp.where(index == place, 1.0, 0.0)


def fill(tok_ref, token_refs, side, tok, sem, meta_ref=None):
    copies = []
    zs = len(token_refs) // 2
    for n, ref in enumerate(token_refs):
        d, part = n % zs, side if n < zs else 1 - side
        start = pl.multiple_of(2 * d * tok + part * tok, tok)
        copies.append(pltpu.make_async_copy(ref.at[pl.ds(0, tok)], tok_ref.at[pl.ds(start, tok)], sem.at[n]))
        copies[-1].start()
    routes = []
    if meta_ref is not None:
        for n, ref in enumerate(token_refs):
            source = ref.at[pl.ds(tok, ROUTE_ROWS)]
            routes.append(pltpu.make_async_copy(source, meta_ref.at[n], sem.at[2 * zs + n]))
            routes[-1].start()
    return copies, routes


def dispatch(rows, experts, group, place_ref, tok_ref, hot_ref, out_ref, level_ref=None):
    def body(g, carry):
        levels = []
        for j in range(group):
            e = g * group + j
            hot = one_hot(rows, place_ref[pl.ds(e, 1), :])
            hot_ref[pl.ds(j * rows, rows), :] = hot.astype(BF16)
            if level_ref is not None:
                levels.append(jnp.sum(hot * level_ref[pl.ds(e, 1), :], axis=1, keepdims=True))
        got = jnp.dot(hot_ref[...], tok_ref[...], preferred_element_type=F32)
        if level_ref is not None:
            got = got * jnp.concatenate(levels, axis=0)
        out_ref[pl.ds(pl.multiple_of(g * group * rows, group * rows), group * rows), :] = got.astype(BF16)
        return carry

    lax.fori_loop(0, experts // group, body, 0)


def places(zs, tok, experts, meta_ref, place_ref, level_ref, first):
    lane = lax.broadcasted_iota(jnp.int32, (TOPK, 2 * tok), 1)
    rows, ids, levels = [], [], []
    for d in range(zs):
        meta = meta_ref[d].astype(F32) + meta_ref[zs + d].astype(F32)
        kinds = [meta[0:TOPK, 2 * tok * n : 2 * tok * (n + 1)] for n in range(5)]
        block = 2 * d + (lane >= tok).astype(jnp.int32)
        rows.append(kinds[1] + block.astype(F32) * CAP)
        ids.append(kinds[0])
        levels.append(kinds[2] + kinds[3] + kinds[4])
    row, expert, level = (jnp.concatenate(v, axis=1) for v in (rows, ids, levels))
    for e in range(experts):
        hit = expert == (first + e).astype(F32)
        place_ref[e : e + 1, :] = jnp.max(jnp.where(hit, row, -1.0), axis=0, keepdims=True)
        level_ref[e : e + 1, :] = jnp.sum(jnp.where(hit, level, 0.0), axis=0, keepdims=True)


def expert_rows(ref, rows, e):
    return ref[pl.ds(pl.multiple_of(e * rows, rows), rows), :]


def forward(rows, count, first, copies, xin_ref, bufs, out_ref):
    for j in range(count):
        x = expert_rows(xin_ref, rows, first + j)
        ready(copies[j])
        for n, buf in enumerate(bufs):
            got = jnp.dot(x, buf[j], preferred_element_type=F32)
            out_ref[j, n * rows : (n + 1) * rows, :] = got.astype(out_ref.dtype)


def x_kernel(cfg, count, s_ref, *refs):
    zs, tok, experts, rows, group = cfg
    tokens = refs[: 2 * zs]
    gate_ref, up_ref, au_ref, xin_ref, place_ref, level_ref = refs[2 * zs : 2 * zs + 6]
    tok_ref, hot_ref, meta_ref, gate, up, sem, tok_sem = refs[2 * zs + 6 :]
    filling, routes = fill(tok_ref, tokens, s_ref[1], tok, tok_sem, meta_ref)
    copies = load((gate_ref, up_ref), s_ref[0], count, (gate, up), sem)
    ready(routes)
    places(zs, tok, experts, meta_ref, place_ref, level_ref, s_ref[2])
    ready(filling)
    dispatch(rows, experts, group, place_ref, tok_ref, hot_ref, xin_ref)
    forward(rows, count, s_ref[0], copies, xin_ref, (gate, up), au_ref)


def x2_kernel(rows, count, s_ref, xin_ref, gate_ref, up_ref, au_ref, gate, up, sem):
    copies = load((gate_ref, up_ref), s_ref[0], count, (gate, up), sem)
    forward(rows, count, s_ref[0], copies, xin_ref, (gate, up), au_ref)


def back_dots(rows, count, first, copies, yin_ref, down, out_ref):
    for j in range(count):
        y = expert_rows(yin_ref, rows, first + j)
        ready(copies[j])
        out_ref[j] = lax.dot_general(y, down[j], NT, preferred_element_type=F32).astype(out_ref.dtype)


def y_kernel(cfg, count, s_ref, *refs):
    zs, tok, experts, rows, group = cfg
    tokens = refs[: 2 * zs]
    place_ref, level_ref, down_ref, dh_ref, yin_ref, tok_ref, hot_ref, down, sem, tok_sem = refs[2 * zs :]
    filling, _ = fill(tok_ref, tokens, s_ref[1], tok, tok_sem)
    copies = load((down_ref,), s_ref[0], count, (down,), sem)
    ready(filling)
    dispatch(rows, experts, group, place_ref, tok_ref, hot_ref, yin_ref, level_ref)
    back_dots(rows, count, s_ref[0], copies, yin_ref, down, dh_ref)


def y2_kernel(rows, count, s_ref, yin_ref, down_ref, dh_ref, down, sem):
    copies = load((down_ref,), s_ref[0], count, (down,), sem)
    back_dots(rows, count, s_ref[0], copies, yin_ref, down, dh_ref)


def final_kernel(rows, scale, at, au_index, dh_index, s_ref, *refs):
    aus, dhs = sorted({n for n, _ in au_index}), sorted({n for n, _ in dh_index})
    au_m, dh_m = refs[:2]
    au_r = dict(zip(aus, refs[2:]))
    dh_r = dict(zip(dhs, refs[2 + len(aus) :]))
    d_ref, score_ref = refs[2 + len(aus) + len(dhs) :]
    for j, ((na, ia), (nd, idx)) in enumerate(zip(au_index, dh_index)):
        au = au_m[at + j] + au_r[na][ia].astype(F32)
        a, u = au[0:rows], au[rows:]
        dh = dh_m[at + j] + dh_r[nd][idx].astype(F32)
        sig = jax.nn.sigmoid(a)
        act = a * sig
        channel = jnp.sum(act * u * dh, axis=0, keepdims=True)
        score_ref[j] = channel * channel * scale
        d_ref[j, 0:rows, :] = (dh * u * sig * (1.0 + a * (1.0 - sig))).astype(BF16)
        d_ref[j, rows:, :] = (dh * act).astype(BF16)


def gradient_rows(rows, d_refs, sizes, copies, gate, up, part_ref, at=0):
    j = 0
    for d_ref, size in zip(d_refs, sizes):
        for i in range(size):
            ready(copies[j])
            part = lax.dot_general(d_ref[i, 0:rows, :], gate[j], NT, preferred_element_type=F32)
            part = part + lax.dot_general(d_ref[i, rows:, :], up[j], NT, preferred_element_type=F32)
            start = at + j * rows
            part_ref[start : start + rows, :] = part.astype(BF16)
            j += 1


def mine_parts_kernel(rows, sizes, s_ref, *refs):
    n = len(sizes)
    gate_ref, up_ref, part_ref, gate, up, sem = refs[n:]
    copies = load((gate_ref, up_ref), s_ref[0], sum(sizes), (gate, up), sem)
    gradient_rows(rows, refs[:n], sizes, copies, gate, up, part_ref)


def early_kernel(rows, zs, tok, half, sizes, s_ref, *refs):
    n = len(sizes)
    count = sum(sizes)
    gate_ref, up_ref, place_ref, mine_ref, keep_ref, send_ref = refs[n : n + 6]
    gate, up, part_ref, hot_ref, acc, sem = refs[n + 6 :]
    first = s_ref[0]
    copies = load((gate_ref, up_ref), first, count, (gate, up), sem)
    start = half - first
    for j in range(half + count):
        e = start + j if j < half else first + j - half
        hot = one_hot(rows, place_ref[pl.ds(e, 1), :])
        hot_ref[j * rows : (j + 1) * rows, :] = hot.astype(BF16)
    cut = half * rows
    acc[...] = lax.dot_general(hot_ref[0:cut, :], mine_ref[...], TN, preferred_element_type=F32)
    gradient_rows(rows, refs[:n], sizes, copies, gate, up, part_ref)
    acc[...] += lax.dot_general(hot_ref[cut:, :], part_ref[...], TN, preferred_element_type=F32)
    side = s_ref[1]
    for d in range(zs):
        keep_ref[d] = acc[pl.ds(pl.multiple_of(2 * d * tok + side * tok, tok), tok), :]
        send_ref[d] = acc[pl.ds(pl.multiple_of(2 * d * tok + (1 - side) * tok, tok), tok), :].astype(BF16)


def late_kernel(rows, zs, pad, count, s_ref, d_ref, gate_ref, up_ref, keep_ref, send_ref, gate, up, part_ref, sem):
    copies = load((gate_ref, up_ref), s_ref[0], count, (gate, up), sem)
    gradient_rows(rows, [d_ref], [count], copies, gate, up, part_ref)
    shape = (zs * pad, count * rows)
    out = lax.broadcasted_iota(jnp.int32, shape, 0)
    source = lax.broadcasted_iota(jnp.int32, shape, 1)
    dist, place = out // pad, out % pad
    expert, slot = place // CAP, place % CAP
    for ref, side in ((keep_ref, s_ref[1]), (send_ref, 1 - s_ref[1])):
        want = expert * rows + (2 * dist + side) * CAP + slot
        want = jnp.where(expert < count, want, -1)
        move = jnp.where(want == source, 1.0, 0.0).astype(BF16)
        got = jnp.dot(move, part_ref[...], preferred_element_type=F32)
        for d in range(zs):
            ref[d] = got[d * pad : (d + 1) * pad].astype(ref.dtype)


def home_kernel(zs, pad, count, experts, s_ref, code_ref, *refs):
    early, late, (out_ref, late_ref) = refs[:zs], refs[zs : 2 * zs], refs[2 * zs :]
    tok = out_ref.shape[0]
    column = lax.broadcasted_iota(jnp.int32, (tok, zs * pad), 1)
    hot = jnp.zeros((tok, zs * pad), F32)
    for d in range(zs):
        late_ref[d * pad : (d + 1) * pad, :] = late[d][...]
        base = ((s_ref[2] + d) % zs * experts + s_ref[0]) * CAP
        for k in range(TOPK):
            at = code_ref[:, k : k + 1] - base
            at = jnp.where((at >= 0) & (at < count * CAP), at + d * pad, -1)
            hot = hot + jnp.where(at == column, 1.0, 0.0)
    total = jnp.dot(hot.astype(BF16), late_ref[...], preferred_element_type=F32)
    for ref in early:
        total = total + ref[...].astype(F32)
    out_ref[...] = total.astype(BF16)


def split(total, sizes):
    ends = [total * sum(sizes[: n + 1]) // sum(sizes) for n in range(len(sizes))]
    return [b - a for a, b in zip([0] + ends[:-1], ends) if b > a]


def locate(sizes, e):
    for n, size in enumerate(sizes):
        if e < size:
            return n, e
        e -= size


def stationary(tokens, out_grad, gates, expert_ids, slots, gate_weight, up_weight, down_weight):
    zs = lax.axis_size("expert")
    tok, width = tokens.shape
    experts, _, ff = gate_weight.shape
    rows = 2 * zs * CAP
    all_tok = 2 * zs * tok
    half = experts // 2
    group = 4 if experts % 4 == 0 else 1
    p, s, z = lax.axis_index("dp"), lax.axis_index("sub"), lax.axis_index("expert")
    mine0, other0 = half * p, half * (1 - p)
    au_sizes, dh_sizes, d_sizes = split(half, (1, 3)), split(half, (1, 1)), split(half, (2, 1, 1))

    def flip(v, axis):
        return lax.ppermute(v, axis, [(0, 1), (1, 0)])

    def turn(v, d):
        pairs = [
            ((i * 2 + a) * 2 + b, (((i + d) % zs) * 2 + b) * 2 + a)
            for i in range(zs)
            for a in range(2)
            for b in range(2)
        ]
        return lax.ppermute(v, ("expert", "dp", "sub"), pairs)

    levels, left = [], gates
    for _ in range(3):
        levels.append(lax.reduce_precision(left, 8, 7))
        left = left - levels[-1]
    kinds = jnp.stack([expert_ids.astype(F32), slots.astype(F32)] + levels).transpose(2, 0, 1)
    none = jnp.zeros_like(kinds)
    kinds = jnp.concatenate([jnp.where(p == 0, kinds, none), jnp.where(p == 0, none, kinds)], axis=2)
    kinds = kinds.reshape(TOPK, 10 * tok).astype(BF16)
    kinds = jnp.pad(kinds, ((0, ROUTE_ROWS - TOPK), (0, width - 10 * tok)))
    loaded = jnp.concatenate([tokens, kinds], axis=0)
    x_own = [turn(loaded, d) for d in range(zs)]
    x_other = [flip(v, "sub") for v in x_own]

    def sds(shape, dtype):
        return jax.ShapeDtypeStruct(shape, dtype)

    vmem, anywhere = pl.BlockSpec(memory_space=pltpu.VMEM), pl.BlockSpec(memory_space=pl.ANY)
    smem = pl.BlockSpec(memory_space=pltpu.SMEM)
    dma = pltpu.SemaphoreType.DMA

    def call(body, first, args, outs, scratch, flops, moved, name):
        ins = [spec for spec, group in args for _ in group]
        arrays = [v for _, group in args for v in group]
        info = jnp.stack([first, s, z * experts]).astype(jnp.int32)
        return pl.pallas_call(
            body,
            out_shape=outs,
            in_specs=[smem] + ins,
            out_specs=jax.tree.map(lambda _: vmem, outs),
            scratch_shapes=scratch,
            compiler_params=pltpu.CompilerParams(vmem_limit_bytes=VMEM_LIMIT),
            cost_estimate=pl.CostEstimate(flops=int(flops), bytes_accessed=int(moved), transcendentals=0),
            name=name,
        )(info, *arrays)

    wbytes = width * ff * 2
    flop = 2 * rows * width * ff
    dflop = 2 * experts * rows * all_tok * width
    cfg = (zs, tok, experts, rows, group)
    hot = pltpu.VMEM((group * rows, all_tok), BF16)
    tok_scratch = pltpu.VMEM((all_tok, width), BF16)

    def wide(count):
        return pltpu.VMEM((count, width, ff), BF16)

    def tall(count):
        return pltpu.VMEM((count, ff, width), BF16)

    place_shape = sds((experts, all_tok), F32)
    rows_shape = sds((experts * rows, width), BF16)
    n = au_sizes[0]
    au0, xin, place, level = call(
        functools.partial(x_kernel, cfg, n),
        other0,
        [(anywhere, (*x_own, *x_other, gate_weight, up_weight))],
        [sds((n, 2 * rows, ff), BF16), rows_shape, place_shape, place_shape],
        [tok_scratch, hot, pltpu.VMEM((2 * zs, ROUTE_ROWS, width), BF16), wide(n), wide(n)]
        + [dma((2 * n,)), dma((4 * zs,))],
        2 * n * flop + dflop,
        2 * n * wbytes,
        "x_first",
    )

    out_grad, au0 = lax.optimization_barrier((out_grad, au0))
    y_own = [turn(out_grad, d) for d in range(zs)]

    def x_call(first, n, dtype, name):
        return call(
            functools.partial(x2_kernel, rows, n),
            first,
            [(vmem, (xin,)), (anywhere, (gate_weight, up_weight))],
            sds((n, 2 * rows, ff), dtype),
            [wide(n), wide(n), dma((2 * n,))],
            2 * n * flop,
            2 * n * wbytes,
            name,
        )

    au_send = [au0]
    at = au_sizes[0]
    for n in au_sizes[1:]:
        au_send.append(x_call(other0 + at, n, BF16, "x_other"))
        at += n
    au_recv = [flip(v, "dp") for v in au_send]
    au_mine = x_call(mine0, half, F32, "x_mine")
    y_other = [flip(v, "sub") for v in y_own]
    n = dh_sizes[0]
    dh0, yin = call(
        functools.partial(y_kernel, cfg, n),
        other0,
        [(anywhere, (*y_own, *y_other)), (vmem, (place, level)), (anywhere, (down_weight,))],
        [sds((n, rows, ff), BF16), rows_shape],
        [tok_scratch, hot, tall(n), dma((n,)), dma((2 * zs,))],
        n * flop + dflop,
        n * wbytes,
        "y_first",
    )

    def y_call(first, n, dtype, name):
        return call(
            functools.partial(y2_kernel, rows, n),
            first,
            [(vmem, (yin,)), (anywhere, (down_weight,))],
            sds((n, rows, ff), dtype),
            [tall(n), dma((n,))],
            n * flop,
            n * wbytes,
            name,
        )

    dh_send, at = [dh0], n
    for n in dh_sizes[1:]:
        dh_send.append(y_call(other0 + at, n, BF16, "y_other"))
        at += n
    dh_recv = [flip(v, "dp") for v in dh_send]
    dh_mine = y_call(mine0, half, F32, "y_mine")
    scale = LOCAL_EXPERTS / (all_tok * TOPK)
    grads, back, scores, at = [], [], [], 0
    for n in d_sizes:
        au_index = [locate(au_sizes, e) for e in range(at, at + n)]
        dh_index = [locate(dh_sizes, e) for e in range(at, at + n)]
        aus = [au_recv[k] for k in sorted({k for k, _ in au_index})]
        dhs = [dh_recv[k] for k in sorted({k for k, _ in dh_index})]
        d, score = call(
            functools.partial(final_kernel, rows, scale, at, au_index, dh_index),
            mine0,
            [(vmem, (au_mine, dh_mine, *aus, *dhs))],
            [sds((n, 2 * rows, ff), BF16), sds((n, 1, ff), F32)],
            [],
            n * rows * ff * 40,
            n * rows * ff * 30,
            "final",
        )
        grads.append(d)
        scores.append(score)
        back.append(flip(d, "dp"))
        at += n

    score = jnp.concatenate(scores, axis=0).reshape(half, ff)
    score_other = flip(score, "dp")
    scores = jnp.concatenate(
        [jnp.where(p == 0, score, score_other), jnp.where(p == 0, score_other, score)], axis=0
    )
    weights = (anywhere, (gate_weight, up_weight))

    def parts_scratch(n):
        return [wide(n), wide(n), pltpu.VMEM((n * rows, width), BF16)]

    mine_parts = call(
        functools.partial(mine_parts_kernel, rows, d_sizes),
        mine0,
        [(vmem, grads), weights],
        sds((half * rows, width), BF16),
        parts_scratch(half)[:2] + [dma((2 * half,))],
        2 * half * flop,
        2 * half * wbytes,
        "mine_parts",
    )
    n_last = d_sizes[-1]
    n = half - n_last
    zshape = (zs, tok, width)
    keep, send = call(
        functools.partial(early_kernel, rows, zs, tok, half, d_sizes[:-1]),
        other0,
        [(vmem, back[:-1]), weights, (vmem, (place, mine_parts))],
        [sds(zshape, F32), sds(zshape, BF16)],
        parts_scratch(n)
        + [pltpu.VMEM(((half + n) * rows, all_tok), BF16), pltpu.VMEM((all_tok, width), F32), dma((2 * n,))],
        2 * n * flop + 2 * (half + n) * rows * width * all_tok,
        2 * n * wbytes,
        "early",
    )
    pad = -(-n_last * CAP // 16) * 16
    late_shape = (zs, pad, width)
    keep_late, send_late = call(
        functools.partial(late_kernel, rows, zs, pad, n_last),
        other0 + n,
        [(vmem, (back[-1],)), weights],
        [sds(late_shape, F32), sds(late_shape, BF16)],
        parts_scratch(n_last) + [dma((2 * n_last,))],
        2 * n_last * flop,
        2 * n_last * wbytes,
        "late",
    )

    def home(keep, send):
        summed = (keep + flip(send, "sub").astype(F32)).astype(BF16)
        return [turn(summed[d], -d) for d in range(zs)]

    early = home(keep, send)
    late = home(keep_late, send_late)
    info = jnp.stack([half * (1 - s) + n, s, z]).astype(jnp.int32)
    token_grad = pl.pallas_call(
        functools.partial(home_kernel, zs, pad, n_last, experts),
        out_shape=sds((tok, width), BF16),
        in_specs=[smem] + [vmem] * (1 + 2 * zs),
        out_specs=vmem,
        scratch_shapes=[pltpu.VMEM((zs * pad, width), BF16)],
        compiler_params=pltpu.CompilerParams(vmem_limit_bytes=VMEM_LIMIT),
        name="home",
    )(info, expert_ids * CAP + slots, *early, *late)
    return (scores, token_grad)


def solution(mesh):
    in_specs = (
        P(("dom", "expert", "dp"), "sub"),
        P(("dom", "expert", "dp"), "sub"),
        P(("dom", "expert", "dp"), None),
        P(("dom", "expert", "dp"), None),
        P(("dom", "expert", "dp"), None),
        P("expert", "dp", "sub"),
        P("expert", "dp", "sub"),
        P("expert", "sub", "dp"),
    )
    out_specs = (P(("dom", "expert"), "sub"), P(("dom", "expert", "dp"), "sub"))
    pairs = mesh.shape["dp"] == 2 and mesh.shape["sub"] == 2
    split = (LOCAL_EXPERTS // mesh.shape["expert"]) % 2 == 0
    local = stationary if pairs and split else gathered
    return jax.shard_map(local, mesh=mesh, in_specs=in_specs, out_specs=out_specs, check_vma=False)
```

```python
import functools

import jax
import jax.numpy as jnp
from jax import lax
from jax.experimental import pallas as pl
from jax.experimental.pallas import tpu as pltpu
from jax.sharding import PartitionSpec as P

LOCAL_EXPERTS = 64
TOPK = 8
CAP = 10
F32 = jnp.float32
BF16 = jnp.bfloat16
NT = (((1,), (1,)), ((), ()))
TN = (((0,), (0,)), ((), ()))
VMEM_LIMIT = 52 * 1024 * 1024


def gathered(tokens, out_grad, gates, expert_ids, slots, gate_weight, up_weight, down_weight):
    expert_count = lax.axis_size("expert")
    group_count = lax.axis_size("dp")
    local_count = gate_weight.shape[0]
    tok_rows = tokens.shape[0]
    half_width = tokens.shape[1]
    slot_count = local_count * expert_count * CAP
    target_dev = expert_ids // local_count
    local_expert = expert_ids % local_count
    slot_rows = ((local_expert * expert_count + target_dev) * CAP + slots).reshape(-1)
    scaled = (gates[:, :, None] * out_grad[:, None, :].astype(F32)).astype(BF16)
    scaled = scaled.reshape(tok_rows * TOPK, half_width)
    repeated = jnp.repeat(tokens, TOPK, axis=0)

    def route(rows):
        send = jnp.zeros((slot_count, half_width), BF16).at[slot_rows].add(rows)
        send = send.reshape(local_count, expert_count, CAP, half_width)
        recv = lax.all_to_all(send, "expert", split_axis=1, concat_axis=1, tiled=True)
        full = lax.all_gather(recv, "sub", axis=3, tiled=True)
        return full.reshape(local_count, expert_count * CAP, full.shape[3])

    x_full, grad_full = route(repeated), route(scaled)
    gate_full = lax.all_gather(gate_weight, "dp", axis=1, tiled=True)
    up_full = lax.all_gather(up_weight, "dp", axis=1, tiled=True)
    down_full = lax.all_gather(down_weight, "dp", axis=2, tiled=True)
    gate_pre = jnp.einsum("erd,edf->erf", x_full, gate_full, preferred_element_type=F32)
    up_pre = jnp.einsum("erd,edf->erf", x_full, up_full, preferred_element_type=F32)
    hidden_grad = jnp.einsum("erd,efd->erf", grad_full, down_full, preferred_element_type=F32)
    gating = jax.nn.sigmoid(gate_pre)
    activated = gate_pre * gating
    channel = lax.psum(jnp.sum(activated * up_pre * hidden_grad, axis=1), "dp")
    scale = LOCAL_EXPERTS / (tok_rows * expert_count * group_count * TOPK)
    scores = channel * channel * scale
    gate_grad = (hidden_grad * up_pre * gating * (1.0 + gate_pre * (1.0 - gating))).astype(BF16)
    up_grad = (hidden_grad * activated).astype(BF16)
    parts = jnp.einsum("erf,edf->erd", gate_grad, gate_full, preferred_element_type=F32)
    parts = parts + jnp.einsum("erf,edf->erd", up_grad, up_full, preferred_element_type=F32)
    summed = lax.psum_scatter(parts.astype(BF16), "sub", scatter_dimension=2, tiled=True)
    summed = summed.reshape(local_count, expert_count, CAP, half_width)
    returned = lax.all_to_all(summed, "expert", split_axis=1, concat_axis=1, tiled=True)
    picked = returned.reshape(slot_count, half_width)[slot_rows].astype(F32)
    token_grad = jnp.sum(picked.reshape(tok_rows, TOPK, half_width), axis=1)
    return (scores, token_grad.astype(BF16))


COST = 1.0


ROUTE_ROWS = 16


def each(count, body):
    def step(j, carry):
        body(j)
        return carry

    lax.fori_loop(0, count, step, 0)


def load(sources, first, count, buffers, sem):
    def copies(j):
        return [
            pltpu.make_async_copy(source.at[first + j], buffer.at[j], sem.at[j * len(sources) + n])
            for n, (source, buffer) in enumerate(zip(sources, buffers))
        ]

    def start(j):
        for copy in copies(j):
            copy.start()

    each(count, start)
    return lambda j: ready(copies(j))


def ready(line):
    for copy in line:
        copy.wait()


def one_hot(rows, place):
    index = lax.broadcasted_iota(jnp.int32, (rows, place.shape[1]), 0).astype(F32)
    return jnp.where(index == place, 1.0, 0.0)


def pack_kernel(p_ref, tokens_ref, ids_ref, slots_ref, gates_ref, out_ref):
    tok = tokens_ref.shape[0]
    out_ref[0:tok, :] = tokens_ref[...]
    out_ref[tok:, :] = jnp.zeros((ROUTE_ROWS, out_ref.shape[1]), BF16)
    lane = lax.broadcasted_iota(jnp.int32, (tok, 2 * tok), 1)
    row = lax.broadcasted_iota(jnp.int32, (tok, 2 * tok), 0) + p_ref[0] * tok
    place = jnp.where(lane == row, 1.0, 0.0).astype(BF16)
    left = gates_ref[...]
    kinds = [ids_ref[...].astype(F32), slots_ref[...].astype(F32)]
    for _ in range(3):
        kinds.append(left.astype(BF16).astype(F32))
        left = left - kinds[-1]
    kinds = jnp.concatenate(kinds, axis=0).astype(BF16)
    moved = jnp.dot(kinds, place, preferred_element_type=F32)
    none = jnp.zeros((ROUTE_ROWS - TOPK, 2 * tok), F32)
    for n in range(5):
        block = jnp.concatenate([moved[n * TOPK : (n + 1) * TOPK], none], axis=0)
        out_ref[tok:, 2 * tok * n : 2 * tok * (n + 1)] = block.astype(BF16)


def fill(tok_ref, token_refs, side, tok, sem, meta_ref=None):
    copies = []
    zs = len(token_refs) // 2
    for n, ref in enumerate(token_refs):
        d, part = n % zs, side if n < zs else 1 - side
        start = pl.multiple_of(2 * d * tok + part * tok, tok)
        copies.append(pltpu.make_async_copy(ref.at[pl.ds(0, tok)], tok_ref.at[pl.ds(start, tok)], sem.at[n]))
        copies[-1].start()
    routes = []
    if meta_ref is not None:
        for n, ref in enumerate(token_refs):
            source = ref.at[pl.ds(tok, ROUTE_ROWS)]
            routes.append(pltpu.make_async_copy(source, meta_ref.at[n], sem.at[2 * zs + n]))
            routes[-1].start()
    return copies, routes


def dispatch(rows, experts, group, place_ref, tok_ref, hot_ref, out_ref, level_ref=None):
    def body(g, carry):
        levels = []
        for j in range(group):
            e = g * group + j
            hot = one_hot(rows, place_ref[pl.ds(e, 1), :])
            hot_ref[pl.ds(j * rows, rows), :] = hot.astype(BF16)
            if level_ref is not None:
                levels.append(jnp.sum(hot * level_ref[pl.ds(e, 1), :], axis=1, keepdims=True))
        got = jnp.dot(hot_ref[...], tok_ref[...], preferred_element_type=F32)
        if level_ref is not None:
            got = got * jnp.concatenate(levels, axis=0)
        out_ref[pl.ds(pl.multiple_of(g * group * rows, group * rows), group * rows), :] = got.astype(BF16)
        return carry

    lax.fori_loop(0, experts // group, body, 0)


def places(zs, tok, experts, meta_ref, place_ref, level_ref, first):
    lane = lax.broadcasted_iota(jnp.int32, (TOPK, 2 * tok), 1)
    rows, ids, levels = [], [], []
    for d in range(zs):
        meta = meta_ref[d].astype(F32) + meta_ref[zs + d].astype(F32)
        kinds = [meta[0:TOPK, 2 * tok * n : 2 * tok * (n + 1)] for n in range(5)]
        block = 2 * d + (lane >= tok).astype(jnp.int32)
        rows.append(kinds[1] + block.astype(F32) * CAP)
        ids.append(kinds[0])
        levels.append(kinds[2] + kinds[3] + kinds[4])
    row, expert, level = (jnp.concatenate(v, axis=1) for v in (rows, ids, levels))
    for e in range(experts):
        hit = expert == (first + e).astype(F32)
        place_ref[e : e + 1, :] = jnp.max(jnp.where(hit, row, -1.0), axis=0, keepdims=True)
        level_ref[e : e + 1, :] = jnp.sum(jnp.where(hit, level, 0.0), axis=0, keepdims=True)


def expert_rows(ref, rows, e):
    return ref[pl.ds(pl.multiple_of(e * rows, rows), rows), :]


def at_rows(rows, j):
    return pl.ds(pl.multiple_of(j * rows, rows), rows)


def forward(rows, count, first, arrived, xin_ref, bufs, out_ref):
    def body(j):
        x = expert_rows(xin_ref, rows, first + j)
        arrived(j)
        for n, buf in enumerate(bufs):
            got = jnp.dot(x, buf[j], preferred_element_type=F32)
            out_ref[j, n * rows : (n + 1) * rows, :] = got.astype(out_ref.dtype)

    each(count, body)


def x_kernel(cfg, count, s_ref, *refs):
    zs, tok, experts, rows, group = cfg
    tokens = refs[: 2 * zs]
    gate_ref, up_ref, au_ref, xin_ref, place_ref, level_ref = refs[2 * zs : 2 * zs + 6]
    tok_ref, hot_ref, meta_ref, gate, up, sem, tok_sem = refs[2 * zs + 6 :]
    filling, routes = fill(tok_ref, tokens, s_ref[1], tok, tok_sem, meta_ref)
    copies = load((gate_ref, up_ref), s_ref[0], count, (gate, up), sem)
    ready(routes)
    places(zs, tok, experts, meta_ref, place_ref, level_ref, s_ref[2])
    ready(filling)
    dispatch(rows, experts, group, place_ref, tok_ref, hot_ref, xin_ref)
    forward(rows, count, s_ref[0], copies, xin_ref, (gate, up), au_ref)


def x2_kernel(rows, counts, s_ref, xin_ref, gate_ref, up_ref, au_ref, mine_ref, gate, up, gate_m, up_m, sem, sem_m):
    copies = load((gate_ref, up_ref), s_ref[0], counts[0], (gate, up), sem)
    copies_m = load((gate_ref, up_ref), s_ref[1], counts[1], (gate_m, up_m), sem_m)
    forward(rows, counts[0], s_ref[0], copies, xin_ref, (gate, up), au_ref)
    forward(rows, counts[1], s_ref[1], copies_m, xin_ref, (gate_m, up_m), mine_ref)


def back_dots(rows, count, first, arrived, yin_ref, down, out_ref):
    def body(j):
        y = expert_rows(yin_ref, rows, first + j)
        arrived(j)
        out_ref[j] = lax.dot_general(y, down[j], NT, preferred_element_type=F32).astype(out_ref.dtype)

    each(count, body)


def y_kernel(cfg, count, s_ref, *refs):
    zs, tok, experts, rows, group = cfg
    tokens = refs[: 2 * zs]
    place_ref, level_ref, down_ref, dh_ref, yin_ref, tok_ref, hot_ref, down, sem, tok_sem = refs[2 * zs :]
    filling, _ = fill(tok_ref, tokens, s_ref[1], tok, tok_sem)
    copies = load((down_ref,), s_ref[0], count, (down,), sem)
    ready(filling)
    dispatch(rows, experts, group, place_ref, tok_ref, hot_ref, yin_ref, level_ref)
    back_dots(rows, count, s_ref[0], copies, yin_ref, down, dh_ref)


def y2_kernel(rows, counts, s_ref, yin_ref, down_ref, dh_ref, mine_ref, down, down_m, sem, sem_m):
    copies = load((down_ref,), s_ref[0], counts[0], (down,), sem)
    copies_m = load((down_ref,), s_ref[1], counts[1], (down_m,), sem_m)
    back_dots(rows, counts[0], s_ref[0], copies, yin_ref, down, dh_ref)
    back_dots(rows, counts[1], s_ref[1], copies_m, yin_ref, down_m, mine_ref)


def final_kernel(rows, scale, at, s_ref, au_m, dh_m, au_r, dh_r, d_ref, score_ref):
    def body(j):
        au = au_m[at + j] + au_r[j].astype(F32)
        a, u = au[0:rows], au[rows:]
        dh = dh_m[at + j] + dh_r[j].astype(F32)
        sig = jax.nn.sigmoid(a)
        act = a * sig
        channel = jnp.sum(act * u * dh, axis=0, keepdims=True)
        score_ref[j] = channel * channel * scale
        d_ref[j, 0:rows, :] = (dh * u * sig * (1.0 + a * (1.0 - sig))).astype(BF16)
        d_ref[j, rows:, :] = (dh * act).astype(BF16)

    each(d_ref.shape[0], body)


def gradient_rows(rows, d_ref, arrived, gate, up, part_ref, at=0):
    def body(j):
        arrived(at + j)
        part = lax.dot_general(d_ref[j, 0:rows, :], gate[at + j], NT, preferred_element_type=F32)
        part = part + lax.dot_general(d_ref[j, rows:, :], up[at + j], NT, preferred_element_type=F32)
        part_ref[at_rows(rows, at + j), :] = part.astype(BF16)

    each(d_ref.shape[0], body)


def mine_parts_kernel(rows, sizes, s_ref, *refs):
    n = len(sizes)
    gate_ref, up_ref, part_ref, gate, up, sem = refs[n:]
    arrived = load((gate_ref, up_ref), s_ref[0], sum(sizes), (gate, up), sem)
    at = 0
    for d_ref, size in zip(refs[:n], sizes):
        gradient_rows(rows, d_ref, arrived, gate, up, part_ref, at)
        at += size


def combine_kernel(rows, zs, tok, half, at, count, s_ref, d_ref, gate_ref, up_ref, place_ref, *refs):
    first = s_ref[0] + at
    if at == 0:
        mine_ref, acc, gate, up, part_ref, hot_ref, sem = refs
    else:
        acc_in, keep_ref, send_ref, gate, up, part_ref, hot_ref, acc, sem = refs
    copies = load((gate_ref, up_ref), first, count, (gate, up), sem)

    def mark(start, e, n):
        def body(j):
            hot = one_hot(rows, place_ref[pl.ds(e + j, 1), :])
            hot_ref[at_rows(rows, start + j), :] = hot.astype(BF16)

        each(n, body)

    mark(half if at == 0 else 0, first, count)
    if at == 0:
        mark(0, half - s_ref[0], half)
    cut = half * rows if at == 0 else 0
    if at == 0:
        acc[...] = lax.dot_general(hot_ref[0:cut, :], mine_ref[...], TN, preferred_element_type=F32)
    gradient_rows(rows, d_ref, copies, gate, up, part_ref)
    total = lax.dot_general(hot_ref[cut:, :], part_ref[...], TN, preferred_element_type=F32)
    if at == 0:
        acc[...] += total
        return
    acc[...] = total + acc_in[...]
    side = s_ref[1]
    for d in range(zs):
        keep_ref[d] = acc[pl.ds(pl.multiple_of(2 * d * tok + side * tok, tok), tok), :]
        send_ref[d] = acc[pl.ds(pl.multiple_of(2 * d * tok + (1 - side) * tok, tok), tok), :].astype(BF16)


def stationary(tokens, out_grad, gates, expert_ids, slots, gate_weight, up_weight, down_weight):
    zs = lax.axis_size("expert")
    tok, width = tokens.shape
    experts, _, ff = gate_weight.shape
    rows = 2 * zs * CAP
    all_tok = 2 * zs * tok
    half = experts // 2
    group = 4 if experts % 4 == 0 else 1
    p, s, z = lax.axis_index("dp"), lax.axis_index("sub"), lax.axis_index("expert")
    mine0, other0 = half * p, half * (1 - p)
    first = half // 2
    rest = half - first
    sizes = [first, rest]

    def flip(v, axis):
        return lax.ppermute(v, axis, [(0, 1), (1, 0)])

    def turn(v, d):
        pairs = [
            ((i * 2 + a) * 2 + b, (((i + d) % zs) * 2 + b) * 2 + a)
            for i in range(zs)
            for a in range(2)
            for b in range(2)
        ]
        return lax.ppermute(v, ("expert", "dp", "sub"), pairs)

    def shift(v, d):
        return lax.ppermute(v, "expert", [(i, (i + d) % zs) for i in range(zs)])

    def sds(shape, dtype):
        return jax.ShapeDtypeStruct(shape, dtype)

    vmem, anywhere = pl.BlockSpec(memory_space=pltpu.VMEM), pl.BlockSpec(memory_space=pltpu.HBM)
    smem = pl.BlockSpec(memory_space=pltpu.SMEM)
    dma = pltpu.SemaphoreType.DMA

    def call(body, first, second, args, outs, scratch, flops, moved, name):
        ins = [spec for spec, group in args for _ in group]
        arrays = [v for _, group in args for v in group]
        info = jnp.stack([jnp.int32(first), jnp.int32(second), jnp.int32(z * experts)])
        return pl.pallas_call(
            body,
            out_shape=outs,
            in_specs=[smem] + ins,
            out_specs=jax.tree.map(lambda _: vmem, outs),
            scratch_shapes=scratch,
            compiler_params=pltpu.CompilerParams(vmem_limit_bytes=VMEM_LIMIT),
            cost_estimate=pl.CostEstimate(flops=int(flops * COST), bytes_accessed=int(moved * COST), transcendentals=0),
            name=name,
        )(info, *arrays)

    loaded = pl.pallas_call(
        pack_kernel,
        out_shape=sds((tok + ROUTE_ROWS, width), BF16),
        in_specs=[smem] + [vmem] * 4,
        out_specs=vmem,
        name="pack",
    )(jnp.stack([p]).astype(jnp.int32), tokens, expert_ids.T, slots.T, gates.T)
    x_own = [turn(loaded, d) for d in range(zs)]
    x_other = [flip(v, "sub") for v in x_own]
    out_grad, _ = lax.optimization_barrier((out_grad, loaded))
    y_here = turn(out_grad, 0)
    wbytes = width * ff * 2
    flop = 2 * rows * width * ff
    dflop = 2 * experts * rows * all_tok * width
    cfg = (zs, tok, experts, rows, group)
    hot = pltpu.VMEM((group * rows, all_tok), BF16)
    tok_scratch = pltpu.VMEM((all_tok, width), BF16)

    def wide(count):
        return pltpu.VMEM((count, width, ff), BF16)

    def tall(count):
        return pltpu.VMEM((count, ff, width), BF16)

    place_shape = sds((experts, all_tok), F32)
    rows_shape = sds((experts * rows, width), BF16)
    weights = (anywhere, (gate_weight, up_weight))
    au_first, xin, place, level = call(
        functools.partial(x_kernel, cfg, first),
        other0,
        s,
        [(anywhere, (*x_own, *x_other)), weights],
        [sds((first, 2 * rows, ff), BF16), rows_shape, place_shape, place_shape],
        [tok_scratch, hot, pltpu.VMEM((2 * zs, ROUTE_ROWS, width), BF16), wide(first), wide(first)]
        + [dma((2 * first,)), dma((4 * zs,))],
        2 * first * flop + dflop,
        2 * first * wbytes,
        "x_first",
    )
    y_here, au_first = lax.optimization_barrier((y_here, au_first))
    y_own = [y_here] + [shift(y_here, d) for d in range(1, zs)]
    au_rest, au_mine = call(
        functools.partial(x2_kernel, rows, (rest, half)),
        other0 + first,
        mine0,
        [(vmem, (xin,)), weights],
        [sds((rest, 2 * rows, ff), BF16), sds((half, 2 * rows, ff), F32)],
        [wide(rest), wide(rest), wide(half), wide(half), dma((2 * rest,)), dma((2 * half,))],
        2 * (rest + half) * flop,
        2 * (rest + half) * wbytes,
        "x_rest",
    )
    au_recv = [flip(v, "dp") for v in (au_first, au_rest)]
    *y_own, au_mine = lax.optimization_barrier((*y_own, au_mine))
    y_other = [flip(v, "sub") for v in y_own]
    dh_first, yin = call(
        functools.partial(y_kernel, cfg, first),
        other0,
        s,
        [(anywhere, (*y_own, *y_other)), (vmem, (place, level)), (anywhere, (down_weight,))],
        [sds((first, rows, ff), BF16), rows_shape],
        [tok_scratch, hot, tall(first), dma((first,)), dma((2 * zs,))],
        first * flop + dflop,
        first * wbytes,
        "y_first",
    )
    dh_rest, dh_mine = call(
        functools.partial(y2_kernel, rows, (rest, half)),
        other0 + first,
        mine0,
        [(vmem, (yin,)), (anywhere, (down_weight,))],
        [sds((rest, rows, ff), BF16), sds((half, rows, ff), F32)],
        [tall(rest), tall(half), dma((rest,)), dma((half,))],
        (rest + half) * flop,
        (rest + half) * wbytes,
        "y_rest",
    )
    dh_recv = [flip(v, "dp") for v in (dh_first, dh_rest)]
    scale = LOCAL_EXPERTS / (all_tok * TOPK)
    grads, back, scores = [], [], []
    for k, n in enumerate(sizes):
        d, score = call(
            functools.partial(final_kernel, rows, scale, k * first),
            mine0,
            s,
            [(vmem, (au_mine, dh_mine, au_recv[k], dh_recv[k]))],
            [sds((n, 2 * rows, ff), BF16), sds((n, 1, ff), F32)],
            [],
            n * rows * ff * 40,
            n * rows * ff * 30,
            "final",
        )
        dh_mine, d = lax.optimization_barrier((dh_mine, d))
        grads.append(d)
        scores.append(score)
        back.append(flip(d, "dp"))
    score = jnp.concatenate(scores, axis=0).reshape(half, ff)
    score_other = flip(score, "dp")
    scores = jnp.concatenate(
        [jnp.where(p == 0, score, score_other), jnp.where(p == 0, score_other, score)], axis=0
    )
    back[0], scores = lax.optimization_barrier((back[0], scores))
    mine_parts = call(
        functools.partial(mine_parts_kernel, rows, sizes),
        mine0,
        s,
        [(vmem, grads), weights],
        sds((half * rows, width), BF16),
        [wide(half), wide(half), dma((2 * half,))],
        2 * half * flop,
        2 * half * wbytes,
        "mine_parts",
    )
    acc_shape, zshape = (all_tok, width), (zs, tok, width)
    given = mine_parts
    for k, n in enumerate(sizes):
        used = n + half * (k == 0)
        given = call(
            functools.partial(combine_kernel, rows, zs, tok, half, k * first, n),
            other0,
            s,
            [(vmem, (back[k],)), weights, (vmem, (place, given))],
            sds(acc_shape, F32) if k == 0 else [sds(zshape, F32), sds(zshape, BF16)],
            [wide(n), wide(n), pltpu.VMEM((n * rows, width), BF16), pltpu.VMEM((used * rows, all_tok), BF16)]
            + ([] if k == 0 else [pltpu.VMEM(acc_shape, F32)])
            + [dma((2 * n,))],
            2 * n * flop + 2 * used * rows * width * all_tok,
            2 * n * wbytes,
            "combine",
        )
    keep, send = given
    summed = (keep + flip(send, "sub").astype(F32)).astype(BF16)
    total = turn(summed[0], 0).astype(F32)
    for d in range(1, zs):
        total = total + turn(summed[d], -d).astype(F32)
    return (scores, total.astype(BF16))


def solution(mesh):
    in_specs = (
        P(("dom", "expert", "dp"), "sub"),
        P(("dom", "expert", "dp"), "sub"),
        P(("dom", "expert", "dp"), None),
        P(("dom", "expert", "dp"), None),
        P(("dom", "expert", "dp"), None),
        P("expert", "dp", "sub"),
        P("expert", "dp", "sub"),
        P("expert", "sub", "dp"),
    )
    out_specs = (P(("dom", "expert"), "sub"), P(("dom", "expert", "dp"), "sub"))
    pairs = mesh.shape["dp"] == 2 and mesh.shape["sub"] == 2
    split = (LOCAL_EXPERTS // mesh.shape["expert"]) % 2 == 0
    local = stationary if pairs and split else gathered
    return jax.shard_map(local, mesh=mesh, in_specs=in_specs, out_specs=out_specs, check_vma=False)
```

```python
import functools

import jax
import jax.numpy as jnp
from jax import lax
from jax.experimental import pallas as pl
from jax.experimental.pallas import tpu as pltpu
from jax.sharding import PartitionSpec as P

LOCAL_EXPERTS = 64
TOPK = 8
CAP = 10
F32 = jnp.float32
BF16 = jnp.bfloat16
NT = (((1,), (1,)), ((), ()))
TN = (((0,), (0,)), ((), ()))
VMEM_LIMIT = 32 * 1024 * 1024


def gathered(tokens, out_grad, gates, expert_ids, slots, gate_weight, up_weight, down_weight):
    expert_count = lax.axis_size("expert")
    group_count = lax.axis_size("dp")
    local_count = gate_weight.shape[0]
    tok_rows = tokens.shape[0]
    half_width = tokens.shape[1]
    slot_count = local_count * expert_count * CAP
    target_dev = expert_ids // local_count
    local_expert = expert_ids % local_count
    slot_rows = ((local_expert * expert_count + target_dev) * CAP + slots).reshape(-1)
    scaled = (gates[:, :, None] * out_grad[:, None, :].astype(F32)).astype(BF16)
    scaled = scaled.reshape(tok_rows * TOPK, half_width)
    repeated = jnp.repeat(tokens, TOPK, axis=0)

    def route(rows):
        send = jnp.zeros((slot_count, half_width), BF16).at[slot_rows].add(rows)
        send = send.reshape(local_count, expert_count, CAP, half_width)
        recv = lax.all_to_all(send, "expert", split_axis=1, concat_axis=1, tiled=True)
        full = lax.all_gather(recv, "sub", axis=3, tiled=True)
        return full.reshape(local_count, expert_count * CAP, full.shape[3])

    x_full, grad_full = route(repeated), route(scaled)
    gate_full = lax.all_gather(gate_weight, "dp", axis=1, tiled=True)
    up_full = lax.all_gather(up_weight, "dp", axis=1, tiled=True)
    down_full = lax.all_gather(down_weight, "dp", axis=2, tiled=True)
    gate_pre = jnp.einsum("erd,edf->erf", x_full, gate_full, preferred_element_type=F32)
    up_pre = jnp.einsum("erd,edf->erf", x_full, up_full, preferred_element_type=F32)
    hidden_grad = jnp.einsum("erd,efd->erf", grad_full, down_full, preferred_element_type=F32)
    gating = jax.nn.sigmoid(gate_pre)
    activated = gate_pre * gating
    channel = lax.psum(jnp.sum(activated * up_pre * hidden_grad, axis=1), "dp")
    scale = LOCAL_EXPERTS / (tok_rows * expert_count * group_count * TOPK)
    scores = channel * channel * scale
    gate_grad = (hidden_grad * up_pre * gating * (1.0 + gate_pre * (1.0 - gating))).astype(BF16)
    up_grad = (hidden_grad * activated).astype(BF16)
    parts = jnp.einsum("erf,edf->erd", gate_grad, gate_full, preferred_element_type=F32)
    parts = parts + jnp.einsum("erf,edf->erd", up_grad, up_full, preferred_element_type=F32)
    summed = lax.psum_scatter(parts.astype(BF16), "sub", scatter_dimension=2, tiled=True)
    summed = summed.reshape(local_count, expert_count, CAP, half_width)
    returned = lax.all_to_all(summed, "expert", split_axis=1, concat_axis=1, tiled=True)
    picked = returned.reshape(slot_count, half_width)[slot_rows].astype(F32)
    token_grad = jnp.sum(picked.reshape(tok_rows, TOPK, half_width), axis=1)
    return (scores, token_grad.astype(BF16))


MINE_COST = 1
PART_COST = 1
SIZES = (1, 1)
COST = 1.0


ROUTE_ROWS = 16


def each(count, body):
    def step(j, carry):
        body(j)
        return carry

    lax.fori_loop(0, count, step, 0)


def load(sources, first, count, buffers, sem):
    def copies(j):
        return [
            pltpu.make_async_copy(source.at[first + j], buffer.at[j], sem.at[j * len(sources) + n])
            for n, (source, buffer) in enumerate(zip(sources, buffers))
        ]

    def start(j):
        for copy in copies(j):
            copy.start()

    each(count, start)
    return lambda j: ready(copies(j))


def ready(line):
    for copy in line:
        copy.wait()


def one_hot(rows, place):
    index = lax.broadcasted_iota(jnp.int32, (rows, place.shape[1]), 0).astype(F32)
    return jnp.where(index == place, 1.0, 0.0)


def pack_kernel(p_ref, tokens_ref, ids_ref, slots_ref, gates_ref, out_ref):
    tok = tokens_ref.shape[0]
    out_ref[0:tok, :] = tokens_ref[...]
    out_ref[tok:, :] = jnp.zeros((ROUTE_ROWS, out_ref.shape[1]), BF16)
    lane = lax.broadcasted_iota(jnp.int32, (tok, 2 * tok), 1)
    row = lax.broadcasted_iota(jnp.int32, (tok, 2 * tok), 0) + p_ref[0] * tok
    place = jnp.where(lane == row, 1.0, 0.0).astype(BF16)
    left = gates_ref[...]
    kinds = [ids_ref[...].astype(F32), slots_ref[...].astype(F32)]
    for _ in range(3):
        kinds.append(left.astype(BF16).astype(F32))
        left = left - kinds[-1]
    kinds = jnp.concatenate(kinds, axis=0).astype(BF16)
    moved = jnp.dot(kinds, place, preferred_element_type=F32)
    none = jnp.zeros((ROUTE_ROWS - TOPK, 2 * tok), F32)
    for n in range(5):
        block = jnp.concatenate([moved[n * TOPK : (n + 1) * TOPK], none], axis=0)
        out_ref[tok:, 2 * tok * n : 2 * tok * (n + 1)] = block.astype(BF16)


def fill(tok_ref, token_refs, side, tok, sem, meta_ref=None):
    copies = []
    zs = len(token_refs) // 2
    for n, ref in enumerate(token_refs):
        d, part = n % zs, side if n < zs else 1 - side
        start = pl.multiple_of(2 * d * tok + part * tok, tok)
        copies.append(pltpu.make_async_copy(ref.at[pl.ds(0, tok)], tok_ref.at[pl.ds(start, tok)], sem.at[n]))
        copies[-1].start()
    routes = []
    if meta_ref is not None:
        for n, ref in enumerate(token_refs):
            source = ref.at[pl.ds(tok, ROUTE_ROWS)]
            routes.append(pltpu.make_async_copy(source, meta_ref.at[n], sem.at[2 * zs + n]))
            routes[-1].start()
    return copies, routes


def dispatch(rows, experts, group, place_ref, tok_ref, hot_ref, out_ref, level_ref=None):
    def body(g, carry):
        levels = []
        for j in range(group):
            e = g * group + j
            hot = one_hot(rows, place_ref[pl.ds(e, 1), :])
            hot_ref[pl.ds(j * rows, rows), :] = hot.astype(BF16)
            if level_ref is not None:
                levels.append(jnp.sum(hot * level_ref[pl.ds(e, 1), :], axis=1, keepdims=True))
        got = jnp.dot(hot_ref[...], tok_ref[...], preferred_element_type=F32)
        if level_ref is not None:
            got = got * jnp.concatenate(levels, axis=0)
        out_ref[pl.ds(pl.multiple_of(g * group * rows, group * rows), group * rows), :] = got.astype(BF16)
        return carry

    lax.fori_loop(0, experts // group, body, 0)


def places(zs, tok, experts, meta_ref, place_ref, level_ref, first):
    lane = lax.broadcasted_iota(jnp.int32, (TOPK, 2 * tok), 1)
    rows, ids, levels = [], [], []
    for d in range(zs):
        meta = meta_ref[d].astype(F32) + meta_ref[zs + d].astype(F32)
        kinds = [meta[0:TOPK, 2 * tok * n : 2 * tok * (n + 1)] for n in range(5)]
        block = 2 * d + (lane >= tok).astype(jnp.int32)
        rows.append(kinds[1] + block.astype(F32) * CAP)
        ids.append(kinds[0])
        levels.append(kinds[2] + kinds[3] + kinds[4])
    row, expert, level = (jnp.concatenate(v, axis=1) for v in (rows, ids, levels))
    for e in range(experts):
        hit = expert == (first + e).astype(F32)
        place_ref[e : e + 1, :] = jnp.max(jnp.where(hit, row, -1.0), axis=0, keepdims=True)
        level_ref[e : e + 1, :] = jnp.sum(jnp.where(hit, level, 0.0), axis=0, keepdims=True)


def expert_rows(ref, rows, e):
    return ref[pl.ds(pl.multiple_of(e * rows, rows), rows), :]


def at_rows(rows, j):
    return pl.ds(pl.multiple_of(j * rows, rows), rows)


def forward(rows, count, first, arrived, xin_ref, bufs, out_ref):
    def body(j):
        x = expert_rows(xin_ref, rows, first + j)
        arrived(j)
        for n, buf in enumerate(bufs):
            got = jnp.dot(x, buf[j], preferred_element_type=F32)
            out_ref[j, n * rows : (n + 1) * rows, :] = got.astype(out_ref.dtype)

    each(count, body)


def x_kernel(cfg, count, s_ref, *refs):
    zs, tok, experts, rows, group = cfg
    tokens = refs[: 2 * zs]
    gate_ref, up_ref, au_ref, xin_ref, place_ref, level_ref = refs[2 * zs : 2 * zs + 6]
    tok_ref, hot_ref, meta_ref, gate, up, sem, tok_sem = refs[2 * zs + 6 :]
    filling, routes = fill(tok_ref, tokens, s_ref[1], tok, tok_sem, meta_ref)
    copies = load((gate_ref, up_ref), s_ref[0], count, (gate, up), sem)
    ready(routes)
    places(zs, tok, experts, meta_ref, place_ref, level_ref, s_ref[2])
    ready(filling)
    dispatch(rows, experts, group, place_ref, tok_ref, hot_ref, xin_ref)
    forward(rows, count, s_ref[0], copies, xin_ref, (gate, up), au_ref)


def x2_kernel(rows, count, s_ref, xin_ref, gate_ref, up_ref, au_ref, gate, up, sem):
    copies = load((gate_ref, up_ref), s_ref[0], count, (gate, up), sem)
    forward(rows, count, s_ref[0], copies, xin_ref, (gate, up), au_ref)


def back_dots(rows, count, first, arrived, yin_ref, down, out_ref):
    def body(j):
        y = expert_rows(yin_ref, rows, first + j)
        arrived(j)
        out_ref[j] = lax.dot_general(y, down[j], NT, preferred_element_type=F32).astype(out_ref.dtype)

    each(count, body)


def y_kernel(cfg, count, s_ref, *refs):
    zs, tok, experts, rows, group = cfg
    tokens = refs[: 2 * zs]
    place_ref, level_ref, down_ref, dh_ref, yin_ref, tok_ref, hot_ref, down, sem, tok_sem = refs[2 * zs :]
    filling, _ = fill(tok_ref, tokens, s_ref[1], tok, tok_sem)
    copies = load((down_ref,), s_ref[0], count, (down,), sem)
    ready(filling)
    dispatch(rows, experts, group, place_ref, tok_ref, hot_ref, yin_ref, level_ref)
    back_dots(rows, count, s_ref[0], copies, yin_ref, down, dh_ref)


def y2_kernel(rows, counts, s_ref, yin_ref, down_ref, dh_ref, mine_ref, down, down_m, sem, sem_m):
    copies = load((down_ref,), s_ref[0], counts[0], (down,), sem)
    copies_m = load((down_ref,), s_ref[1], counts[1], (down_m,), sem_m)
    back_dots(rows, counts[0], s_ref[0], copies, yin_ref, down, dh_ref)
    back_dots(rows, counts[1], s_ref[1], copies_m, yin_ref, down_m, mine_ref)


def final_kernel(rows, scale, at, s_ref, au_m, dh_m, au_r, dh_r, d_ref, score_ref):
    def body(j):
        au = au_m[at + j] + au_r[j].astype(F32)
        a, u = au[0:rows], au[rows:]
        dh = dh_m[at + j] + dh_r[j].astype(F32)
        sig = jax.nn.sigmoid(a)
        act = a * sig
        channel = jnp.sum(act * u * dh, axis=0, keepdims=True)
        score_ref[j] = channel * channel * scale
        d_ref[j, 0:rows, :] = (dh * u * sig * (1.0 + a * (1.0 - sig))).astype(BF16)
        d_ref[j, rows:, :] = (dh * act).astype(BF16)

    each(d_ref.shape[0], body)


def gradient_rows(rows, d_ref, arrived, gate, up, part_ref, at=0):
    def body(j):
        arrived(at + j)
        part = lax.dot_general(d_ref[j, 0:rows, :], gate[at + j], NT, preferred_element_type=F32)
        part = part + lax.dot_general(d_ref[j, rows:, :], up[at + j], NT, preferred_element_type=F32)
        part_ref[at_rows(rows, at + j), :] = part.astype(BF16)

    each(d_ref.shape[0], body)


def mine_parts_kernel(rows, s_ref, d_ref, gate_ref, up_ref, part_ref, gate, up, sem):
    arrived = load((gate_ref, up_ref), s_ref[0], d_ref.shape[0], (gate, up), sem)
    gradient_rows(rows, d_ref, arrived, gate, up, part_ref)


def combine_kernel(rows, zs, tok, half, at, count, s_ref, d_ref, gate_ref, up_ref, place_ref, *refs):
    first = s_ref[0] + at
    if at == 0:
        *mine_refs, acc, gate, up, part_ref, hot_ref, sem = refs
    else:
        acc_in, keep_ref, send_ref, gate, up, part_ref, hot_ref, acc, sem = refs
    copies = load((gate_ref, up_ref), first, count, (gate, up), sem)

    def mark(start, e, n):
        def body(j):
            hot = one_hot(rows, place_ref[pl.ds(e + j, 1), :])
            hot_ref[at_rows(rows, start + j), :] = hot.astype(BF16)

        each(n, body)

    mark(half if at == 0 else 0, first, count)
    if at == 0:
        mark(0, half - s_ref[0], half)
    cut = 0
    if at == 0:
        for n, mine_ref in enumerate(mine_refs):
            size = mine_ref.shape[0]
            own = lax.dot_general(hot_ref[cut : cut + size, :], mine_ref[...], TN, preferred_element_type=F32)
            acc[...] = own if n == 0 else acc[...] + own
            cut += size
    gradient_rows(rows, d_ref, copies, gate, up, part_ref)
    total = lax.dot_general(hot_ref[cut:, :], part_ref[...], TN, preferred_element_type=F32)
    if at == 0:
        acc[...] += total
        return
    acc[...] = total + acc_in[...]
    side = s_ref[1]
    for d in range(zs):
        keep_ref[d] = acc[pl.ds(pl.multiple_of(2 * d * tok + side * tok, tok), tok), :]
        send_ref[d] = acc[pl.ds(pl.multiple_of(2 * d * tok + (1 - side) * tok, tok), tok), :].astype(BF16)


def stationary(tokens, out_grad, gates, expert_ids, slots, gate_weight, up_weight, down_weight):
    zs = lax.axis_size("expert")
    tok, width = tokens.shape
    experts, _, ff = gate_weight.shape
    rows = 2 * zs * CAP
    all_tok = 2 * zs * tok
    half = experts // 2
    group = 4 if experts % 4 == 0 else 1
    p, s, z = lax.axis_index("dp"), lax.axis_index("sub"), lax.axis_index("expert")
    mine0, other0 = half * p, half * (1 - p)
    first = half // 2
    rest = half - first
    sizes = [first, rest]

    def flip(v, axis):
        return lax.ppermute(v, axis, [(0, 1), (1, 0)])

    def turn(v, d):
        pairs = [
            ((i * 2 + a) * 2 + b, (((i + d) % zs) * 2 + b) * 2 + a)
            for i in range(zs)
            for a in range(2)
            for b in range(2)
        ]
        return lax.ppermute(v, ("expert", "dp", "sub"), pairs)

    def shift(v, d):
        return lax.ppermute(v, "expert", [(i, (i + d) % zs) for i in range(zs)])

    def sds(shape, dtype):
        return jax.ShapeDtypeStruct(shape, dtype)

    vmem, anywhere = pl.BlockSpec(memory_space=pltpu.VMEM), pl.BlockSpec(memory_space=pltpu.HBM)
    smem = pl.BlockSpec(memory_space=pltpu.SMEM)
    dma = pltpu.SemaphoreType.DMA

    def call(body, first, second, args, outs, scratch, flops, moved, name, factor=1):
        ins = [spec for spec, group in args for _ in group]
        arrays = [v for _, group in args for v in group]
        info = jnp.stack([jnp.int32(first), jnp.int32(second), jnp.int32(z * experts)])
        return pl.pallas_call(
            body,
            out_shape=outs,
            in_specs=[smem] + ins,
            out_specs=jax.tree.map(lambda _: vmem, outs),
            scratch_shapes=scratch,
            compiler_params=pltpu.CompilerParams(vmem_limit_bytes=VMEM_LIMIT),
            cost_estimate=pl.CostEstimate(flops=int(flops * COST * factor), bytes_accessed=int(moved * COST * factor), transcendentals=0),
            name=name,
        )(info, *arrays)

    loaded = pl.pallas_call(
        pack_kernel,
        out_shape=sds((tok + ROUTE_ROWS, width), BF16),
        in_specs=[smem] + [vmem] * 4,
        out_specs=vmem,
        name="pack",
    )(jnp.stack([p]).astype(jnp.int32), tokens, expert_ids.T, slots.T, gates.T)
    x_own = [turn(loaded, d) for d in range(zs)]
    x_other = [flip(v, "sub") for v in x_own]
    out_grad, _ = lax.optimization_barrier((out_grad, loaded))
    y_here = turn(out_grad, 0)
    wbytes = width * ff * 2
    flop = 2 * rows * width * ff
    dflop = 2 * experts * rows * all_tok * width
    cfg = (zs, tok, experts, rows, group)
    hot = pltpu.VMEM((group * rows, all_tok), BF16)
    tok_scratch = pltpu.VMEM((all_tok, width), BF16)

    def wide(count):
        return pltpu.VMEM((count, width, ff), BF16)

    def tall(count):
        return pltpu.VMEM((count, ff, width), BF16)

    place_shape = sds((experts, all_tok), F32)
    rows_shape = sds((experts * rows, width), BF16)
    def pinned(*arrays):
        return tuple(pltpu.with_memory_space_constraint(v, pltpu.HBM) for v in arrays)

    weights = (anywhere, pinned(gate_weight, up_weight))
    down_weight, = pinned(down_weight)
    au_first, xin, place, level = call(
        functools.partial(x_kernel, cfg, first),
        other0,
        s,
        [(anywhere, pinned(*x_own, *x_other)), weights],
        [sds((first, 2 * rows, ff), BF16), rows_shape, place_shape, place_shape],
        [tok_scratch, hot, pltpu.VMEM((2 * zs, ROUTE_ROWS, width), BF16), wide(first), wide(first)]
        + [dma((2 * first,)), dma((4 * zs,))],
        2 * first * flop + dflop,
        2 * first * wbytes,
        "x_first",
    )
    y_here, au_first = lax.optimization_barrier((y_here, au_first))
    y_own = [y_here] + [shift(y_here, d) for d in range(1, zs)]

    def x_call(first, n, dtype, name, factor):
        return call(
            functools.partial(x2_kernel, rows, n),
            first,
            s,
            [(vmem, (xin,)), weights],
            sds((n, 2 * rows, ff), dtype),
            [wide(n), wide(n), dma((2 * n,))],
            2 * n * flop,
            2 * n * wbytes,
            name,
            factor,
        )

    au_rest = x_call(other0 + first, rest, BF16, "x_other", 1)
    xin, au_rest = lax.optimization_barrier((xin, au_rest))
    au_mine = x_call(mine0, half, F32, "x_mine", MINE_COST)
    au_recv = [flip(v, "dp") for v in (au_first, au_rest)]
    *y_own, au_mine = lax.optimization_barrier((*y_own, au_mine))
    place, au_recv[0] = lax.optimization_barrier((place, au_recv[0]))
    y_other = [flip(v, "sub") for v in y_own]
    dh_first, yin = call(
        functools.partial(y_kernel, cfg, first),
        other0,
        s,
        [(anywhere, pinned(*y_own, *y_other)), (vmem, (place, level)), (anywhere, (down_weight,))],
        [sds((first, rows, ff), BF16), rows_shape],
        [tok_scratch, hot, tall(first), dma((first,)), dma((2 * zs,))],
        first * flop + dflop,
        first * wbytes,
        "y_first",
    )
    yin, au_recv[1] = lax.optimization_barrier((yin, au_recv[1]))
    dh_rest, dh_mine = call(
        functools.partial(y2_kernel, rows, (rest, half)),
        other0 + first,
        mine0,
        [(vmem, (yin,)), (anywhere, (down_weight,))],
        [sds((rest, rows, ff), BF16), sds((half, rows, ff), F32)],
        [tall(rest), tall(half), dma((rest,)), dma((half,))],
        (rest + half) * flop,
        (rest + half) * wbytes,
        "y_rest",
    )
    dh_recv = [flip(v, "dp") for v in (dh_first, dh_rest)]
    scale = LOCAL_EXPERTS / (all_tok * TOPK)
    given, back, scores = [], [], []
    for k, n in enumerate(sizes):
        d, score = call(
            functools.partial(final_kernel, rows, scale, k * first),
            mine0,
            s,
            [(vmem, (au_mine, dh_mine, au_recv[k], dh_recv[k]))],
            [sds((n, 2 * rows, ff), BF16), sds((n, 1, ff), F32)],
            [],
            n * rows * ff * 40,
            n * rows * ff * 30,
            "final",
        )
        scores.append(score)
        back.append(flip(d, "dp"))
        part = call(
            functools.partial(mine_parts_kernel, rows),
            mine0 + k * first,
            s,
            [(vmem, (d,)), weights],
            sds((n * rows, width), BF16),
            [wide(n), wide(n), dma((2 * n,))],
            2 * n * flop,
            2 * n * wbytes,
            "mine_parts",
            PART_COST,
        )
        dh_mine, part = lax.optimization_barrier((dh_mine, part))
        given.append(part)
    score = jnp.concatenate(scores, axis=0).reshape(half, ff)
    score_other = flip(score, "dp")
    acc_shape, zshape = (all_tok, width), (zs, tok, width)
    for k, n in enumerate(sizes):
        used = n + half * (k == 0)
        given = call(
            functools.partial(combine_kernel, rows, zs, tok, half, k * first, n),
            other0,
            s,
            [(vmem, (back[k],)), weights, (vmem, (place, *given))],
            sds(acc_shape, F32) if k == 0 else [sds(zshape, F32), sds(zshape, BF16)],
            [wide(n), wide(n), pltpu.VMEM((n * rows, width), BF16), pltpu.VMEM((used * rows, all_tok), BF16)]
            + ([] if k == 0 else [pltpu.VMEM(acc_shape, F32)])
            + [dma((2 * n,))],
            2 * n * flop + 2 * used * rows * width * all_tok,
            2 * n * wbytes,
            "combine",
        )
        given = [given] if k == 0 else given
    keep, send = given
    summed = (keep + flip(send, "sub").astype(F32)).astype(BF16)
    summed, score_other = lax.optimization_barrier((summed, score_other))
    scores = jnp.concatenate(
        [jnp.where(p == 0, score, score_other), jnp.where(p == 0, score_other, score)], axis=0
    )
    total = turn(summed[0], 0).astype(F32)
    for d in range(1, zs):
        total = total + turn(summed[d], -d).astype(F32)
    return (scores, total.astype(BF16))


def solution(mesh):
    in_specs = (
        P(("dom", "expert", "dp"), "sub"),
        P(("dom", "expert", "dp"), "sub"),
        P(("dom", "expert", "dp"), None),
        P(("dom", "expert", "dp"), None),
        P(("dom", "expert", "dp"), None),
        P("expert", "dp", "sub"),
        P("expert", "dp", "sub"),
        P("expert", "sub", "dp"),
    )
    out_specs = (P(("dom", "expert"), "sub"), P(("dom", "expert", "dp"), "sub"))
    pairs = mesh.shape["dp"] == 2 and mesh.shape["sub"] == 2
    split = (LOCAL_EXPERTS // mesh.shape["expert"]) % 2 == 0
    local = stationary if pairs and split else gathered
    return jax.shard_map(local, mesh=mesh, in_specs=in_specs, out_specs=out_specs, check_vma=False)
```

```python
import functools

import jax
import jax.numpy as jnp
from jax import lax
from jax.experimental import pallas as pl
from jax.experimental.pallas import tpu as pltpu
from jax.sharding import PartitionSpec as P

LOCAL_EXPERTS = 64
TOPK = 8
CAP = 10
F32 = jnp.float32
BF16 = jnp.bfloat16
NT = (((1,), (1,)), ((), ()))
TN = (((0,), (0,)), ((), ()))
VMEM_LIMIT = 32 * 1024 * 1024


def gathered(tokens, out_grad, gates, expert_ids, slots, gate_weight, up_weight, down_weight):
    expert_count = lax.axis_size("expert")
    group_count = lax.axis_size("dp")
    local_count = gate_weight.shape[0]
    tok_rows = tokens.shape[0]
    half_width = tokens.shape[1]
    slot_count = local_count * expert_count * CAP
    target_dev = expert_ids // local_count
    local_expert = expert_ids % local_count
    slot_rows = ((local_expert * expert_count + target_dev) * CAP + slots).reshape(-1)
    scaled = (gates[:, :, None] * out_grad[:, None, :].astype(F32)).astype(BF16)
    scaled = scaled.reshape(tok_rows * TOPK, half_width)
    repeated = jnp.repeat(tokens, TOPK, axis=0)

    def route(rows):
        send = jnp.zeros((slot_count, half_width), BF16).at[slot_rows].add(rows)
        send = send.reshape(local_count, expert_count, CAP, half_width)
        recv = lax.all_to_all(send, "expert", split_axis=1, concat_axis=1, tiled=True)
        full = lax.all_gather(recv, "sub", axis=3, tiled=True)
        return full.reshape(local_count, expert_count * CAP, full.shape[3])

    x_full, grad_full = route(repeated), route(scaled)
    gate_full = lax.all_gather(gate_weight, "dp", axis=1, tiled=True)
    up_full = lax.all_gather(up_weight, "dp", axis=1, tiled=True)
    down_full = lax.all_gather(down_weight, "dp", axis=2, tiled=True)
    gate_pre = jnp.einsum("erd,edf->erf", x_full, gate_full, preferred_element_type=F32)
    up_pre = jnp.einsum("erd,edf->erf", x_full, up_full, preferred_element_type=F32)
    hidden_grad = jnp.einsum("erd,efd->erf", grad_full, down_full, preferred_element_type=F32)
    gating = jax.nn.sigmoid(gate_pre)
    activated = gate_pre * gating
    channel = lax.psum(jnp.sum(activated * up_pre * hidden_grad, axis=1), "dp")
    scale = LOCAL_EXPERTS / (tok_rows * expert_count * group_count * TOPK)
    scores = channel * channel * scale
    gate_grad = (hidden_grad * up_pre * gating * (1.0 + gate_pre * (1.0 - gating))).astype(BF16)
    up_grad = (hidden_grad * activated).astype(BF16)
    parts = jnp.einsum("erf,edf->erd", gate_grad, gate_full, preferred_element_type=F32)
    parts = parts + jnp.einsum("erf,edf->erd", up_grad, up_full, preferred_element_type=F32)
    summed = lax.psum_scatter(parts.astype(BF16), "sub", scatter_dimension=2, tiled=True)
    summed = summed.reshape(local_count, expert_count, CAP, half_width)
    returned = lax.all_to_all(summed, "expert", split_axis=1, concat_axis=1, tiled=True)
    picked = returned.reshape(slot_count, half_width)[slot_rows].astype(F32)
    token_grad = jnp.sum(picked.reshape(tok_rows, TOPK, half_width), axis=1)
    return (scores, token_grad.astype(BF16))


MINE_COST = 1
PART_COST = 1
COST = 1.0


ROUTE_ROWS = 16


def each(count, body):
    def step(j, carry):
        body(j)
        return carry

    lax.fori_loop(0, count, step, 0)


def load(sources, first, count, buffers, sem):
    def copies(j):
        return [
            pltpu.make_async_copy(source.at[first + j], buffer.at[j], sem.at[j * len(sources) + n])
            for n, (source, buffer) in enumerate(zip(sources, buffers))
        ]

    def start(j):
        for copy in copies(j):
            copy.start()

    each(count, start)
    return lambda j: ready(copies(j))


def ready(line):
    for copy in line:
        copy.wait()


def one_hot(rows, place):
    index = lax.broadcasted_iota(jnp.int32, (rows, place.shape[1]), 0).astype(F32)
    return jnp.where(index == place, 1.0, 0.0)


def pack_kernel(p_ref, tokens_ref, ids_ref, slots_ref, gates_ref, out_ref):
    tok = tokens_ref.shape[0]
    out_ref[0:tok, :] = tokens_ref[...]
    out_ref[tok:, :] = jnp.zeros((ROUTE_ROWS, out_ref.shape[1]), BF16)
    lane = lax.broadcasted_iota(jnp.int32, (tok, 2 * tok), 1)
    row = lax.broadcasted_iota(jnp.int32, (tok, 2 * tok), 0) + p_ref[0] * tok
    place = jnp.where(lane == row, 1.0, 0.0).astype(BF16)
    left = gates_ref[...]
    kinds = [ids_ref[...].astype(F32), slots_ref[...].astype(F32)]
    for _ in range(3):
        kinds.append(left.astype(BF16).astype(F32))
        left = left - kinds[-1]
    kinds = jnp.concatenate(kinds, axis=0).astype(BF16)
    moved = jnp.dot(kinds, place, preferred_element_type=F32)
    none = jnp.zeros((ROUTE_ROWS - TOPK, 2 * tok), F32)
    for n in range(5):
        block = jnp.concatenate([moved[n * TOPK : (n + 1) * TOPK], none], axis=0)
        out_ref[tok:, 2 * tok * n : 2 * tok * (n + 1)] = block.astype(BF16)


def fill(tok_ref, token_refs, side, tok, sem, meta_ref=None):
    copies = []
    zs = len(token_refs) // 2
    for n, ref in enumerate(token_refs):
        d, part = n % zs, side if n < zs else 1 - side
        start = pl.multiple_of(2 * d * tok + part * tok, tok)
        copies.append(pltpu.make_async_copy(ref.at[pl.ds(0, tok)], tok_ref.at[pl.ds(start, tok)], sem.at[n]))
        copies[-1].start()
    routes = []
    if meta_ref is not None:
        for n, ref in enumerate(token_refs):
            source = ref.at[pl.ds(tok, ROUTE_ROWS)]
            routes.append(pltpu.make_async_copy(source, meta_ref.at[n], sem.at[2 * zs + n]))
            routes[-1].start()
    return copies, routes


def dispatch(rows, experts, group, place_ref, tok_ref, hot_ref, out_ref, level_ref=None):
    def body(g, carry):
        levels = []
        for j in range(group):
            e = g * group + j
            hot = one_hot(rows, place_ref[pl.ds(e, 1), :])
            hot_ref[pl.ds(j * rows, rows), :] = hot.astype(BF16)
            if level_ref is not None:
                levels.append(jnp.sum(hot * level_ref[pl.ds(e, 1), :], axis=1, keepdims=True))
        got = jnp.dot(hot_ref[...], tok_ref[...], preferred_element_type=F32)
        if level_ref is not None:
            got = got * jnp.concatenate(levels, axis=0)
        out_ref[pl.ds(g * group, group)] = got.astype(BF16).reshape(group, rows, got.shape[1])
        return carry

    lax.fori_loop(0, experts // group, body, 0)


def places(zs, tok, experts, meta_ref, place_ref, level_ref, first):
    lane = lax.broadcasted_iota(jnp.int32, (TOPK, 2 * tok), 1)
    rows, ids, levels = [], [], []
    for d in range(zs):
        meta = meta_ref[d].astype(F32) + meta_ref[zs + d].astype(F32)
        kinds = [meta[0:TOPK, 2 * tok * n : 2 * tok * (n + 1)] for n in range(5)]
        block = 2 * d + (lane >= tok).astype(jnp.int32)
        rows.append(kinds[1] + block.astype(F32) * CAP)
        ids.append(kinds[0])
        levels.append(kinds[2] + kinds[3] + kinds[4])
    row, expert, level = (jnp.concatenate(v, axis=1) for v in (rows, ids, levels))
    for e in range(experts):
        hit = expert == (first + e).astype(F32)
        place_ref[e : e + 1, :] = jnp.max(jnp.where(hit, row, -1.0), axis=0, keepdims=True)
        level_ref[e : e + 1, :] = jnp.sum(jnp.where(hit, level, 0.0), axis=0, keepdims=True)


def at_rows(rows, j):
    return pl.ds(pl.multiple_of(j * rows, rows), rows)


def forward(rows, count, first, arrived, xs, bufs, out_ref):
    def body(j):
        arrived(j)
        x = xs[first + j]
        for n, buf in enumerate(bufs):
            got = jnp.dot(x, buf[j], preferred_element_type=F32)
            out_ref[j, n * rows : (n + 1) * rows, :] = got.astype(out_ref.dtype)

    each(count, body)


def x_kernel(cfg, count, s_ref, *refs):
    zs, tok, experts, rows, group = cfg
    tokens = refs[: 2 * zs]
    gate_ref, up_ref, au_ref, xin_ref, place_ref, level_ref = refs[2 * zs : 2 * zs + 6]
    tok_ref, hot_ref, meta_ref, rows_ref, gate, up, sem, tok_sem, out_sem = refs[2 * zs + 6 :]
    filling, routes = fill(tok_ref, tokens, s_ref[1], tok, tok_sem, meta_ref)
    copies = load((gate_ref, up_ref), s_ref[0], count, (gate, up), sem)
    ready(routes)
    places(zs, tok, experts, meta_ref, place_ref, level_ref, s_ref[2])
    ready(filling)
    dispatch(rows, experts, group, place_ref, tok_ref, hot_ref, rows_ref)
    leaving = pltpu.make_async_copy(rows_ref, xin_ref, out_sem)
    leaving.start()
    forward(rows, count, s_ref[0], copies, rows_ref, (gate, up), au_ref)
    leaving.wait()


def x2_kernel(rows, count, s_ref, xin_ref, gate_ref, up_ref, au_ref, xs, gate, up, sem):
    arrived = load((xin_ref, gate_ref, up_ref), s_ref[0], count, (xs, gate, up), sem)
    forward(rows, count, 0, arrived, xs, (gate, up), au_ref)


def back_dots(count, first, arrived, ys, down, out_ref):
    def body(j):
        arrived(j)
        out_ref[j] = lax.dot_general(ys[first + j], down[j], NT, preferred_element_type=F32).astype(out_ref.dtype)

    each(count, body)


def y_kernel(cfg, count, s_ref, *refs):
    zs, tok, experts, rows, group = cfg
    tokens = refs[: 2 * zs]
    place_ref, level_ref, down_ref, dh_ref, yin_ref = refs[2 * zs : 2 * zs + 5]
    tok_ref, hot_ref, rows_ref, down, sem, tok_sem, out_sem = refs[2 * zs + 5 :]
    filling, _ = fill(tok_ref, tokens, s_ref[1], tok, tok_sem)
    copies = load((down_ref,), s_ref[0], count, (down,), sem)
    ready(filling)
    dispatch(rows, experts, group, place_ref, tok_ref, hot_ref, rows_ref, level_ref)
    leaving = pltpu.make_async_copy(rows_ref, yin_ref, out_sem)
    leaving.start()
    back_dots(count, s_ref[0], copies, rows_ref, down, dh_ref)
    leaving.wait()


def y2_kernel(count, s_ref, yin_ref, down_ref, dh_ref, ys, down, sem):
    arrived = load((yin_ref, down_ref), s_ref[0], count, (ys, down), sem)
    back_dots(count, 0, arrived, ys, down, dh_ref)


def final_kernel(rows, scale, at, off, s_ref, au_m, dh_m, au_r, dh_r, d_ref, score_ref):
    def body(j):
        au = au_m[at + j] + au_r[at + j].astype(F32)
        a, u = au[0:rows], au[rows:]
        dh = dh_m[at + j] + dh_r[off + j].astype(F32)
        sig = jax.nn.sigmoid(a)
        act = a * sig
        channel = jnp.sum(act * u * dh, axis=0, keepdims=True)
        score_ref[j] = channel * channel * scale
        d_ref[j, 0:rows, :] = (dh * u * sig * (1.0 + a * (1.0 - sig))).astype(BF16)
        d_ref[j, rows:, :] = (dh * act).astype(BF16)

    each(d_ref.shape[0], body)


def gradient_rows(rows, d_ref, arrived, gate, up, part_ref, at=0):
    def body(j):
        arrived(at + j)
        part = lax.dot_general(d_ref[j, 0:rows, :], gate[at + j], NT, preferred_element_type=F32)
        part = part + lax.dot_general(d_ref[j, rows:, :], up[at + j], NT, preferred_element_type=F32)
        part_ref[at_rows(rows, at + j), :] = part.astype(BF16)

    each(d_ref.shape[0], body)


def mine_parts_kernel(rows, sizes, s_ref, *refs):
    n = len(sizes)
    gate_ref, up_ref, part_ref, gate, up, sem = refs[n:]
    arrived = load((gate_ref, up_ref), s_ref[0], sum(sizes), (gate, up), sem)
    at = 0
    for d_ref, size in zip(refs[:n], sizes):
        gradient_rows(rows, d_ref, arrived, gate, up, part_ref, at)
        at += size


def combine_kernel(rows, zs, tok, half, at, count, last, s_ref, d_ref, gate_ref, up_ref, place_ref, *refs):
    first = s_ref[0] + at
    if at == 0:
        *mine_refs, acc, gate, up, part_ref, hot_ref, sem = refs
    elif last:
        acc_in, keep_ref, send_ref, gate, up, part_ref, hot_ref, acc, sem = refs
    else:
        acc_in, acc, gate, up, part_ref, hot_ref, sem = refs
    copies = load((gate_ref, up_ref), first, count, (gate, up), sem)

    def mark(start, e, n):
        def body(j):
            hot = one_hot(rows, place_ref[pl.ds(e + j, 1), :])
            hot_ref[at_rows(rows, start + j), :] = hot.astype(BF16)

        each(n, body)

    mark(half if at == 0 else 0, first, count)
    if at == 0:
        mark(0, half - s_ref[0], half)
    cut = 0
    if at == 0:
        for n, mine_ref in enumerate(mine_refs):
            size = mine_ref.shape[0]
            own = lax.dot_general(hot_ref[cut : cut + size, :], mine_ref[...], TN, preferred_element_type=F32)
            acc[...] = own if n == 0 else acc[...] + own
            cut += size
    gradient_rows(rows, d_ref, copies, gate, up, part_ref)
    total = lax.dot_general(hot_ref[cut:, :], part_ref[...], TN, preferred_element_type=F32)
    if at == 0:
        acc[...] += total
        return
    acc[...] = total + acc_in[...]
    if not last:
        return
    side = s_ref[1]
    for d in range(zs):
        keep_ref[d] = acc[pl.ds(pl.multiple_of(2 * d * tok + side * tok, tok), tok), :]
        send_ref[d] = acc[pl.ds(pl.multiple_of(2 * d * tok + (1 - side) * tok, tok), tok), :].astype(BF16)


def stationary(tokens, out_grad, gates, expert_ids, slots, gate_weight, up_weight, down_weight):
    zs = lax.axis_size("expert")
    tok, width = tokens.shape
    experts, _, ff = gate_weight.shape
    rows = 2 * zs * CAP
    all_tok = 2 * zs * tok
    half = experts // 2
    group = 4 if experts % 4 == 0 else 1
    p, s, z = lax.axis_index("dp"), lax.axis_index("sub"), lax.axis_index("expert")
    mine0, other0 = half * p, half * (1 - p)
    first = half // 2
    rest = half - first
    sizes = [first, rest]

    def flip(v, axis):
        return lax.ppermute(v, axis, [(0, 1), (1, 0)])

    def turn(v, d):
        pairs = [
            ((i * 2 + a) * 2 + b, (((i + d) % zs) * 2 + b) * 2 + a)
            for i in range(zs)
            for a in range(2)
            for b in range(2)
        ]
        return lax.ppermute(v, ("expert", "dp", "sub"), pairs)

    def shift(v, d):
        return lax.ppermute(v, "expert", [(i, (i + d) % zs) for i in range(zs)])

    def sds(shape, dtype):
        return jax.ShapeDtypeStruct(shape, dtype)

    vmem, anywhere = pl.BlockSpec(memory_space=pltpu.VMEM), pl.BlockSpec(memory_space=pltpu.HBM)
    smem = pl.BlockSpec(memory_space=pltpu.SMEM)
    dma = pltpu.SemaphoreType.DMA

    def call(body, first, second, args, outs, scratch, flops, moved, name, factor=1):
        ins = [spec for spec, group in args for _ in group]
        arrays = [v for _, group in args for v in group]
        info = jnp.stack([jnp.int32(first), jnp.int32(second), jnp.int32(z * experts)])
        return pl.pallas_call(
            body,
            out_shape=outs,
            in_specs=[smem] + ins,
            out_specs=jax.tree.map(lambda v: anywhere if v is rows_shape else vmem, outs),
            scratch_shapes=scratch,
            compiler_params=pltpu.CompilerParams(vmem_limit_bytes=VMEM_LIMIT),
            cost_estimate=pl.CostEstimate(flops=int(flops * COST * factor), bytes_accessed=int(moved * COST * factor), transcendentals=0),
            name=name,
        )(info, *arrays)

    loaded = pl.pallas_call(
        pack_kernel,
        out_shape=sds((tok + ROUTE_ROWS, width), BF16),
        in_specs=[smem] + [vmem] * 4,
        out_specs=vmem,
        name="pack",
    )(jnp.stack([p]).astype(jnp.int32), tokens, expert_ids.T, slots.T, gates.T)
    x_own = [turn(loaded, d) for d in range(zs)]
    out_grad, _ = lax.optimization_barrier((out_grad, loaded))
    y_here = turn(out_grad, 0)
    *x_own, y_here = lax.optimization_barrier((*x_own, y_here))
    x_other = [flip(v, "sub") for v in x_own]
    wbytes = width * ff * 2
    flop = 2 * rows * width * ff
    dflop = 2 * experts * rows * all_tok * width
    cfg = (zs, tok, experts, rows, group)
    hot = pltpu.VMEM((group * rows, all_tok), BF16)
    tok_scratch = pltpu.VMEM((all_tok, width), BF16)

    def wide(count):
        return pltpu.VMEM((count, width, ff), BF16)

    def tall(count):
        return pltpu.VMEM((count, ff, width), BF16)

    place_shape = sds((experts, all_tok), F32)
    rows_shape = pltpu.HBM((experts, rows, width), BF16)
    rows_scratch = pltpu.VMEM((experts, rows, width), BF16)
    def pinned(*arrays):
        return tuple(pltpu.with_memory_space_constraint(v, pltpu.HBM) for v in arrays)

    weights = (anywhere, pinned(gate_weight, up_weight))
    down_weight, = pinned(down_weight)
    au_send, xin, place, level = call(
        functools.partial(x_kernel, cfg, half),
        other0,
        s,
        [(anywhere, pinned(*x_own, *x_other)), weights],
        [sds((half, 2 * rows, ff), BF16), rows_shape, place_shape, place_shape],
        [tok_scratch, hot, pltpu.VMEM((2 * zs, ROUTE_ROWS, width), BF16), rows_scratch, wide(half), wide(half)]
        + [dma((2 * half,)), dma((4 * zs,)), dma],
        2 * half * flop + dflop,
        2 * half * wbytes,
        "x_first",
    )
    y_here, au_send = lax.optimization_barrier((y_here, au_send))
    y_own = [y_here] + [shift(y_here, d) for d in range(1, zs)]

    def x_call(first, n, dtype, name, factor):
        return call(
            functools.partial(x2_kernel, rows, n),
            first,
            s,
            [(anywhere, pinned(xin)), weights],
            sds((n, 2 * rows, ff), dtype),
            [pltpu.VMEM((n, rows, width), BF16), wide(n), wide(n), dma((3 * n,))],
            2 * n * flop,
            2 * n * wbytes,
            name,
            factor,
        )

    au_mine = x_call(mine0, half, F32, "x_mine", MINE_COST)
    au_recv = flip(au_send, "dp")
    *y_own, au_mine = lax.optimization_barrier((*y_own, au_mine))
    y_other = [flip(v, "sub") for v in y_own]
    dh_first, yin = call(
        functools.partial(y_kernel, cfg, first),
        other0,
        s,
        [(anywhere, pinned(*y_own, *y_other)), (vmem, (place, level)), (anywhere, (down_weight,))],
        [sds((first, rows, ff), BF16), rows_shape],
        [tok_scratch, hot, rows_scratch, tall(first), dma((first,)), dma((2 * zs,)), dma],
        first * flop + dflop,
        first * wbytes,
        "y_first",
    )

    def y_call(first, n, dtype, name):
        return call(
            functools.partial(y2_kernel, n),
            first,
            s,
            [(anywhere, pinned(yin, down_weight))],
            sds((n, rows, ff), dtype),
            [pltpu.VMEM((n, rows, width), BF16), tall(n), dma((2 * n,))],
            n * flop,
            n * wbytes,
            name,
        )

    yin, au_recv = lax.optimization_barrier((yin, au_recv))
    dh_rest = y_call(other0 + first, rest, BF16, "y_other")
    yin, dh_rest = lax.optimization_barrier((yin, dh_rest))
    dh_mine = y_call(mine0, half, F32, "y_mine")
    dh_recv = [flip(v, "dp") for v in (dh_first, dh_rest)]
    scale = LOCAL_EXPERTS / (all_tok * TOPK)
    last = 0
    chunks = [(0, 0, first)] + [(1, at, n) for at, n in ((0, rest - last), (rest - last, last)) if n]
    back, scores = [], []

    def final_call(k, at, n):
        d, score = call(
            functools.partial(final_kernel, rows, scale, k * first + at, at),
            mine0,
            s,
            [(vmem, (au_mine, dh_mine, au_recv, dh_recv[k]))],
            [sds((n, 2 * rows, ff), BF16), sds((n, 1, ff), F32)],
            [],
            n * rows * ff * 40,
            n * rows * ff * 30,
            "final",
        )
        scores.append(score)
        if k == 0:
            sent, dh_recv[1] = lax.optimization_barrier((d, dh_recv[1]))
        else:
            sent = d
        back.append(flip(sent, "dp"))
        return d

    def parts_call(start, ds):
        counts = [d.shape[0] for d in ds]
        n = sum(counts)
        return call(
            functools.partial(mine_parts_kernel, rows, counts),
            mine0 + start,
            s,
            [(vmem, ds), weights],
            sds((n * rows, width), BF16),
            [wide(n), wide(n), dma((2 * n,))],
            2 * n * flop,
            2 * n * wbytes,
            "mine_parts",
            PART_COST,
        )

    given = [parts_call(0, [final_call(*chunks[0])])]
    dh_mine, given[0] = lax.optimization_barrier((dh_mine, given[0]))
    ds = []
    for chunk in chunks[1:]:
        ds.append(final_call(*chunk))
        dh_mine, ds[-1] = lax.optimization_barrier((dh_mine, ds[-1]))
    given.append(parts_call(first, ds))
    score = jnp.concatenate(scores, axis=0).reshape(half, ff)
    score_other = flip(score, "dp")
    acc_shape, zshape = (all_tok, width), (zs, tok, width)
    for k, (part, at, n) in enumerate(chunks):
        used, final = n + half * (k == 0), k == len(chunks) - 1
        given = call(
            functools.partial(combine_kernel, rows, zs, tok, half, part * first + at, n, final),
            other0,
            s,
            [(vmem, (back[k],)), weights, (vmem, (place, *given))],
            [sds(zshape, F32), sds(zshape, BF16)] if final else [sds(acc_shape, F32)],
            [wide(n), wide(n), pltpu.VMEM((n * rows, width), BF16), pltpu.VMEM((used * rows, all_tok), BF16)]
            + ([pltpu.VMEM(acc_shape, F32)] if final else [])
            + [dma((2 * n,))],
            2 * n * flop + 2 * used * rows * width * all_tok,
            2 * n * wbytes,
            "combine",
        )
        if k == len(chunks) - 2:
            *given, score_other = lax.optimization_barrier((*given, score_other))
            scores = jnp.concatenate(
                [jnp.where(p == 0, score, score_other), jnp.where(p == 0, score_other, score)], axis=0
            )
    keep, send = given
    summed = (keep + flip(send, "sub").astype(F32)).astype(BF16)
    total = turn(summed[0], 0).astype(F32)
    for d in range(1, zs):
        total = total + turn(summed[d], -d).astype(F32)
    return (scores, total.astype(BF16))


def solution(mesh):
    in_specs = (
        P(("dom", "expert", "dp"), "sub"),
        P(("dom", "expert", "dp"), "sub"),
        P(("dom", "expert", "dp"), None),
        P(("dom", "expert", "dp"), None),
        P(("dom", "expert", "dp"), None),
        P("expert", "dp", "sub"),
        P("expert", "dp", "sub"),
        P("expert", "sub", "dp"),
    )
    out_specs = (P(("dom", "expert"), "sub"), P(("dom", "expert", "dp"), "sub"))
    pairs = mesh.shape["dp"] == 2 and mesh.shape["sub"] == 2
    split = (LOCAL_EXPERTS // mesh.shape["expert"]) % 2 == 0
    local = stationary if pairs and split else gathered
    return jax.shard_map(local, mesh=mesh, in_specs=in_specs, out_specs=out_specs, check_vma=False)
```

```python
import functools

import jax
import jax.numpy as jnp
from jax import lax
from jax.experimental import pallas as pl
from jax.experimental.pallas import tpu as pltpu
from jax.sharding import PartitionSpec as P

LOCAL_EXPERTS = 64
TOPK = 8
CAP = 10
F32 = jnp.float32
BF16 = jnp.bfloat16
NT = (((1,), (1,)), ((), ()))
TN = (((0,), (0,)), ((), ()))
VMEM_LIMIT = 32 * 1024 * 1024


def gathered(tokens, out_grad, gates, expert_ids, slots, gate_weight, up_weight, down_weight):
    expert_count = lax.axis_size("expert")
    group_count = lax.axis_size("dp")
    local_count = gate_weight.shape[0]
    tok_rows = tokens.shape[0]
    half_width = tokens.shape[1]
    slot_count = local_count * expert_count * CAP
    target_dev = expert_ids // local_count
    local_expert = expert_ids % local_count
    slot_rows = ((local_expert * expert_count + target_dev) * CAP + slots).reshape(-1)
    scaled = (gates[:, :, None] * out_grad[:, None, :].astype(F32)).astype(BF16)
    scaled = scaled.reshape(tok_rows * TOPK, half_width)
    repeated = jnp.repeat(tokens, TOPK, axis=0)

    def route(rows):
        send = jnp.zeros((slot_count, half_width), BF16).at[slot_rows].add(rows)
        send = send.reshape(local_count, expert_count, CAP, half_width)
        recv = lax.all_to_all(send, "expert", split_axis=1, concat_axis=1, tiled=True)
        full = lax.all_gather(recv, "sub", axis=3, tiled=True)
        return full.reshape(local_count, expert_count * CAP, full.shape[3])

    x_full, grad_full = route(repeated), route(scaled)
    gate_full = lax.all_gather(gate_weight, "dp", axis=1, tiled=True)
    up_full = lax.all_gather(up_weight, "dp", axis=1, tiled=True)
    down_full = lax.all_gather(down_weight, "dp", axis=2, tiled=True)
    gate_pre = jnp.einsum("erd,edf->erf", x_full, gate_full, preferred_element_type=F32)
    up_pre = jnp.einsum("erd,edf->erf", x_full, up_full, preferred_element_type=F32)
    hidden_grad = jnp.einsum("erd,efd->erf", grad_full, down_full, preferred_element_type=F32)
    gating = jax.nn.sigmoid(gate_pre)
    activated = gate_pre * gating
    channel = lax.psum(jnp.sum(activated * up_pre * hidden_grad, axis=1), "dp")
    scale = LOCAL_EXPERTS / (tok_rows * expert_count * group_count * TOPK)
    scores = channel * channel * scale
    gate_grad = (hidden_grad * up_pre * gating * (1.0 + gate_pre * (1.0 - gating))).astype(BF16)
    up_grad = (hidden_grad * activated).astype(BF16)
    parts = jnp.einsum("erf,edf->erd", gate_grad, gate_full, preferred_element_type=F32)
    parts = parts + jnp.einsum("erf,edf->erd", up_grad, up_full, preferred_element_type=F32)
    summed = lax.psum_scatter(parts.astype(BF16), "sub", scatter_dimension=2, tiled=True)
    summed = summed.reshape(local_count, expert_count, CAP, half_width)
    returned = lax.all_to_all(summed, "expert", split_axis=1, concat_axis=1, tiled=True)
    picked = returned.reshape(slot_count, half_width)[slot_rows].astype(F32)
    token_grad = jnp.sum(picked.reshape(tok_rows, TOPK, half_width), axis=1)
    return (scores, token_grad.astype(BF16))


PART_COST = 1
COST = 1.0


ROUTE_ROWS = 16


def each(count, body):
    def step(j, carry):
        body(j)
        return carry

    lax.fori_loop(0, count, step, 0)


def load(sources, first, count, buffers, sem):
    def copies(j):
        return [
            pltpu.make_async_copy(source.at[first + j], buffer.at[j], sem.at[j * len(sources) + n])
            for n, (source, buffer) in enumerate(zip(sources, buffers))
        ]

    def start(j):
        for copy in copies(j):
            copy.start()

    each(count, start)
    return lambda j: ready(copies(j))


def ready(line):
    for copy in line:
        copy.wait()


def one_hot(rows, place):
    index = lax.broadcasted_iota(jnp.int32, (rows, place.shape[1]), 0).astype(F32)
    return jnp.where(index == place, 1.0, 0.0)


def pack_kernel(p_ref, tokens_ref, ids_ref, slots_ref, gates_ref, out_ref):
    tok = tokens_ref.shape[0]
    out_ref[0:tok, :] = tokens_ref[...]
    out_ref[tok:, :] = jnp.zeros((ROUTE_ROWS, out_ref.shape[1]), BF16)
    lane = lax.broadcasted_iota(jnp.int32, (tok, 2 * tok), 1)
    row = lax.broadcasted_iota(jnp.int32, (tok, 2 * tok), 0) + p_ref[0] * tok
    place = jnp.where(lane == row, 1.0, 0.0).astype(BF16)
    left = gates_ref[...]
    kinds = [ids_ref[...].astype(F32), slots_ref[...].astype(F32)]
    for _ in range(3):
        kinds.append(left.astype(BF16).astype(F32))
        left = left - kinds[-1]
    kinds = jnp.concatenate(kinds, axis=0).astype(BF16)
    moved = jnp.dot(kinds, place, preferred_element_type=F32)
    none = jnp.zeros((ROUTE_ROWS - TOPK, 2 * tok), F32)
    for n in range(5):
        block = jnp.concatenate([moved[n * TOPK : (n + 1) * TOPK], none], axis=0)
        out_ref[tok:, 2 * tok * n : 2 * tok * (n + 1)] = block.astype(BF16)


def fill(tok_ref, token_refs, side, tok, sem, meta_ref=None):
    copies = []
    zs = len(token_refs) // 2
    for n, ref in enumerate(token_refs):
        d, part = n % zs, side if n < zs else 1 - side
        start = pl.multiple_of(2 * d * tok + part * tok, tok)
        copies.append(pltpu.make_async_copy(ref.at[pl.ds(0, tok)], tok_ref.at[pl.ds(start, tok)], sem.at[n]))
        copies[-1].start()
    routes = []
    if meta_ref is not None:
        for n, ref in enumerate(token_refs):
            source = ref.at[pl.ds(tok, ROUTE_ROWS)]
            routes.append(pltpu.make_async_copy(source, meta_ref.at[n], sem.at[2 * zs + n]))
            routes[-1].start()
    return copies, routes


def dispatch(rows, first, count, group, place_ref, tok_ref, hot_ref, out_ref, level_ref=None):
    def body(g, carry):
        levels = []
        for j in range(group):
            e = first + g * group + j
            hot = one_hot(rows, place_ref[pl.ds(e, 1), :])
            hot_ref[pl.ds(j * rows, rows), :] = hot.astype(BF16)
            if level_ref is not None:
                levels.append(jnp.sum(hot * level_ref[pl.ds(e, 1), :], axis=1, keepdims=True))
        got = jnp.dot(hot_ref[...], tok_ref[...], preferred_element_type=F32)
        if level_ref is not None:
            got = got * jnp.concatenate(levels, axis=0)
        out_ref[pl.ds(g * group, group)] = got.astype(BF16).reshape(group, rows, got.shape[1])
        return carry

    lax.fori_loop(0, count // group, body, 0)


def places(zs, tok, experts, meta_ref, place_ref, level_ref, first):
    lane = lax.broadcasted_iota(jnp.int32, (TOPK, 2 * tok), 1)
    rows, ids, levels = [], [], []
    for d in range(zs):
        meta = meta_ref[d].astype(F32) + meta_ref[zs + d].astype(F32)
        kinds = [meta[0:TOPK, 2 * tok * n : 2 * tok * (n + 1)] for n in range(5)]
        block = 2 * d + (lane >= tok).astype(jnp.int32)
        rows.append(kinds[1] + block.astype(F32) * CAP)
        ids.append(kinds[0])
        levels.append(kinds[2] + kinds[3] + kinds[4])
    row, expert, level = (jnp.concatenate(v, axis=1) for v in (rows, ids, levels))
    for e in range(experts):
        hit = expert == (first + e).astype(F32)
        place_ref[e : e + 1, :] = jnp.max(jnp.where(hit, row, -1.0), axis=0, keepdims=True)
        level_ref[e : e + 1, :] = jnp.sum(jnp.where(hit, level, 0.0), axis=0, keepdims=True)


def at_rows(rows, j):
    return pl.ds(pl.multiple_of(j * rows, rows), rows)


def forward(rows, count, first, arrived, xs, bufs, out_ref):
    def body(j):
        arrived(j)
        x = xs[first + j]
        for n, buf in enumerate(bufs):
            got = jnp.dot(x, buf[j], preferred_element_type=F32)
            out_ref[j, n * rows : (n + 1) * rows, :] = got.astype(out_ref.dtype)

    each(count, body)


def x_kernel(cfg, count, s_ref, *refs):
    zs, tok, experts, rows, group = cfg
    tokens = refs[: 2 * zs]
    gate_ref, up_ref, au_ref, place_ref, level_ref = refs[2 * zs : 2 * zs + 5]
    tok_ref, hot_ref, meta_ref, rows_ref, gate, up, sem, tok_sem = refs[2 * zs + 5 :]
    filling, routes = fill(tok_ref, tokens, s_ref[1], tok, tok_sem, meta_ref)
    copies = load((gate_ref, up_ref), s_ref[0], count, (gate, up), sem)
    ready(routes)
    places(zs, tok, experts, meta_ref, place_ref, level_ref, s_ref[2])
    ready(filling)
    dispatch(rows, s_ref[0], count, group, place_ref, tok_ref, hot_ref, rows_ref)
    forward(rows, count, 0, copies, rows_ref, (gate, up), au_ref)


def x2_kernel(cfg, count, s_ref, *refs):
    zs, tok, experts, rows, group = cfg
    place_ref, gate_ref, up_ref, au_ref, tok_ref, hot_ref, rows_ref, gate, up, sem, tok_sem = refs[2 * zs :]
    filling, _ = fill(tok_ref, refs[: 2 * zs], s_ref[1], tok, tok_sem)
    copies = load((gate_ref, up_ref), s_ref[0], count, (gate, up), sem)
    ready(filling)
    dispatch(rows, s_ref[0], count, group, place_ref, tok_ref, hot_ref, rows_ref)
    forward(rows, count, 0, copies, rows_ref, (gate, up), au_ref)


def back_dots(count, first, arrived, ys, down, out_ref):
    def body(j):
        arrived(j)
        out_ref[j] = lax.dot_general(ys[first + j], down[j], NT, preferred_element_type=F32).astype(out_ref.dtype)

    each(count, body)


def y_kernel(cfg, count, s_ref, *refs):
    zs, tok, experts, rows, group = cfg
    tokens = refs[: 2 * zs]
    place_ref, level_ref, down_ref, dh_ref, yin_ref = refs[2 * zs : 2 * zs + 5]
    tok_ref, hot_ref, rows_ref, down, sem, tok_sem, out_sem = refs[2 * zs + 5 :]
    filling, _ = fill(tok_ref, tokens, s_ref[1], tok, tok_sem)
    copies = load((down_ref,), s_ref[0], count, (down,), sem)
    ready(filling)
    dispatch(rows, 0, experts, group, place_ref, tok_ref, hot_ref, rows_ref, level_ref)
    leaving = pltpu.make_async_copy(rows_ref, yin_ref, out_sem)
    leaving.start()
    back_dots(count, s_ref[0], copies, rows_ref, down, dh_ref)
    leaving.wait()


def y2_kernel(count, s_ref, yin_ref, down_ref, dh_ref, ys, down, sem):
    arrived = load((yin_ref, down_ref), s_ref[0], count, (ys, down), sem)
    back_dots(count, 0, arrived, ys, down, dh_ref)


def final_kernel(rows, scale, at, off, s_ref, au_m, dh_m, au_r, dh_r, d_ref, score_ref):
    def body(j):
        au = au_m[at + j] + au_r[at + j].astype(F32)
        a, u = au[0:rows], au[rows:]
        dh = dh_m[at + j] + dh_r[off + j].astype(F32)
        sig = jax.nn.sigmoid(a)
        act = a * sig
        channel = jnp.sum(act * u * dh, axis=0, keepdims=True)
        score_ref[j] = channel * channel * scale
        d_ref[j, 0:rows, :] = (dh * u * sig * (1.0 + a * (1.0 - sig))).astype(BF16)
        d_ref[j, rows:, :] = (dh * act).astype(BF16)

    each(d_ref.shape[0], body)


def gradient_rows(rows, d_ref, arrived, gate, up, part_ref, at=0):
    def body(j):
        arrived(at + j)
        part = lax.dot_general(d_ref[j, 0:rows, :], gate[at + j], NT, preferred_element_type=F32)
        part = part + lax.dot_general(d_ref[j, rows:, :], up[at + j], NT, preferred_element_type=F32)
        part_ref[at_rows(rows, at + j), :] = part.astype(BF16)

    each(d_ref.shape[0], body)


def mine_parts_kernel(rows, sizes, s_ref, *refs):
    n = len(sizes)
    gate_ref, up_ref, part_ref, gate, up, sem = refs[n:]
    arrived = load((gate_ref, up_ref), s_ref[0], sum(sizes), (gate, up), sem)
    at = 0
    for d_ref, size in zip(refs[:n], sizes):
        gradient_rows(rows, d_ref, arrived, gate, up, part_ref, at)
        at += size


def combine_kernel(rows, zs, tok, half, at, count, last, s_ref, d_ref, gate_ref, up_ref, place_ref, *refs):
    first = s_ref[0] + at
    if at == 0:
        *mine_refs, acc, gate, up, part_ref, hot_ref, sem = refs
    elif last:
        acc_in, keep_ref, send_ref, gate, up, part_ref, hot_ref, acc, sem = refs
    else:
        acc_in, acc, gate, up, part_ref, hot_ref, sem = refs
    copies = load((gate_ref, up_ref), first, count, (gate, up), sem)

    def mark(start, e, n):
        def body(j):
            hot = one_hot(rows, place_ref[pl.ds(e + j, 1), :])
            hot_ref[at_rows(rows, start + j), :] = hot.astype(BF16)

        each(n, body)

    mark(half if at == 0 else 0, first, count)
    if at == 0:
        mark(0, half - s_ref[0], half)
    cut = 0
    if at == 0:
        for n, mine_ref in enumerate(mine_refs):
            size = mine_ref.shape[0]
            own = lax.dot_general(hot_ref[cut : cut + size, :], mine_ref[...], TN, preferred_element_type=F32)
            acc[...] = own if n == 0 else acc[...] + own
            cut += size
    gradient_rows(rows, d_ref, copies, gate, up, part_ref)
    total = lax.dot_general(hot_ref[cut:, :], part_ref[...], TN, preferred_element_type=F32)
    if at == 0:
        acc[...] += total
        return
    acc[...] = total + acc_in[...]
    if not last:
        return
    side = s_ref[1]
    for d in range(zs):
        keep_ref[d] = acc[pl.ds(pl.multiple_of(2 * d * tok + side * tok, tok), tok), :]
        send_ref[d] = acc[pl.ds(pl.multiple_of(2 * d * tok + (1 - side) * tok, tok), tok), :].astype(BF16)


def stationary(tokens, out_grad, gates, expert_ids, slots, gate_weight, up_weight, down_weight):
    zs = lax.axis_size("expert")
    tok, width = tokens.shape
    experts, _, ff = gate_weight.shape
    rows = 2 * zs * CAP
    all_tok = 2 * zs * tok
    half = experts // 2
    group = 4 if half % 4 == 0 else 1
    p, s, z = lax.axis_index("dp"), lax.axis_index("sub"), lax.axis_index("expert")
    mine0, other0 = half * p, half * (1 - p)
    first = half // 2
    rest = half - first
    sizes = [first, rest]

    def flip(v, axis):
        return lax.ppermute(v, axis, [(0, 1), (1, 0)])

    def turn(v, d):
        pairs = [
            ((i * 2 + a) * 2 + b, (((i + d) % zs) * 2 + b) * 2 + a)
            for i in range(zs)
            for a in range(2)
            for b in range(2)
        ]
        return lax.ppermute(v, ("expert", "dp", "sub"), pairs)

    def shift(v, d):
        return lax.ppermute(v, "expert", [(i, (i + d) % zs) for i in range(zs)])

    def sds(shape, dtype):
        return jax.ShapeDtypeStruct(shape, dtype)

    vmem, anywhere = pl.BlockSpec(memory_space=pltpu.VMEM), pl.BlockSpec(memory_space=pltpu.HBM)
    smem = pl.BlockSpec(memory_space=pltpu.SMEM)
    dma = pltpu.SemaphoreType.DMA

    def call(body, first, second, args, outs, scratch, flops, moved, name, factor=1):
        ins = [spec for spec, group in args for _ in group]
        arrays = [v for _, group in args for v in group]
        info = jnp.stack([jnp.int32(first), jnp.int32(second), jnp.int32(z * experts)])
        return pl.pallas_call(
            body,
            out_shape=outs,
            in_specs=[smem] + ins,
            out_specs=jax.tree.map(lambda v: anywhere if v is rows_shape else vmem, outs),
            scratch_shapes=scratch,
            compiler_params=pltpu.CompilerParams(vmem_limit_bytes=VMEM_LIMIT),
            cost_estimate=pl.CostEstimate(flops=int(flops * COST * factor), bytes_accessed=int(moved * COST * factor), transcendentals=0),
            name=name,
        )(info, *arrays)

    loaded = pl.pallas_call(
        pack_kernel,
        out_shape=sds((tok + ROUTE_ROWS, width), BF16),
        in_specs=[smem] + [vmem] * 4,
        out_specs=vmem,
        name="pack",
    )(jnp.stack([p]).astype(jnp.int32), tokens, expert_ids.T, slots.T, gates.T)
    x_own = [turn(loaded, d) for d in range(zs)]
    out_grad, _ = lax.optimization_barrier((out_grad, loaded))
    y_here = turn(out_grad, 0)
    *x_own, y_here = lax.optimization_barrier((*x_own, y_here))
    x_other = [flip(v, "sub") for v in x_own]
    wbytes = width * ff * 2
    flop = 2 * rows * width * ff
    dflop = 2 * experts * rows * all_tok * width
    cfg = (zs, tok, experts, rows, group)
    hot = pltpu.VMEM((group * rows, all_tok), BF16)
    tok_scratch = pltpu.VMEM((all_tok, width), BF16)

    def wide(count):
        return pltpu.VMEM((count, width, ff), BF16)

    def tall(count):
        return pltpu.VMEM((count, ff, width), BF16)

    place_shape = sds((experts, all_tok), F32)
    rows_shape = pltpu.HBM((experts, rows, width), BF16)
    half_rows = pltpu.VMEM((half, rows, width), BF16)
    rows_scratch = pltpu.VMEM((experts, rows, width), BF16)
    def pinned(*arrays):
        return tuple(pltpu.with_memory_space_constraint(v, pltpu.HBM) for v in arrays)

    weights = (anywhere, pinned(gate_weight, up_weight))
    down_weight, = pinned(down_weight)
    au_send, place, level = call(
        functools.partial(x_kernel, cfg, half),
        other0,
        s,
        [(anywhere, pinned(*x_own, *x_other)), weights],
        [sds((half, 2 * rows, ff), BF16), place_shape, place_shape],
        [tok_scratch, hot, pltpu.VMEM((2 * zs, ROUTE_ROWS, width), BF16), half_rows, wide(half), wide(half)]
        + [dma((2 * half,)), dma((4 * zs,))],
        2 * half * flop + dflop // 2,
        2 * half * wbytes,
        "x_first",
    )
    y_here, au_send = lax.optimization_barrier((y_here, au_send))
    y_own = [y_here] + [shift(y_here, d) for d in range(1, zs)]

    au_mine = call(
        functools.partial(x2_kernel, cfg, half),
        mine0,
        s,
        [(anywhere, pinned(*x_own, *x_other)), (vmem, (place,)), weights],
        sds((half, 2 * rows, ff), F32),
        [tok_scratch, hot, half_rows, wide(half), wide(half), dma((2 * half,)), dma((2 * zs,))],
        2 * half * flop + dflop // 2,
        2 * half * wbytes,
        "x_mine",
    )
    au_recv = flip(au_send, "dp")
    *y_own, au_mine = lax.optimization_barrier((*y_own, au_mine))
    y_other = [flip(v, "sub") for v in y_own]
    dh_first, yin = call(
        functools.partial(y_kernel, cfg, first),
        other0,
        s,
        [(anywhere, pinned(*y_own, *y_other)), (vmem, (place, level)), (anywhere, (down_weight,))],
        [sds((first, rows, ff), BF16), rows_shape],
        [tok_scratch, hot, rows_scratch, tall(first), dma((first,)), dma((2 * zs,)), dma],
        first * flop + dflop,
        first * wbytes,
        "y_first",
    )

    def y_call(first, n, dtype, name):
        return call(
            functools.partial(y2_kernel, n),
            first,
            s,
            [(anywhere, pinned(yin, down_weight))],
            sds((n, rows, ff), dtype),
            [pltpu.VMEM((n, rows, width), BF16), tall(n), dma((2 * n,))],
            n * flop,
            n * wbytes,
            name,
        )

    yin, au_recv = lax.optimization_barrier((yin, au_recv))
    dh_rest = y_call(other0 + first, rest, BF16, "y_other")
    yin, dh_rest = lax.optimization_barrier((yin, dh_rest))
    dh_mine = y_call(mine0, half, F32, "y_mine")
    dh_recv = [flip(v, "dp") for v in (dh_first, dh_rest)]
    scale = LOCAL_EXPERTS / (all_tok * TOPK)
    last = 0
    chunks = [(0, 0, first)] + [(1, at, n) for at, n in ((0, rest - last), (rest - last, last)) if n]
    back, scores = [], []

    def final_call(k, at, n):
        d, score = call(
            functools.partial(final_kernel, rows, scale, k * first + at, at),
            mine0,
            s,
            [(vmem, (au_mine, dh_mine, au_recv, dh_recv[k]))],
            [sds((n, 2 * rows, ff), BF16), sds((n, 1, ff), F32)],
            [],
            n * rows * ff * 40,
            n * rows * ff * 30,
            "final",
        )
        scores.append(score)
        if k == 0:
            sent, dh_recv[1] = lax.optimization_barrier((d, dh_recv[1]))
        else:
            sent = d
        back.append(flip(sent, "dp"))
        return d

    def parts_call(start, ds):
        counts = [d.shape[0] for d in ds]
        n = sum(counts)
        return call(
            functools.partial(mine_parts_kernel, rows, counts),
            mine0 + start,
            s,
            [(vmem, ds), weights],
            sds((n * rows, width), BF16),
            [wide(n), wide(n), dma((2 * n,))],
            2 * n * flop,
            2 * n * wbytes,
            "mine_parts",
            PART_COST,
        )

    given = [parts_call(0, [final_call(*chunks[0])])]
    dh_mine, given[0] = lax.optimization_barrier((dh_mine, given[0]))
    ds = []
    for chunk in chunks[1:]:
        ds.append(final_call(*chunk))
        dh_mine, ds[-1] = lax.optimization_barrier((dh_mine, ds[-1]))
    given.append(parts_call(first, ds))
    score = jnp.concatenate(scores, axis=0).reshape(half, ff)
    score_other = flip(score, "dp")
    acc_shape, zshape = (all_tok, width), (zs, tok, width)
    for k, (part, at, n) in enumerate(chunks):
        used, final = n + half * (k == 0), k == len(chunks) - 1
        given = call(
            functools.partial(combine_kernel, rows, zs, tok, half, part * first + at, n, final),
            other0,
            s,
            [(vmem, (back[k],)), weights, (vmem, (place, *given))],
            [sds(zshape, F32), sds(zshape, BF16)] if final else [sds(acc_shape, F32)],
            [wide(n), wide(n), pltpu.VMEM((n * rows, width), BF16), pltpu.VMEM((used * rows, all_tok), BF16)]
            + ([pltpu.VMEM(acc_shape, F32)] if final else [])
            + [dma((2 * n,))],
            2 * n * flop + 2 * used * rows * width * all_tok,
            2 * n * wbytes,
            "combine",
        )
        if k == len(chunks) - 2:
            *given, score_other = lax.optimization_barrier((*given, score_other))
            scores = jnp.concatenate(
                [jnp.where(p == 0, score, score_other), jnp.where(p == 0, score_other, score)], axis=0
            )
    keep, send = given
    summed = (keep + flip(send, "sub").astype(F32)).astype(BF16)
    total = turn(summed[0], 0).astype(F32)
    for d in range(1, zs):
        total = total + turn(summed[d], -d).astype(F32)
    return (scores, total.astype(BF16))


def solution(mesh):
    in_specs = (
        P(("dom", "expert", "dp"), "sub"),
        P(("dom", "expert", "dp"), "sub"),
        P(("dom", "expert", "dp"), None),
        P(("dom", "expert", "dp"), None),
        P(("dom", "expert", "dp"), None),
        P("expert", "dp", "sub"),
        P("expert", "dp", "sub"),
        P("expert", "sub", "dp"),
    )
    out_specs = (P(("dom", "expert"), "sub"), P(("dom", "expert", "dp"), "sub"))
    pairs = mesh.shape["dp"] == 2 and mesh.shape["sub"] == 2
    split = (LOCAL_EXPERTS // mesh.shape["expert"]) % 2 == 0
    local = stationary if pairs and split else gathered
    return jax.shard_map(local, mesh=mesh, in_specs=in_specs, out_specs=out_specs, check_vma=False)
```

```python
import functools

import jax
import jax.numpy as jnp
from jax import lax
from jax.experimental import pallas as pl
from jax.experimental.pallas import tpu as pltpu
from jax.sharding import PartitionSpec as P

LOCAL_EXPERTS = 64
TOPK = 8
CAP = 10
F32 = jnp.float32
BF16 = jnp.bfloat16
NT = (((1,), (1,)), ((), ()))
TN = (((0,), (0,)), ((), ()))
VMEM_LIMIT = 32 * 1024 * 1024


def gathered(tokens, out_grad, gates, expert_ids, slots, gate_weight, up_weight, down_weight):
    expert_count = lax.axis_size("expert")
    group_count = lax.axis_size("dp")
    local_count = gate_weight.shape[0]
    tok_rows = tokens.shape[0]
    half_width = tokens.shape[1]
    slot_count = local_count * expert_count * CAP
    target_dev = expert_ids // local_count
    local_expert = expert_ids % local_count
    slot_rows = ((local_expert * expert_count + target_dev) * CAP + slots).reshape(-1)
    scaled = (gates[:, :, None] * out_grad[:, None, :].astype(F32)).astype(BF16)
    scaled = scaled.reshape(tok_rows * TOPK, half_width)
    repeated = jnp.repeat(tokens, TOPK, axis=0)

    def route(rows):
        send = jnp.zeros((slot_count, half_width), BF16).at[slot_rows].add(rows)
        send = send.reshape(local_count, expert_count, CAP, half_width)
        recv = lax.all_to_all(send, "expert", split_axis=1, concat_axis=1, tiled=True)
        full = lax.all_gather(recv, "sub", axis=3, tiled=True)
        return full.reshape(local_count, expert_count * CAP, full.shape[3])

    x_full, grad_full = route(repeated), route(scaled)
    gate_full = lax.all_gather(gate_weight, "dp", axis=1, tiled=True)
    up_full = lax.all_gather(up_weight, "dp", axis=1, tiled=True)
    down_full = lax.all_gather(down_weight, "dp", axis=2, tiled=True)
    gate_pre = jnp.einsum("erd,edf->erf", x_full, gate_full, preferred_element_type=F32)
    up_pre = jnp.einsum("erd,edf->erf", x_full, up_full, preferred_element_type=F32)
    hidden_grad = jnp.einsum("erd,efd->erf", grad_full, down_full, preferred_element_type=F32)
    gating = jax.nn.sigmoid(gate_pre)
    activated = gate_pre * gating
    channel = lax.psum(jnp.sum(activated * up_pre * hidden_grad, axis=1), "dp")
    scale = LOCAL_EXPERTS / (tok_rows * expert_count * group_count * TOPK)
    scores = channel * channel * scale
    gate_grad = (hidden_grad * up_pre * gating * (1.0 + gate_pre * (1.0 - gating))).astype(BF16)
    up_grad = (hidden_grad * activated).astype(BF16)
    parts = jnp.einsum("erf,edf->erd", gate_grad, gate_full, preferred_element_type=F32)
    parts = parts + jnp.einsum("erf,edf->erd", up_grad, up_full, preferred_element_type=F32)
    summed = lax.psum_scatter(parts.astype(BF16), "sub", scatter_dimension=2, tiled=True)
    summed = summed.reshape(local_count, expert_count, CAP, half_width)
    returned = lax.all_to_all(summed, "expert", split_axis=1, concat_axis=1, tiled=True)
    picked = returned.reshape(slot_count, half_width)[slot_rows].astype(F32)
    token_grad = jnp.sum(picked.reshape(tok_rows, TOPK, half_width), axis=1)
    return (scores, token_grad.astype(BF16))


PART_COST = 1
COST = 1.0


ROUTE_ROWS = 16


def each(count, body):
    def step(j, carry):
        body(j)
        return carry

    lax.fori_loop(0, count, step, 0)


def load(sources, first, count, buffers, sem):
    def copies(j):
        return [
            pltpu.make_async_copy(source.at[first + j], buffer.at[j], sem.at[j * len(sources) + n])
            for n, (source, buffer) in enumerate(zip(sources, buffers))
        ]

    def start(j):
        for copy in copies(j):
            copy.start()

    each(count, start)
    return lambda j: ready(copies(j))


def ready(line):
    for copy in line:
        copy.wait()


def one_hot(rows, place):
    index = lax.broadcasted_iota(jnp.int32, (rows, place.shape[1]), 0).astype(F32)
    return jnp.where(index == place, 1.0, 0.0)


def pack_kernel(p_ref, tokens_ref, ids_ref, slots_ref, gates_ref, out_ref):
    tok = tokens_ref.shape[0]
    out_ref[0:tok, :] = tokens_ref[...]
    out_ref[tok:, :] = jnp.zeros((ROUTE_ROWS, out_ref.shape[1]), BF16)
    lane = lax.broadcasted_iota(jnp.int32, (tok, 2 * tok), 1)
    row = lax.broadcasted_iota(jnp.int32, (tok, 2 * tok), 0) + p_ref[0] * tok
    place = jnp.where(lane == row, 1.0, 0.0).astype(BF16)
    left = gates_ref[...]
    kinds = [ids_ref[...].astype(F32), slots_ref[...].astype(F32)]
    for _ in range(3):
        kinds.append(left.astype(BF16).astype(F32))
        left = left - kinds[-1]
    kinds = jnp.concatenate(kinds, axis=0).astype(BF16)
    moved = jnp.dot(kinds, place, preferred_element_type=F32)
    none = jnp.zeros((ROUTE_ROWS - TOPK, 2 * tok), F32)
    for n in range(5):
        block = jnp.concatenate([moved[n * TOPK : (n + 1) * TOPK], none], axis=0)
        out_ref[tok:, 2 * tok * n : 2 * tok * (n + 1)] = block.astype(BF16)


def fill(tok_ref, token_refs, side, tok, sem, meta_ref=None):
    copies = []
    zs = len(token_refs) // 2
    for n, ref in enumerate(token_refs):
        d, part = n % zs, side if n < zs else 1 - side
        start = pl.multiple_of(2 * d * tok + part * tok, tok)
        copies.append(pltpu.make_async_copy(ref.at[pl.ds(0, tok)], tok_ref.at[pl.ds(start, tok)], sem.at[n]))
        copies[-1].start()
    routes = []
    if meta_ref is not None:
        for n, ref in enumerate(token_refs):
            source = ref.at[pl.ds(tok, ROUTE_ROWS)]
            routes.append(pltpu.make_async_copy(source, meta_ref.at[n], sem.at[2 * zs + n]))
            routes[-1].start()
    return copies, routes


def dispatch(rows, first, count, group, place_ref, tok_ref, hot_ref, out_ref, level_ref=None):
    def body(g, carry):
        levels = []
        for j in range(group):
            e = first + g * group + j
            hot = one_hot(rows, place_ref[pl.ds(e, 1), :])
            hot_ref[pl.ds(j * rows, rows), :] = hot.astype(BF16)
            if level_ref is not None:
                levels.append(jnp.sum(hot * level_ref[pl.ds(e, 1), :], axis=1, keepdims=True))
        got = jnp.dot(hot_ref[...], tok_ref[...], preferred_element_type=F32)
        if level_ref is not None:
            got = got * jnp.concatenate(levels, axis=0)
        out_ref[pl.ds(g * group, group)] = got.astype(BF16).reshape(group, rows, got.shape[1])
        return carry

    lax.fori_loop(0, count // group, body, 0)


def places(zs, tok, experts, meta_ref, place_ref, level_ref, first):
    lane = lax.broadcasted_iota(jnp.int32, (TOPK, 2 * tok), 1)
    rows, ids, levels = [], [], []
    for d in range(zs):
        meta = meta_ref[d].astype(F32) + meta_ref[zs + d].astype(F32)
        kinds = [meta[0:TOPK, 2 * tok * n : 2 * tok * (n + 1)] for n in range(5)]
        block = 2 * d + (lane >= tok).astype(jnp.int32)
        rows.append(kinds[1] + block.astype(F32) * CAP)
        ids.append(kinds[0])
        levels.append(kinds[2] + kinds[3] + kinds[4])
    row, expert, level = (jnp.concatenate(v, axis=1) for v in (rows, ids, levels))
    for e in range(experts):
        hit = expert == (first + e).astype(F32)
        place_ref[e : e + 1, :] = jnp.max(jnp.where(hit, row, -1.0), axis=0, keepdims=True)
        level_ref[e : e + 1, :] = jnp.sum(jnp.where(hit, level, 0.0), axis=0, keepdims=True)


def at_rows(rows, j):
    return pl.ds(pl.multiple_of(j * rows, rows), rows)


def forward(rows, count, first, arrived, xs, bufs, out_ref):
    def body(j):
        arrived(j)
        x = xs[first + j]
        for n, buf in enumerate(bufs):
            got = jnp.dot(x, buf[j], preferred_element_type=F32)
            out_ref[j, n * rows : (n + 1) * rows, :] = got.astype(out_ref.dtype)

    each(count, body)


def x_kernel(cfg, count, s_ref, *refs):
    zs, tok, experts, rows, group = cfg
    tokens = refs[: 2 * zs]
    gate_ref, up_ref, au_ref, place_ref, level_ref = refs[2 * zs : 2 * zs + 5]
    tok_ref, hot_ref, meta_ref, rows_ref, gate, up, sem, tok_sem = refs[2 * zs + 5 :]
    filling, routes = fill(tok_ref, tokens, s_ref[1], tok, tok_sem, meta_ref)
    copies = load((gate_ref, up_ref), s_ref[0], count, (gate, up), sem)
    ready(routes)
    places(zs, tok, experts, meta_ref, place_ref, level_ref, s_ref[2])
    ready(filling)
    dispatch(rows, s_ref[0], count, group, place_ref, tok_ref, hot_ref, rows_ref)
    forward(rows, count, 0, copies, rows_ref, (gate, up), au_ref)


def x2_kernel(cfg, count, s_ref, *refs):
    zs, tok, experts, rows, group = cfg
    place_ref, gate_ref, up_ref, au_ref, tok_ref, hot_ref, rows_ref, gate, up, sem, tok_sem = refs[2 * zs :]
    filling, _ = fill(tok_ref, refs[: 2 * zs], s_ref[1], tok, tok_sem)
    copies = load((gate_ref, up_ref), s_ref[0], count, (gate, up), sem)
    ready(filling)
    dispatch(rows, s_ref[0], count, group, place_ref, tok_ref, hot_ref, rows_ref)
    forward(rows, count, 0, copies, rows_ref, (gate, up), au_ref)


def back_dots(count, arrived, ys, down, out_ref):
    def body(j):
        arrived(j)
        out_ref[j] = lax.dot_general(ys[j], down[j], NT, preferred_element_type=F32).astype(out_ref.dtype)

    each(count, body)


def y_kernel(cfg, count, s_ref, *refs):
    zs, tok, experts, rows, group = cfg
    tokens = refs[: 2 * zs]
    place_ref, level_ref, down_ref, dh_ref, yin_ref = refs[2 * zs : 2 * zs + 5]
    tok_ref, hot_ref, rows_ref, down, sem, tok_sem, out_sem = refs[2 * zs + 5 :]
    filling, _ = fill(tok_ref, tokens, s_ref[1], tok, tok_sem)
    copies = load((down_ref,), s_ref[0], count, (down,), sem)
    ready(filling)
    dispatch(rows, s_ref[0], experts // 2, group, place_ref, tok_ref, hot_ref, rows_ref, level_ref)
    leaving = pltpu.make_async_copy(rows_ref, yin_ref, out_sem)
    leaving.start()
    back_dots(count, copies, rows_ref, down, dh_ref)
    leaving.wait()


def y2_kernel(start, count, s_ref, yin_ref, down_ref, dh_ref, ys, down, sem, row_sem):
    rows_here = load((yin_ref,), start, count, (ys,), row_sem)
    arrived = load((down_ref,), s_ref[0], count, (down,), sem)
    each(count, rows_here)
    back_dots(count, arrived, ys, down, dh_ref)


def y3_kernel(cfg, count, s_ref, *refs):
    zs, tok, experts, rows, group = cfg
    place_ref, level_ref, down_ref, dh_ref, tok_ref, hot_ref, rows_ref, down, sem, tok_sem = refs[2 * zs :]
    filling, _ = fill(tok_ref, refs[: 2 * zs], s_ref[1], tok, tok_sem)
    copies = load((down_ref,), s_ref[0], count, (down,), sem)
    ready(filling)
    dispatch(rows, s_ref[0], count, group, place_ref, tok_ref, hot_ref, rows_ref, level_ref)
    back_dots(count, copies, rows_ref, down, dh_ref)


def final_kernel(rows, scale, at, off, s_ref, au_m, dh_m, au_r, dh_r, d_ref, score_ref):
    def body(j):
        au = au_m[at + j] + au_r[at + j].astype(F32)
        a, u = au[0:rows], au[rows:]
        dh = dh_m[at + j] + dh_r[off + j].astype(F32)
        sig = jax.nn.sigmoid(a)
        act = a * sig
        channel = jnp.sum(act * u * dh, axis=0, keepdims=True)
        score_ref[j] = channel * channel * scale
        d_ref[j, 0:rows, :] = (dh * u * sig * (1.0 + a * (1.0 - sig))).astype(BF16)
        d_ref[j, rows:, :] = (dh * act).astype(BF16)

    each(d_ref.shape[0], body)


def gradient_rows(rows, d_ref, arrived, gate, up, part_ref, at=0):
    def body(j):
        arrived(at + j)
        part = lax.dot_general(d_ref[j, 0:rows, :], gate[at + j], NT, preferred_element_type=F32)
        part = part + lax.dot_general(d_ref[j, rows:, :], up[at + j], NT, preferred_element_type=F32)
        part_ref[at_rows(rows, at + j), :] = part.astype(BF16)

    each(d_ref.shape[0], body)


def mine_parts_kernel(rows, sizes, s_ref, *refs):
    n = len(sizes)
    gate_ref, up_ref, part_ref, gate, up, sem = refs[n:]
    arrived = load((gate_ref, up_ref), s_ref[0], sum(sizes), (gate, up), sem)
    at = 0
    for d_ref, size in zip(refs[:n], sizes):
        gradient_rows(rows, d_ref, arrived, gate, up, part_ref, at)
        at += size


def combine_kernel(rows, zs, tok, half, at, count, last, s_ref, d_ref, gate_ref, up_ref, place_ref, *refs):
    first = s_ref[0] + at
    if at == 0:
        *mine_refs, acc, gate, up, part_ref, hot_ref, sem = refs
    elif last:
        acc_in, keep_ref, send_ref, gate, up, part_ref, hot_ref, acc, sem = refs
    else:
        acc_in, acc, gate, up, part_ref, hot_ref, sem = refs
    copies = load((gate_ref, up_ref), first, count, (gate, up), sem)

    def mark(start, e, n):
        def body(j):
            hot = one_hot(rows, place_ref[pl.ds(e + j, 1), :])
            hot_ref[at_rows(rows, start + j), :] = hot.astype(BF16)

        each(n, body)

    mark(half if at == 0 else 0, first, count)
    if at == 0:
        mark(0, half - s_ref[0], half)
    cut = 0
    if at == 0:
        for n, mine_ref in enumerate(mine_refs):
            size = mine_ref.shape[0]
            own = lax.dot_general(hot_ref[cut : cut + size, :], mine_ref[...], TN, preferred_element_type=F32)
            acc[...] = own if n == 0 else acc[...] + own
            cut += size
    gradient_rows(rows, d_ref, copies, gate, up, part_ref)
    total = lax.dot_general(hot_ref[cut:, :], part_ref[...], TN, preferred_element_type=F32)
    if at == 0:
        acc[...] += total
        return
    acc[...] = total + acc_in[...]
    if not last:
        return
    side = s_ref[1]
    for d in range(zs):
        keep_ref[d] = acc[pl.ds(pl.multiple_of(2 * d * tok + side * tok, tok), tok), :]
        send_ref[d] = acc[pl.ds(pl.multiple_of(2 * d * tok + (1 - side) * tok, tok), tok), :].astype(BF16)


def stationary(tokens, out_grad, gates, expert_ids, slots, gate_weight, up_weight, down_weight):
    zs = lax.axis_size("expert")
    tok, width = tokens.shape
    experts, _, ff = gate_weight.shape
    rows = 2 * zs * CAP
    all_tok = 2 * zs * tok
    half = experts // 2
    group = 4 if half % 4 == 0 else 1
    p, s, z = lax.axis_index("dp"), lax.axis_index("sub"), lax.axis_index("expert")
    mine0, other0 = half * p, half * (1 - p)
    first = half // 2
    rest = half - first
    sizes = [first, rest]

    def flip(v, axis):
        return lax.ppermute(v, axis, [(0, 1), (1, 0)])

    def turn(v, d):
        pairs = [
            ((i * 2 + a) * 2 + b, (((i + d) % zs) * 2 + b) * 2 + a)
            for i in range(zs)
            for a in range(2)
            for b in range(2)
        ]
        return lax.ppermute(v, ("expert", "dp", "sub"), pairs)

    def shift(v, d):
        return lax.ppermute(v, "expert", [(i, (i + d) % zs) for i in range(zs)])

    def sds(shape, dtype):
        return jax.ShapeDtypeStruct(shape, dtype)

    vmem, anywhere = pl.BlockSpec(memory_space=pltpu.VMEM), pl.BlockSpec(memory_space=pltpu.HBM)
    smem = pl.BlockSpec(memory_space=pltpu.SMEM)
    dma = pltpu.SemaphoreType.DMA

    def call(body, first, second, args, outs, scratch, flops, moved, name, factor=1):
        ins = [spec for spec, group in args for _ in group]
        arrays = [v for _, group in args for v in group]
        info = jnp.stack([jnp.int32(first), jnp.int32(second), jnp.int32(z * experts)])
        return pl.pallas_call(
            body,
            out_shape=outs,
            in_specs=[smem] + ins,
            out_specs=jax.tree.map(lambda v: anywhere if v is rows_shape else vmem, outs),
            scratch_shapes=scratch,
            compiler_params=pltpu.CompilerParams(vmem_limit_bytes=VMEM_LIMIT),
            cost_estimate=pl.CostEstimate(flops=int(flops * COST * factor), bytes_accessed=int(moved * COST * factor), transcendentals=0),
            name=name,
        )(info, *arrays)

    loaded = pl.pallas_call(
        pack_kernel,
        out_shape=sds((tok + ROUTE_ROWS, width), BF16),
        in_specs=[smem] + [vmem] * 4,
        out_specs=vmem,
        name="pack",
    )(jnp.stack([p]).astype(jnp.int32), tokens, expert_ids.T, slots.T, gates.T)
    x_own = [turn(loaded, d) for d in range(zs)]
    out_grad, _ = lax.optimization_barrier((out_grad, loaded))
    y_here = turn(out_grad, 0)
    *x_own, y_here = lax.optimization_barrier((*x_own, y_here))
    x_other = [flip(v, "sub") for v in x_own]
    wbytes = width * ff * 2
    flop = 2 * rows * width * ff
    dflop = 2 * experts * rows * all_tok * width
    cfg = (zs, tok, experts, rows, group)
    hot = pltpu.VMEM((group * rows, all_tok), BF16)
    tok_scratch = pltpu.VMEM((all_tok, width), BF16)

    def wide(count):
        return pltpu.VMEM((count, width, ff), BF16)

    def tall(count):
        return pltpu.VMEM((count, ff, width), BF16)

    place_shape = sds((experts, all_tok), F32)
    rows_shape = pltpu.HBM((half, rows, width), BF16)
    half_rows = pltpu.VMEM((half, rows, width), BF16)
    def pinned(*arrays):
        return tuple(pltpu.with_memory_space_constraint(v, pltpu.HBM) for v in arrays)

    weights = (anywhere, pinned(gate_weight, up_weight))
    down_weight, = pinned(down_weight)
    au_send, place, level = call(
        functools.partial(x_kernel, cfg, half),
        other0,
        s,
        [(anywhere, pinned(*x_own, *x_other)), weights],
        [sds((half, 2 * rows, ff), BF16), place_shape, place_shape],
        [tok_scratch, hot, pltpu.VMEM((2 * zs, ROUTE_ROWS, width), BF16), half_rows, wide(half), wide(half)]
        + [dma((2 * half,)), dma((4 * zs,))],
        2 * half * flop + dflop // 2,
        2 * half * wbytes,
        "x_first",
    )
    y_here, au_send = lax.optimization_barrier((y_here, au_send))
    y_own = [y_here] + [shift(y_here, d) for d in range(1, zs)]

    au_mine = call(
        functools.partial(x2_kernel, cfg, half),
        mine0,
        s,
        [(anywhere, pinned(*x_own, *x_other)), (vmem, (place,)), weights],
        sds((half, 2 * rows, ff), F32),
        [tok_scratch, hot, half_rows, wide(half), wide(half), dma((2 * half,)), dma((2 * zs,))],
        2 * half * flop + dflop // 2,
        2 * half * wbytes,
        "x_mine",
    )
    au_recv = flip(au_send, "dp")
    *y_own, au_mine = lax.optimization_barrier((*y_own, au_mine))
    y_other = [flip(v, "sub") for v in y_own]
    dh_first, yin = call(
        functools.partial(y_kernel, cfg, first),
        other0,
        s,
        [(anywhere, pinned(*y_own, *y_other)), (vmem, (place, level)), (anywhere, (down_weight,))],
        [sds((first, rows, ff), BF16), rows_shape],
        [tok_scratch, hot, half_rows, tall(first), dma((first,)), dma((2 * zs,)), dma],
        first * flop + dflop // 2,
        first * wbytes,
        "y_first",
    )

    yin, au_recv = lax.optimization_barrier((yin, au_recv))
    dh_rest = call(
        functools.partial(y2_kernel, first, rest),
        other0 + first,
        s,
        [(anywhere, pinned(yin, down_weight))],
        sds((rest, rows, ff), BF16),
        [pltpu.VMEM((rest, rows, width), BF16), tall(rest), dma((rest,)), dma((rest,))],
        rest * flop,
        rest * wbytes,
        "y_other",
    )
    place_y, dh_rest = lax.optimization_barrier((place, dh_rest))
    dh_mine = call(
        functools.partial(y3_kernel, cfg, half),
        mine0,
        s,
        [(anywhere, pinned(*y_own, *y_other)), (vmem, (place_y, level)), (anywhere, (down_weight,))],
        sds((half, rows, ff), F32),
        [tok_scratch, hot, half_rows, tall(half), dma((half,)), dma((2 * zs,))],
        half * flop + dflop // 2,
        half * wbytes,
        "y_mine",
    )
    dh_recv = [flip(v, "dp") for v in (dh_first, dh_rest)]
    scale = LOCAL_EXPERTS / (all_tok * TOPK)
    last = 0
    chunks = [(0, 0, first)] + [(1, at, n) for at, n in ((0, rest - last), (rest - last, last)) if n]
    back, scores = [], []

    def final_call(k, at, n):
        d, score = call(
            functools.partial(final_kernel, rows, scale, k * first + at, at),
            mine0,
            s,
            [(vmem, (au_mine, dh_mine, au_recv, dh_recv[k]))],
            [sds((n, 2 * rows, ff), BF16), sds((n, 1, ff), F32)],
            [],
            n * rows * ff * 40,
            n * rows * ff * 30,
            "final",
        )
        scores.append(score)
        if k == 0:
            sent, dh_recv[1] = lax.optimization_barrier((d, dh_recv[1]))
        else:
            sent = d
        back.append(flip(sent, "dp"))
        return d

    def parts_call(start, ds):
        counts = [d.shape[0] for d in ds]
        n = sum(counts)
        return call(
            functools.partial(mine_parts_kernel, rows, counts),
            mine0 + start,
            s,
            [(vmem, ds), weights],
            sds((n * rows, width), BF16),
            [wide(n), wide(n), dma((2 * n,))],
            2 * n * flop,
            2 * n * wbytes,
            "mine_parts",
            PART_COST,
        )

    given = [parts_call(0, [final_call(*chunks[0])])]
    dh_mine, given[0] = lax.optimization_barrier((dh_mine, given[0]))
    ds = []
    for chunk in chunks[1:]:
        ds.append(final_call(*chunk))
        dh_mine, ds[-1] = lax.optimization_barrier((dh_mine, ds[-1]))
    given.append(parts_call(first, ds))
    score = jnp.concatenate(scores, axis=0).reshape(half, ff)
    score_other = flip(score, "dp")
    acc_shape, zshape = (all_tok, width), (zs, tok, width)
    for k, (part, at, n) in enumerate(chunks):
        used, final = n + half * (k == 0), k == len(chunks) - 1
        given = call(
            functools.partial(combine_kernel, rows, zs, tok, half, part * first + at, n, final),
            other0,
            s,
            [(vmem, (back[k],)), weights, (vmem, (place, *given))],
            [sds(zshape, F32), sds(zshape, BF16)] if final else [sds(acc_shape, F32)],
            [wide(n), wide(n), pltpu.VMEM((n * rows, width), BF16), pltpu.VMEM((used * rows, all_tok), BF16)]
            + ([pltpu.VMEM(acc_shape, F32)] if final else [])
            + [dma((2 * n,))],
            2 * n * flop + 2 * used * rows * width * all_tok,
            2 * n * wbytes,
            "combine",
        )
        if k == len(chunks) - 2:
            *given, score_other = lax.optimization_barrier((*given, score_other))
            scores = jnp.concatenate(
                [jnp.where(p == 0, score, score_other), jnp.where(p == 0, score_other, score)], axis=0
            )
    keep, send = given
    summed = (keep + flip(send, "sub").astype(F32)).astype(BF16)
    total = turn(summed[0], 0).astype(F32)
    for d in range(1, zs):
        total = total + turn(summed[d], -d).astype(F32)
    return (scores, total.astype(BF16))


def solution(mesh):
    in_specs = (
        P(("dom", "expert", "dp"), "sub"),
        P(("dom", "expert", "dp"), "sub"),
        P(("dom", "expert", "dp"), None),
        P(("dom", "expert", "dp"), None),
        P(("dom", "expert", "dp"), None),
        P("expert", "dp", "sub"),
        P("expert", "dp", "sub"),
        P("expert", "sub", "dp"),
    )
    out_specs = (P(("dom", "expert"), "sub"), P(("dom", "expert", "dp"), "sub"))
    pairs = mesh.shape["dp"] == 2 and mesh.shape["sub"] == 2
    split = (LOCAL_EXPERTS // mesh.shape["expert"]) % 2 == 0
    local = stationary if pairs and split else gathered
    return jax.shard_map(local, mesh=mesh, in_specs=in_specs, out_specs=out_specs, check_vma=False)
```

```python
import functools

import jax
import jax.numpy as jnp
from jax import lax
from jax.experimental import pallas as pl
from jax.experimental.pallas import tpu as pltpu
from jax.sharding import PartitionSpec as P

LOCAL_EXPERTS = 64
TOPK = 8
CAP = 10
F32 = jnp.float32
BF16 = jnp.bfloat16
NT = (((1,), (1,)), ((), ()))
TN = (((0,), (0,)), ((), ()))
VMEM_LIMIT = 32 * 1024 * 1024


def gathered(tokens, out_grad, gates, expert_ids, slots, gate_weight, up_weight, down_weight):
    expert_count = lax.axis_size("expert")
    group_count = lax.axis_size("dp")
    local_count = gate_weight.shape[0]
    tok_rows = tokens.shape[0]
    half_width = tokens.shape[1]
    slot_count = local_count * expert_count * CAP
    target_dev = expert_ids // local_count
    local_expert = expert_ids % local_count
    slot_rows = ((local_expert * expert_count + target_dev) * CAP + slots).reshape(-1)
    scaled = (gates[:, :, None] * out_grad[:, None, :].astype(F32)).astype(BF16)
    scaled = scaled.reshape(tok_rows * TOPK, half_width)
    repeated = jnp.repeat(tokens, TOPK, axis=0)

    def route(rows):
        send = jnp.zeros((slot_count, half_width), BF16).at[slot_rows].add(rows)
        send = send.reshape(local_count, expert_count, CAP, half_width)
        recv = lax.all_to_all(send, "expert", split_axis=1, concat_axis=1, tiled=True)
        full = lax.all_gather(recv, "sub", axis=3, tiled=True)
        return full.reshape(local_count, expert_count * CAP, full.shape[3])

    x_full, grad_full = route(repeated), route(scaled)
    gate_full = lax.all_gather(gate_weight, "dp", axis=1, tiled=True)
    up_full = lax.all_gather(up_weight, "dp", axis=1, tiled=True)
    down_full = lax.all_gather(down_weight, "dp", axis=2, tiled=True)
    gate_pre = jnp.einsum("erd,edf->erf", x_full, gate_full, preferred_element_type=F32)
    up_pre = jnp.einsum("erd,edf->erf", x_full, up_full, preferred_element_type=F32)
    hidden_grad = jnp.einsum("erd,efd->erf", grad_full, down_full, preferred_element_type=F32)
    gating = jax.nn.sigmoid(gate_pre)
    activated = gate_pre * gating
    channel = lax.psum(jnp.sum(activated * up_pre * hidden_grad, axis=1), "dp")
    scale = LOCAL_EXPERTS / (tok_rows * expert_count * group_count * TOPK)
    scores = channel * channel * scale
    gate_grad = (hidden_grad * up_pre * gating * (1.0 + gate_pre * (1.0 - gating))).astype(BF16)
    up_grad = (hidden_grad * activated).astype(BF16)
    parts = jnp.einsum("erf,edf->erd", gate_grad, gate_full, preferred_element_type=F32)
    parts = parts + jnp.einsum("erf,edf->erd", up_grad, up_full, preferred_element_type=F32)
    summed = lax.psum_scatter(parts.astype(BF16), "sub", scatter_dimension=2, tiled=True)
    summed = summed.reshape(local_count, expert_count, CAP, half_width)
    returned = lax.all_to_all(summed, "expert", split_axis=1, concat_axis=1, tiled=True)
    picked = returned.reshape(slot_count, half_width)[slot_rows].astype(F32)
    token_grad = jnp.sum(picked.reshape(tok_rows, TOPK, half_width), axis=1)
    return (scores, token_grad.astype(BF16))


PART_COST = 1
COST = 1.0


ROUTE_ROWS = 16


def each(count, body):
    def step(j, carry):
        body(j)
        return carry

    lax.fori_loop(0, count, step, 0)


def load(sources, first, count, buffers, sem):
    def copies(j):
        return [
            pltpu.make_async_copy(source.at[first + j], buffer.at[j], sem.at[j * len(sources) + n])
            for n, (source, buffer) in enumerate(zip(sources, buffers))
        ]

    def start(j):
        for copy in copies(j):
            copy.start()

    each(count, start)
    return lambda j: ready(copies(j))


def ready(line):
    for copy in line:
        copy.wait()


def one_hot(rows, place):
    index = lax.broadcasted_iota(jnp.int32, (rows, place.shape[1]), 0).astype(F32)
    return jnp.where(index == place, 1.0, 0.0)


def pack_kernel(p_ref, tokens_ref, ids_ref, slots_ref, gates_ref, out_ref):
    tok = tokens_ref.shape[0]
    out_ref[0:tok, :] = tokens_ref[...]
    out_ref[tok:, :] = jnp.zeros((ROUTE_ROWS, out_ref.shape[1]), BF16)
    lane = lax.broadcasted_iota(jnp.int32, (tok, 2 * tok), 1)
    row = lax.broadcasted_iota(jnp.int32, (tok, 2 * tok), 0) + p_ref[0] * tok
    place = jnp.where(lane == row, 1.0, 0.0).astype(BF16)
    left = gates_ref[...]
    kinds = [ids_ref[...].astype(F32), slots_ref[...].astype(F32)]
    for _ in range(3):
        kinds.append(left.astype(BF16).astype(F32))
        left = left - kinds[-1]
    kinds = jnp.concatenate(kinds, axis=0).astype(BF16)
    moved = jnp.dot(kinds, place, preferred_element_type=F32)
    none = jnp.zeros((ROUTE_ROWS - TOPK, 2 * tok), F32)
    for n in range(5):
        block = jnp.concatenate([moved[n * TOPK : (n + 1) * TOPK], none], axis=0)
        out_ref[tok:, 2 * tok * n : 2 * tok * (n + 1)] = block.astype(BF16)


def fill(tok_ref, token_refs, side, tok, sem, meta_ref=None):
    copies = []
    zs = len(token_refs) // 2
    for n, ref in enumerate(token_refs):
        d, part = n % zs, side if n < zs else 1 - side
        start = pl.multiple_of(2 * d * tok + part * tok, tok)
        copies.append(pltpu.make_async_copy(ref.at[pl.ds(0, tok)], tok_ref.at[pl.ds(start, tok)], sem.at[n]))
        copies[-1].start()
    routes = []
    if meta_ref is not None:
        for n, ref in enumerate(token_refs):
            source = ref.at[pl.ds(tok, ROUTE_ROWS)]
            routes.append(pltpu.make_async_copy(source, meta_ref.at[n], sem.at[2 * zs + n]))
            routes[-1].start()
    return copies, routes


def dispatch(rows, first, count, group, place_ref, tok_ref, hot_ref, out_ref, level_ref=None):
    def body(g, carry):
        levels = []
        for j in range(group):
            e = first + g * group + j
            hot = one_hot(rows, place_ref[pl.ds(e, 1), :])
            hot_ref[pl.ds(j * rows, rows), :] = hot.astype(BF16)
            if level_ref is not None:
                levels.append(jnp.sum(hot * level_ref[pl.ds(e, 1), :], axis=1, keepdims=True))
        got = jnp.dot(hot_ref[...], tok_ref[...], preferred_element_type=F32)
        if level_ref is not None:
            got = got * jnp.concatenate(levels, axis=0)
        out_ref[pl.ds(g * group, group)] = got.astype(BF16).reshape(group, rows, got.shape[1])
        return carry

    lax.fori_loop(0, count // group, body, 0)


def places(zs, tok, experts, meta_ref, place_ref, level_ref, first):
    lane = lax.broadcasted_iota(jnp.int32, (TOPK, 2 * tok), 1)
    rows, ids, levels = [], [], []
    for d in range(zs):
        meta = meta_ref[d].astype(F32) + meta_ref[zs + d].astype(F32)
        kinds = [meta[0:TOPK, 2 * tok * n : 2 * tok * (n + 1)] for n in range(5)]
        block = 2 * d + (lane >= tok).astype(jnp.int32)
        rows.append(kinds[1] + block.astype(F32) * CAP)
        ids.append(kinds[0])
        levels.append(kinds[2] + kinds[3] + kinds[4])
    row, expert, level = (jnp.concatenate(v, axis=1) for v in (rows, ids, levels))
    for e in range(experts):
        hit = expert == (first + e).astype(F32)
        place_ref[e : e + 1, :] = jnp.max(jnp.where(hit, row, -1.0), axis=0, keepdims=True)
        level_ref[e : e + 1, :] = jnp.sum(jnp.where(hit, level, 0.0), axis=0, keepdims=True)


def at_rows(rows, j):
    return pl.ds(pl.multiple_of(j * rows, rows), rows)


def forward(rows, count, first, arrived, xs, bufs, out_ref):
    def body(j):
        arrived(j)
        x = xs[first + j]
        for n, buf in enumerate(bufs):
            got = jnp.dot(x, buf[j], preferred_element_type=F32)
            out_ref[j, n * rows : (n + 1) * rows, :] = got.astype(out_ref.dtype)

    each(count, body)


def x_kernel(cfg, count, s_ref, *refs):
    zs, tok, experts, rows, group = cfg
    tokens = refs[: 2 * zs]
    gate_ref, up_ref, au_ref, place_ref, level_ref = refs[2 * zs : 2 * zs + 5]
    tok_ref, hot_ref, meta_ref, rows_ref, gate, up, sem, tok_sem = refs[2 * zs + 5 :]
    filling, routes = fill(tok_ref, tokens, s_ref[1], tok, tok_sem, meta_ref)
    copies = load((gate_ref, up_ref), s_ref[0], count, (gate, up), sem)
    ready(routes)
    places(zs, tok, experts, meta_ref, place_ref, level_ref, s_ref[2])
    ready(filling)
    dispatch(rows, s_ref[0], count, group, place_ref, tok_ref, hot_ref, rows_ref)
    forward(rows, count, 0, copies, rows_ref, (gate, up), au_ref)


def x2_kernel(cfg, count, s_ref, *refs):
    zs, tok, experts, rows, group = cfg
    place_ref, gate_ref, up_ref, au_ref, tok_ref, hot_ref, rows_ref, gate, up, sem, tok_sem = refs[2 * zs :]
    filling, _ = fill(tok_ref, refs[: 2 * zs], s_ref[1], tok, tok_sem)
    copies = load((gate_ref, up_ref), s_ref[0], count, (gate, up), sem)
    ready(filling)
    dispatch(rows, s_ref[0], count, group, place_ref, tok_ref, hot_ref, rows_ref)
    forward(rows, count, 0, copies, rows_ref, (gate, up), au_ref)


def back_dots(count, arrived, ys, down, out_ref):
    def body(j):
        arrived(j)
        out_ref[j] = lax.dot_general(ys[j], down[j], NT, preferred_element_type=F32).astype(out_ref.dtype)

    each(count, body)


def y_kernel(cfg, count, s_ref, *refs):
    zs, tok, experts, rows, group = cfg
    tokens = refs[: 2 * zs]
    place_ref, level_ref, down_ref, dh_ref, yin_ref = refs[2 * zs : 2 * zs + 5]
    tok_ref, hot_ref, rows_ref, down, sem, tok_sem, out_sem = refs[2 * zs + 5 :]
    filling, _ = fill(tok_ref, tokens, s_ref[1], tok, tok_sem)
    copies = load((down_ref,), s_ref[0], count, (down,), sem)
    ready(filling)
    dispatch(rows, s_ref[0], experts // 2, group, place_ref, tok_ref, hot_ref, rows_ref, level_ref)
    leaving = pltpu.make_async_copy(rows_ref, yin_ref, out_sem)
    leaving.start()
    back_dots(count, copies, rows_ref, down, dh_ref)
    leaving.wait()


def y2_kernel(start, count, s_ref, yin_ref, down_ref, dh_ref, ys, down, sem, row_sem):
    rows_here = load((yin_ref,), start, count, (ys,), row_sem)
    arrived = load((down_ref,), s_ref[0], count, (down,), sem)
    each(count, rows_here)
    back_dots(count, arrived, ys, down, dh_ref)


def y3_kernel(cfg, count, s_ref, *refs):
    zs, tok, experts, rows, group = cfg
    place_ref, level_ref, down_ref, dh_ref, tok_ref, hot_ref, rows_ref, down, sem, tok_sem = refs[2 * zs :]
    filling, _ = fill(tok_ref, refs[: 2 * zs], s_ref[1], tok, tok_sem)
    copies = load((down_ref,), s_ref[0], count, (down,), sem)
    ready(filling)
    dispatch(rows, s_ref[0], count, group, place_ref, tok_ref, hot_ref, rows_ref, level_ref)
    back_dots(count, copies, rows_ref, down, dh_ref)


def final_kernel(rows, scale, at, off, s_ref, au_m, dh_m, au_r, dh_r, d_ref, score_ref):
    def body(j):
        au = au_m[at + j] + au_r[at + j].astype(F32)
        a, u = au[0:rows], au[rows:]
        dh = dh_m[at + j] + dh_r[off + j].astype(F32)
        sig = jax.nn.sigmoid(a)
        act = a * sig
        channel = jnp.sum(act * u * dh, axis=0, keepdims=True)
        score_ref[j] = channel * channel * scale
        d_ref[j, 0:rows, :] = (dh * u * sig * (1.0 + a * (1.0 - sig))).astype(BF16)
        d_ref[j, rows:, :] = (dh * act).astype(BF16)

    each(d_ref.shape[0], body)


def gradient_rows(rows, d_ref, arrived, gate, up, part_ref, at=0):
    def body(j):
        arrived(at + j)
        part = lax.dot_general(d_ref[j, 0:rows, :], gate[at + j], NT, preferred_element_type=F32)
        part = part + lax.dot_general(d_ref[j, rows:, :], up[at + j], NT, preferred_element_type=F32)
        part_ref[at_rows(rows, at + j), :] = part.astype(BF16)

    each(d_ref.shape[0], body)


def mine_parts_kernel(rows, sizes, s_ref, *refs):
    n = len(sizes)
    gate_ref, up_ref, part_ref, gate, up, sem = refs[n:]
    arrived = load((gate_ref, up_ref), s_ref[0], sum(sizes), (gate, up), sem)
    at = 0
    for d_ref, size in zip(refs[:n], sizes):
        gradient_rows(rows, d_ref, arrived, gate, up, part_ref, at)
        at += size


def combine_kernel(rows, zs, tok, half, at, count, last, s_ref, d_ref, gate_ref, up_ref, place_ref, *refs):
    first = s_ref[0] + at
    if at == 0:
        *mine_refs, acc, gate, up, part_ref, hot_ref, sem = refs
    elif last:
        acc_in, keep_ref, send_ref, gate, up, part_ref, hot_ref, sem = refs
    else:
        acc_in, acc, gate, up, part_ref, hot_ref, sem = refs
    copies = load((gate_ref, up_ref), first, count, (gate, up), sem)

    def mark(start, e, n):
        def body(j):
            hot = one_hot(rows, place_ref[pl.ds(e + j, 1), :])
            hot_ref[at_rows(rows, start + j), :] = hot.astype(BF16)

        each(n, body)

    mark(half if at == 0 else 0, first, count)
    if at == 0:
        mark(0, half - s_ref[0], half)
    cut = 0
    if at == 0:
        for n, mine_ref in enumerate(mine_refs):
            size = mine_ref.shape[0]
            own = lax.dot_general(hot_ref[cut : cut + size, :], mine_ref[...], TN, preferred_element_type=F32)
            acc[...] = own if n == 0 else acc[...] + own
            cut += size
    gradient_rows(rows, d_ref, copies, gate, up, part_ref)
    total = lax.dot_general(hot_ref[cut:, :], part_ref[...], TN, preferred_element_type=F32)
    if at == 0:
        acc[...] += total
        return
    total = total + acc_in[...]
    if not last:
        acc[...] = total
        return
    for d in range(zs):
        low, high = total[2 * d * tok : (2 * d + 1) * tok], total[(2 * d + 1) * tok : 2 * (d + 1) * tok]
        keep_ref[d] = jnp.where(s_ref[1] == 0, low, high)
        send_ref[d] = jnp.where(s_ref[1] == 0, high, low).astype(BF16)


def stationary(tokens, out_grad, gates, expert_ids, slots, gate_weight, up_weight, down_weight):
    zs = lax.axis_size("expert")
    tok, width = tokens.shape
    experts, _, ff = gate_weight.shape
    rows = 2 * zs * CAP
    all_tok = 2 * zs * tok
    half = experts // 2
    group = 4 if half % 4 == 0 else 1
    p, s, z = lax.axis_index("dp"), lax.axis_index("sub"), lax.axis_index("expert")
    mine0, other0 = half * p, half * (1 - p)
    first = half // 2
    rest = half - first
    sizes = [first, rest]

    def flip(v, axis):
        return lax.ppermute(v, axis, [(0, 1), (1, 0)])

    def turn(v, d):
        pairs = [
            ((i * 2 + a) * 2 + b, (((i + d) % zs) * 2 + b) * 2 + a)
            for i in range(zs)
            for a in range(2)
            for b in range(2)
        ]
        return lax.ppermute(v, ("expert", "dp", "sub"), pairs)

    def shift(v, d):
        return lax.ppermute(v, "expert", [(i, (i + d) % zs) for i in range(zs)])

    def sds(shape, dtype):
        return jax.ShapeDtypeStruct(shape, dtype)

    vmem, anywhere = pl.BlockSpec(memory_space=pltpu.VMEM), pl.BlockSpec(memory_space=pltpu.HBM)
    smem = pl.BlockSpec(memory_space=pltpu.SMEM)
    dma = pltpu.SemaphoreType.DMA

    def call(body, first, second, args, outs, scratch, flops, moved, name, factor=1):
        ins = [spec for spec, group in args for _ in group]
        arrays = [v for _, group in args for v in group]
        info = jnp.stack([jnp.int32(first), jnp.int32(second), jnp.int32(z * experts)])
        return pl.pallas_call(
            body,
            out_shape=outs,
            in_specs=[smem] + ins,
            out_specs=jax.tree.map(lambda v: anywhere if v is rows_shape else vmem, outs),
            scratch_shapes=scratch,
            compiler_params=pltpu.CompilerParams(vmem_limit_bytes=VMEM_LIMIT),
            cost_estimate=pl.CostEstimate(flops=int(flops * COST * factor), bytes_accessed=int(moved * COST * factor), transcendentals=0),
            name=name,
        )(info, *arrays)

    loaded = pl.pallas_call(
        pack_kernel,
        out_shape=sds((tok + ROUTE_ROWS, width), BF16),
        in_specs=[smem] + [vmem] * 4,
        out_specs=vmem,
        name="pack",
    )(jnp.stack([p]).astype(jnp.int32), tokens, expert_ids.T, slots.T, gates.T)
    x_own = [turn(loaded, d) for d in range(zs)]
    out_grad, _ = lax.optimization_barrier((out_grad, loaded))
    y_here = turn(out_grad, 0)
    *x_own, y_here = lax.optimization_barrier((*x_own, y_here))
    x_other = [flip(v, "sub") for v in x_own]
    wbytes = width * ff * 2
    flop = 2 * rows * width * ff
    dflop = 2 * experts * rows * all_tok * width
    cfg = (zs, tok, experts, rows, group)
    hot = pltpu.VMEM((group * rows, all_tok), BF16)
    tok_scratch = pltpu.VMEM((all_tok, width), BF16)

    def wide(count):
        return pltpu.VMEM((count, width, ff), BF16)

    def tall(count):
        return pltpu.VMEM((count, ff, width), BF16)

    place_shape = sds((experts, all_tok), F32)
    rows_shape = pltpu.HBM((half, rows, width), BF16)
    half_rows = pltpu.VMEM((half, rows, width), BF16)
    def pinned(*arrays):
        return tuple(pltpu.with_memory_space_constraint(v, pltpu.HBM) for v in arrays)

    weights = (anywhere, pinned(gate_weight, up_weight))
    down_weight, = pinned(down_weight)
    au_send, place, level = call(
        functools.partial(x_kernel, cfg, half),
        other0,
        s,
        [(anywhere, pinned(*x_own, *x_other)), weights],
        [sds((half, 2 * rows, ff), BF16), place_shape, place_shape],
        [tok_scratch, hot, pltpu.VMEM((2 * zs, ROUTE_ROWS, width), BF16), half_rows, wide(half), wide(half)]
        + [dma((2 * half,)), dma((4 * zs,))],
        2 * half * flop + dflop // 2,
        2 * half * wbytes,
        "x_first",
    )
    y_here, au_send = lax.optimization_barrier((y_here, au_send))
    y_own = [y_here] + [shift(y_here, d) for d in range(1, zs)]

    au_mine = call(
        functools.partial(x2_kernel, cfg, half),
        mine0,
        s,
        [(anywhere, pinned(*x_own, *x_other)), (vmem, (place,)), weights],
        sds((half, 2 * rows, ff), F32),
        [tok_scratch, hot, half_rows, wide(half), wide(half), dma((2 * half,)), dma((2 * zs,))],
        2 * half * flop + dflop // 2,
        2 * half * wbytes,
        "x_mine",
    )
    au_recv = flip(au_send, "dp")
    *y_own, au_mine = lax.optimization_barrier((*y_own, au_mine))
    y_other = [flip(v, "sub") for v in y_own]
    dh_first, yin = call(
        functools.partial(y_kernel, cfg, first),
        other0,
        s,
        [(anywhere, pinned(*y_own, *y_other)), (vmem, (place, level)), (anywhere, (down_weight,))],
        [sds((first, rows, ff), BF16), rows_shape],
        [tok_scratch, hot, half_rows, tall(first), dma((first,)), dma((2 * zs,)), dma],
        first * flop + dflop // 2,
        first * wbytes,
        "y_first",
    )

    yin, au_recv = lax.optimization_barrier((yin, au_recv))
    dh_rest = call(
        functools.partial(y2_kernel, first, rest),
        other0 + first,
        s,
        [(anywhere, pinned(yin, down_weight))],
        sds((rest, rows, ff), BF16),
        [pltpu.VMEM((rest, rows, width), BF16), tall(rest), dma((rest,)), dma((rest,))],
        rest * flop,
        rest * wbytes,
        "y_other",
    )
    place_y, dh_rest = lax.optimization_barrier((place, dh_rest))
    dh_mine = call(
        functools.partial(y3_kernel, cfg, half),
        mine0,
        s,
        [(anywhere, pinned(*y_own, *y_other)), (vmem, (place_y, level)), (anywhere, (down_weight,))],
        sds((half, rows, ff), F32),
        [tok_scratch, hot, half_rows, tall(half), dma((half,)), dma((2 * zs,))],
        half * flop + dflop // 2,
        half * wbytes,
        "y_mine",
    )
    dh_recv = [flip(v, "dp") for v in (dh_first, dh_rest)]
    scale = LOCAL_EXPERTS / (all_tok * TOPK)
    last = 0
    chunks = [(0, 0, first)] + [(1, at, n) for at, n in ((0, rest - last), (rest - last, last)) if n]
    back, scores = [], []

    def final_call(k, at, n):
        d, score = call(
            functools.partial(final_kernel, rows, scale, k * first + at, at),
            mine0,
            s,
            [(vmem, (au_mine, dh_mine, au_recv, dh_recv[k]))],
            [sds((n, 2 * rows, ff), BF16), sds((n, 1, ff), F32)],
            [],
            n * rows * ff * 40,
            n * rows * ff * 30,
            "final",
        )
        scores.append(score)
        sent = d
        back.append(flip(sent, "dp"))
        return d

    def parts_call(start, ds):
        counts = [d.shape[0] for d in ds]
        n = sum(counts)
        return call(
            functools.partial(mine_parts_kernel, rows, counts),
            mine0 + start,
            s,
            [(vmem, ds), weights],
            sds((n * rows, width), BF16),
            [wide(n), wide(n), dma((2 * n,))],
            2 * n * flop,
            2 * n * wbytes,
            "mine_parts",
            PART_COST,
        )

    given = [parts_call(0, [final_call(*chunks[0])])]
    dh_mine, given[0] = lax.optimization_barrier((dh_mine, given[0]))
    ds = []
    for chunk in chunks[1:]:
        ds.append(final_call(*chunk))
        dh_mine, ds[-1] = lax.optimization_barrier((dh_mine, ds[-1]))
    given.append(parts_call(first, ds))
    score = jnp.concatenate(scores, axis=0).reshape(half, ff)
    score_other = flip(score, "dp")
    acc_shape, zshape = (all_tok, width), (zs, tok, width)
    for k, (part, at, n) in enumerate(chunks):
        used, final = n + half * (k == 0), k == len(chunks) - 1
        given = call(
            functools.partial(combine_kernel, rows, zs, tok, half, part * first + at, n, final),
            other0,
            s,
            [(vmem, (back[k],)), weights, (vmem, (place, *given))],
            [sds(zshape, F32), sds(zshape, BF16)] if final else [sds(acc_shape, F32)],
            [wide(n), wide(n), pltpu.VMEM((n * rows, width), BF16), pltpu.VMEM((used * rows, all_tok), BF16)]
            + [dma((2 * n,))],
            2 * n * flop + 2 * used * rows * width * all_tok,
            2 * n * wbytes,
            "combine",
        )
        if k == len(chunks) - 2:
            *given, score_other = lax.optimization_barrier((*given, score_other))
            scores = jnp.concatenate(
                [jnp.where(p == 0, score, score_other), jnp.where(p == 0, score_other, score)], axis=0
            )
    keep, send = given
    summed = (keep + flip(send, "sub").astype(F32)).astype(BF16)
    total = turn(summed[0], 0).astype(F32)
    for d in range(1, zs):
        total = total + turn(summed[d], -d).astype(F32)
    return (scores, total.astype(BF16))


def solution(mesh):
    in_specs = (
        P(("dom", "expert", "dp"), "sub"),
        P(("dom", "expert", "dp"), "sub"),
        P(("dom", "expert", "dp"), None),
        P(("dom", "expert", "dp"), None),
        P(("dom", "expert", "dp"), None),
        P("expert", "dp", "sub"),
        P("expert", "dp", "sub"),
        P("expert", "sub", "dp"),
    )
    out_specs = (P(("dom", "expert"), "sub"), P(("dom", "expert", "dp"), "sub"))
    pairs = mesh.shape["dp"] == 2 and mesh.shape["sub"] == 2
    split = (LOCAL_EXPERTS // mesh.shape["expert"]) % 2 == 0
    local = stationary if pairs and split else gathered
    return jax.shard_map(local, mesh=mesh, in_specs=in_specs, out_specs=out_specs, check_vma=False)
```

```python
import functools

import jax
import jax.numpy as jnp
from jax import lax
from jax.experimental import pallas as pl
from jax.experimental.pallas import tpu as pltpu
from jax.sharding import PartitionSpec as P

LOCAL_EXPERTS = 64
TOPK = 8
CAP = 10
F32 = jnp.float32
BF16 = jnp.bfloat16
NT = (((1,), (1,)), ((), ()))
TN = (((0,), (0,)), ((), ()))
VMEM_LIMIT = 32 * 1024 * 1024


def gathered(tokens, out_grad, gates, expert_ids, slots, gate_weight, up_weight, down_weight):
    expert_count = lax.axis_size("expert")
    group_count = lax.axis_size("dp")
    local_count = gate_weight.shape[0]
    tok_rows = tokens.shape[0]
    half_width = tokens.shape[1]
    slot_count = local_count * expert_count * CAP
    target_dev = expert_ids // local_count
    local_expert = expert_ids % local_count
    slot_rows = ((local_expert * expert_count + target_dev) * CAP + slots).reshape(-1)
    scaled = (gates[:, :, None] * out_grad[:, None, :].astype(F32)).astype(BF16)
    scaled = scaled.reshape(tok_rows * TOPK, half_width)
    repeated = jnp.repeat(tokens, TOPK, axis=0)

    def route(rows):
        send = jnp.zeros((slot_count, half_width), BF16).at[slot_rows].add(rows)
        send = send.reshape(local_count, expert_count, CAP, half_width)
        recv = lax.all_to_all(send, "expert", split_axis=1, concat_axis=1, tiled=True)
        full = lax.all_gather(recv, "sub", axis=3, tiled=True)
        return full.reshape(local_count, expert_count * CAP, full.shape[3])

    x_full, grad_full = route(repeated), route(scaled)
    gate_full = lax.all_gather(gate_weight, "dp", axis=1, tiled=True)
    up_full = lax.all_gather(up_weight, "dp", axis=1, tiled=True)
    down_full = lax.all_gather(down_weight, "dp", axis=2, tiled=True)
    gate_pre = jnp.einsum("erd,edf->erf", x_full, gate_full, preferred_element_type=F32)
    up_pre = jnp.einsum("erd,edf->erf", x_full, up_full, preferred_element_type=F32)
    hidden_grad = jnp.einsum("erd,efd->erf", grad_full, down_full, preferred_element_type=F32)
    gating = jax.nn.sigmoid(gate_pre)
    activated = gate_pre * gating
    channel = lax.psum(jnp.sum(activated * up_pre * hidden_grad, axis=1), "dp")
    scale = LOCAL_EXPERTS / (tok_rows * expert_count * group_count * TOPK)
    scores = channel * channel * scale
    gate_grad = (hidden_grad * up_pre * gating * (1.0 + gate_pre * (1.0 - gating))).astype(BF16)
    up_grad = (hidden_grad * activated).astype(BF16)
    parts = jnp.einsum("erf,edf->erd", gate_grad, gate_full, preferred_element_type=F32)
    parts = parts + jnp.einsum("erf,edf->erd", up_grad, up_full, preferred_element_type=F32)
    summed = lax.psum_scatter(parts.astype(BF16), "sub", scatter_dimension=2, tiled=True)
    summed = summed.reshape(local_count, expert_count, CAP, half_width)
    returned = lax.all_to_all(summed, "expert", split_axis=1, concat_axis=1, tiled=True)
    picked = returned.reshape(slot_count, half_width)[slot_rows].astype(F32)
    token_grad = jnp.sum(picked.reshape(tok_rows, TOPK, half_width), axis=1)
    return (scores, token_grad.astype(BF16))


PART_COST = 1
COST = 1.0


ROUTE_ROWS = 16


def each(count, body):
    def step(j, carry):
        body(j)
        return carry

    lax.fori_loop(0, count, step, 0)


def load(sources, first, count, buffers, sem):
    def copies(j):
        return [
            pltpu.make_async_copy(source.at[first + j], buffer.at[j], sem.at[j * len(sources) + n])
            for n, (source, buffer) in enumerate(zip(sources, buffers))
        ]

    def start(j):
        for copy in copies(j):
            copy.start()

    each(count, start)
    return lambda j: ready(copies(j))


def ready(line):
    for copy in line:
        copy.wait()


def one_hot(rows, place):
    index = lax.broadcasted_iota(jnp.int32, (rows, place.shape[1]), 0).astype(F32)
    return jnp.where(index == place, 1.0, 0.0)


def pack_kernel(p_ref, tokens_ref, ids_ref, slots_ref, gates_ref, out_ref):
    tok = tokens_ref.shape[0]
    out_ref[0:tok, :] = tokens_ref[...]
    out_ref[tok:, :] = jnp.zeros((ROUTE_ROWS, out_ref.shape[1]), BF16)
    lane = lax.broadcasted_iota(jnp.int32, (tok, 2 * tok), 1)
    row = lax.broadcasted_iota(jnp.int32, (tok, 2 * tok), 0) + p_ref[0] * tok
    place = jnp.where(lane == row, 1.0, 0.0).astype(BF16)
    left = gates_ref[...]
    kinds = [ids_ref[...].astype(F32), slots_ref[...].astype(F32)]
    for _ in range(3):
        kinds.append(left.astype(BF16).astype(F32))
        left = left - kinds[-1]
    kinds = jnp.concatenate(kinds, axis=0).astype(BF16)
    moved = jnp.dot(kinds, place, preferred_element_type=F32)
    none = jnp.zeros((ROUTE_ROWS - TOPK, 2 * tok), F32)
    for n in range(5):
        block = jnp.concatenate([moved[n * TOPK : (n + 1) * TOPK], none], axis=0)
        out_ref[tok:, 2 * tok * n : 2 * tok * (n + 1)] = block.astype(BF16)


def fill(tok_ref, token_refs, side, tok, sem, meta_ref=None):
    copies = []
    zs = len(token_refs) // 2
    for n, ref in enumerate(token_refs):
        d, part = n % zs, side if n < zs else 1 - side
        start = pl.multiple_of(2 * d * tok + part * tok, tok)
        copies.append(pltpu.make_async_copy(ref.at[pl.ds(0, tok)], tok_ref.at[pl.ds(start, tok)], sem.at[n]))
        copies[-1].start()
    routes = []
    if meta_ref is not None:
        for n, ref in enumerate(token_refs):
            source = ref.at[pl.ds(tok, ROUTE_ROWS)]
            routes.append(pltpu.make_async_copy(source, meta_ref.at[n], sem.at[2 * zs + n]))
            routes[-1].start()
    return copies, routes


def dispatch(rows, first, count, group, place_ref, tok_ref, hot_ref, out_ref, level_ref=None):
    def body(g, carry):
        levels = []
        for j in range(group):
            e = first + g * group + j
            hot = one_hot(rows, place_ref[pl.ds(e, 1), :])
            hot_ref[pl.ds(j * rows, rows), :] = hot.astype(BF16)
            if level_ref is not None:
                levels.append(jnp.sum(hot * level_ref[pl.ds(e, 1), :], axis=1, keepdims=True))
        got = jnp.dot(hot_ref[...], tok_ref[...], preferred_element_type=F32)
        if level_ref is not None:
            got = got * jnp.concatenate(levels, axis=0)
        out_ref[pl.ds(g * group, group)] = got.astype(BF16).reshape(group, rows, got.shape[1])
        return carry

    lax.fori_loop(0, count // group, body, 0)


def places(zs, tok, experts, meta_ref, place_ref, level_ref, first):
    lane = lax.broadcasted_iota(jnp.int32, (TOPK, 2 * tok), 1)
    rows, ids, levels = [], [], []
    for d in range(zs):
        meta = meta_ref[d].astype(F32) + meta_ref[zs + d].astype(F32)
        kinds = [meta[0:TOPK, 2 * tok * n : 2 * tok * (n + 1)] for n in range(5)]
        block = 2 * d + (lane >= tok).astype(jnp.int32)
        rows.append(kinds[1] + block.astype(F32) * CAP)
        ids.append(kinds[0])
        levels.append(kinds[2] + kinds[3] + kinds[4])
    row, expert, level = (jnp.concatenate(v, axis=1) for v in (rows, ids, levels))
    for e in range(experts):
        hit = expert == (first + e).astype(F32)
        place_ref[e : e + 1, :] = jnp.max(jnp.where(hit, row, -1.0), axis=0, keepdims=True)
        level_ref[e : e + 1, :] = jnp.sum(jnp.where(hit, level, 0.0), axis=0, keepdims=True)


def at_rows(rows, j):
    return pl.ds(pl.multiple_of(j * rows, rows), rows)


def forward(rows, count, first, arrived, xs, bufs, out_ref):
    def body(j):
        arrived(j)
        x = xs[first + j]
        for n, buf in enumerate(bufs):
            got = jnp.dot(x, buf[j], preferred_element_type=F32)
            out_ref[j, n * rows : (n + 1) * rows, :] = got.astype(out_ref.dtype)

    each(count, body)


def x_kernel(cfg, count, s_ref, *refs):
    zs, tok, experts, rows, group = cfg
    tokens = refs[: 2 * zs]
    gate_ref, up_ref, au_ref, place_ref, level_ref = refs[2 * zs : 2 * zs + 5]
    tok_ref, hot_ref, meta_ref, rows_ref, gate, up, sem, tok_sem = refs[2 * zs + 5 :]
    filling, routes = fill(tok_ref, tokens, s_ref[1], tok, tok_sem, meta_ref)
    copies = load((gate_ref, up_ref), s_ref[0], count, (gate, up), sem)
    ready(routes)
    places(zs, tok, experts, meta_ref, place_ref, level_ref, s_ref[2])
    ready(filling)
    dispatch(rows, s_ref[0], count, group, place_ref, tok_ref, hot_ref, rows_ref)
    forward(rows, count, 0, copies, rows_ref, (gate, up), au_ref)


def x2_kernel(cfg, count, s_ref, *refs):
    zs, tok, experts, rows, group = cfg
    place_ref, gate_ref, up_ref, au_ref, tok_ref, hot_ref, rows_ref, gate, up, sem, tok_sem = refs[2 * zs :]
    filling, _ = fill(tok_ref, refs[: 2 * zs], s_ref[1], tok, tok_sem)
    copies = load((gate_ref, up_ref), s_ref[0], count, (gate, up), sem)
    ready(filling)
    dispatch(rows, s_ref[0], count, group, place_ref, tok_ref, hot_ref, rows_ref)
    forward(rows, count, 0, copies, rows_ref, (gate, up), au_ref)


def back_dots(count, arrived, ys, down, out_ref):
    def body(j):
        arrived(j)
        out_ref[j] = lax.dot_general(ys[j], down[j], NT, preferred_element_type=F32).astype(out_ref.dtype)

    each(count, body)


def y_kernel(cfg, count, s_ref, *refs):
    zs, tok, experts, rows, group = cfg
    tokens = refs[: 2 * zs]
    place_ref, level_ref, down_ref, dh_ref, yin_ref = refs[2 * zs : 2 * zs + 5]
    tok_ref, hot_ref, rows_ref, down, sem, tok_sem, out_sem = refs[2 * zs + 5 :]
    filling, _ = fill(tok_ref, tokens, s_ref[1], tok, tok_sem)
    copies = load((down_ref,), s_ref[0], count, (down,), sem)
    ready(filling)
    dispatch(rows, s_ref[0], experts // 2, group, place_ref, tok_ref, hot_ref, rows_ref, level_ref)
    leaving = pltpu.make_async_copy(rows_ref, yin_ref, out_sem)
    leaving.start()
    back_dots(count, copies, rows_ref, down, dh_ref)
    leaving.wait()


def y2_kernel(start, count, s_ref, yin_ref, down_ref, dh_ref, ys, down, sem, row_sem):
    rows_here = load((yin_ref,), start, count, (ys,), row_sem)
    arrived = load((down_ref,), s_ref[0], count, (down,), sem)
    each(count, rows_here)
    back_dots(count, arrived, ys, down, dh_ref)


def y3_kernel(cfg, count, s_ref, *refs):
    zs, tok, experts, rows, group = cfg
    place_ref, level_ref, down_ref, dh_ref, tok_ref, hot_ref, rows_ref, down, sem, tok_sem = refs[2 * zs :]
    filling, _ = fill(tok_ref, refs[: 2 * zs], s_ref[1], tok, tok_sem)
    copies = load((down_ref,), s_ref[0], count, (down,), sem)
    ready(filling)
    dispatch(rows, s_ref[0], count, group, place_ref, tok_ref, hot_ref, rows_ref, level_ref)
    back_dots(count, copies, rows_ref, down, dh_ref)


def final_kernel(rows, scale, at, off, s_ref, au_m, dh_m, au_r, dh_r, d_ref, score_ref):
    def body(j):
        au = au_m[at + j] + au_r[at + j].astype(F32)
        a, u = au[0:rows], au[rows:]
        dh = dh_m[at + j] + dh_r[off + j].astype(F32)
        sig = jax.nn.sigmoid(a)
        act = a * sig
        channel = jnp.sum(act * u * dh, axis=0, keepdims=True)
        score_ref[j] = channel * channel * scale
        d_ref[j, 0:rows, :] = (dh * u * sig * (1.0 + a * (1.0 - sig))).astype(BF16)
        d_ref[j, rows:, :] = (dh * act).astype(BF16)

    each(d_ref.shape[0], body)


def gradient_rows(rows, d_ref, arrived, gate, up, part_ref, at=0):
    def body(j):
        arrived(at + j)
        part = lax.dot_general(d_ref[j, 0:rows, :], gate[at + j], NT, preferred_element_type=F32)
        part = part + lax.dot_general(d_ref[j, rows:, :], up[at + j], NT, preferred_element_type=F32)
        part_ref[at_rows(rows, at + j), :] = part.astype(BF16)

    each(d_ref.shape[0], body)


def mine_parts_kernel(rows, sizes, s_ref, *refs):
    n = len(sizes)
    gate_ref, up_ref, part_ref, gate, up, sem = refs[n:]
    arrived = load((gate_ref, up_ref), s_ref[0], sum(sizes), (gate, up), sem)
    at = 0
    for d_ref, size in zip(refs[:n], sizes):
        gradient_rows(rows, d_ref, arrived, gate, up, part_ref, at)
        at += size


def combine_kernel(rows, zs, tok, half, at, count, last, s_ref, d_ref, gate_ref, up_ref, place_ref, *refs):
    first = s_ref[0] + at
    if at == 0:
        *mine_refs, acc, gate, up, part_ref, hot_ref, sem = refs
    elif last:
        acc_in, keep_ref, send_ref, gate, up, part_ref, hot_ref, sem = refs
    else:
        acc_in, acc, gate, up, part_ref, hot_ref, sem = refs
    copies = load((gate_ref, up_ref), first, count, (gate, up), sem)

    def mark(start, e, n):
        def body(j):
            hot = one_hot(rows, place_ref[pl.ds(e + j, 1), :])
            hot_ref[at_rows(rows, start + j), :] = hot.astype(BF16)

        each(n, body)

    mark(half if at == 0 else 0, first, count)
    if at == 0:
        mark(0, half - s_ref[0], half)
    cut = 0
    if at == 0:
        for n, mine_ref in enumerate(mine_refs):
            size = mine_ref.shape[0]
            own = lax.dot_general(hot_ref[cut : cut + size, :], mine_ref[...], TN, preferred_element_type=F32)
            acc[...] = own if n == 0 else acc[...] + own
            cut += size
    gradient_rows(rows, d_ref, copies, gate, up, part_ref)
    total = lax.dot_general(hot_ref[cut:, :], part_ref[...], TN, preferred_element_type=F32)
    if at == 0:
        acc[...] += total
        return
    total = total + acc_in[...]
    if not last:
        acc[...] = total
        return
    for d in range(zs):
        low, high = total[2 * d * tok : (2 * d + 1) * tok], total[(2 * d + 1) * tok : 2 * (d + 1) * tok]
        keep_ref[d] = jnp.where(s_ref[1] == 0, low, high)
        send_ref[d] = jnp.where(s_ref[1] == 0, high, low).astype(BF16)


def stationary(tokens, out_grad, gates, expert_ids, slots, gate_weight, up_weight, down_weight):
    zs = lax.axis_size("expert")
    tok, width = tokens.shape
    experts, _, ff = gate_weight.shape
    rows = 2 * zs * CAP
    all_tok = 2 * zs * tok
    half = experts // 2
    group = half
    p, s, z = lax.axis_index("dp"), lax.axis_index("sub"), lax.axis_index("expert")
    mine0, other0 = half * p, half * (1 - p)
    first = half // 2
    rest = half - first
    sizes = [first, rest]

    def flip(v, axis):
        return lax.ppermute(v, axis, [(0, 1), (1, 0)])

    def turn(v, d):
        pairs = [
            ((i * 2 + a) * 2 + b, (((i + d) % zs) * 2 + b) * 2 + a)
            for i in range(zs)
            for a in range(2)
            for b in range(2)
        ]
        return lax.ppermute(v, ("expert", "dp", "sub"), pairs)

    def shift(v, d):
        return lax.ppermute(v, "expert", [(i, (i + d) % zs) for i in range(zs)])

    def sds(shape, dtype):
        return jax.ShapeDtypeStruct(shape, dtype)

    vmem, anywhere = pl.BlockSpec(memory_space=pltpu.VMEM), pl.BlockSpec(memory_space=pltpu.HBM)
    smem = pl.BlockSpec(memory_space=pltpu.SMEM)
    dma = pltpu.SemaphoreType.DMA

    def call(body, first, second, args, outs, scratch, flops, moved, name, factor=1):
        ins = [spec for spec, group in args for _ in group]
        arrays = [v for _, group in args for v in group]
        info = jnp.stack([jnp.int32(first), jnp.int32(second), jnp.int32(z * experts)])
        return pl.pallas_call(
            body,
            out_shape=outs,
            in_specs=[smem] + ins,
            out_specs=jax.tree.map(lambda v: anywhere if v is rows_shape else vmem, outs),
            scratch_shapes=scratch,
            compiler_params=pltpu.CompilerParams(vmem_limit_bytes=VMEM_LIMIT),
            cost_estimate=pl.CostEstimate(flops=int(flops * COST * factor), bytes_accessed=int(moved * COST * factor), transcendentals=0),
            name=name,
        )(info, *arrays)

    loaded = pl.pallas_call(
        pack_kernel,
        out_shape=sds((tok + ROUTE_ROWS, width), BF16),
        in_specs=[smem] + [vmem] * 4,
        out_specs=vmem,
        name="pack",
    )(jnp.stack([p]).astype(jnp.int32), tokens, expert_ids.T, slots.T, gates.T)
    x_own = [turn(loaded, d) for d in range(zs)]
    out_grad, _ = lax.optimization_barrier((out_grad, loaded))
    y_here = turn(out_grad, 0)
    *x_own, y_here = lax.optimization_barrier((*x_own, y_here))
    x_other = [flip(v, "sub") for v in x_own]
    wbytes = width * ff * 2
    flop = 2 * rows * width * ff
    dflop = 2 * experts * rows * all_tok * width
    cfg = (zs, tok, experts, rows, group)
    hot = pltpu.VMEM((group * rows, all_tok), BF16)
    tok_scratch = pltpu.VMEM((all_tok, width), BF16)

    def wide(count):
        return pltpu.VMEM((count, width, ff), BF16)

    def tall(count):
        return pltpu.VMEM((count, ff, width), BF16)

    place_shape = sds((experts, all_tok), F32)
    rows_shape = pltpu.HBM((half, rows, width), BF16)
    half_rows = pltpu.VMEM((half, rows, width), BF16)
    def pinned(*arrays):
        return tuple(pltpu.with_memory_space_constraint(v, pltpu.HBM) for v in arrays)

    weights = (anywhere, pinned(gate_weight, up_weight))
    down_weight, = pinned(down_weight)
    au_send, place, level = call(
        functools.partial(x_kernel, cfg, half),
        other0,
        s,
        [(anywhere, pinned(*x_own, *x_other)), weights],
        [sds((half, 2 * rows, ff), BF16), place_shape, place_shape],
        [tok_scratch, hot, pltpu.VMEM((2 * zs, ROUTE_ROWS, width), BF16), half_rows, wide(half), wide(half)]
        + [dma((2 * half,)), dma((4 * zs,))],
        2 * half * flop + dflop // 2,
        2 * half * wbytes,
        "x_first",
    )
    y_here, au_send = lax.optimization_barrier((y_here, au_send))
    y_own = [y_here] + [shift(y_here, d) for d in range(1, zs)]

    au_mine = call(
        functools.partial(x2_kernel, cfg, half),
        mine0,
        s,
        [(anywhere, pinned(*x_own, *x_other)), (vmem, (place,)), weights],
        sds((half, 2 * rows, ff), F32),
        [tok_scratch, hot, half_rows, wide(half), wide(half), dma((2 * half,)), dma((2 * zs,))],
        2 * half * flop + dflop // 2,
        2 * half * wbytes,
        "x_mine",
    )
    au_recv = flip(au_send, "dp")
    *y_own, au_mine = lax.optimization_barrier((*y_own, au_mine))
    y_other = [flip(v, "sub") for v in y_own]
    dh_first, yin = call(
        functools.partial(y_kernel, cfg, first),
        other0,
        s,
        [(anywhere, pinned(*y_own, *y_other)), (vmem, (place, level)), (anywhere, (down_weight,))],
        [sds((first, rows, ff), BF16), rows_shape],
        [tok_scratch, hot, half_rows, tall(first), dma((first,)), dma((2 * zs,)), dma],
        first * flop + dflop // 2,
        first * wbytes,
        "y_first",
    )

    yin, au_recv = lax.optimization_barrier((yin, au_recv))
    dh_rest = call(
        functools.partial(y2_kernel, first, rest),
        other0 + first,
        s,
        [(anywhere, pinned(yin, down_weight))],
        sds((rest, rows, ff), BF16),
        [pltpu.VMEM((rest, rows, width), BF16), tall(rest), dma((rest,)), dma((rest,))],
        rest * flop,
        rest * wbytes,
        "y_other",
    )
    place_y, dh_rest = lax.optimization_barrier((place, dh_rest))
    dh_mine = call(
        functools.partial(y3_kernel, cfg, half),
        mine0,
        s,
        [(anywhere, pinned(*y_own, *y_other)), (vmem, (place_y, level)), (anywhere, (down_weight,))],
        sds((half, rows, ff), F32),
        [tok_scratch, hot, half_rows, tall(half), dma((half,)), dma((2 * zs,))],
        half * flop + dflop // 2,
        half * wbytes,
        "y_mine",
    )
    dh_recv = [flip(v, "dp") for v in (dh_first, dh_rest)]
    scale = LOCAL_EXPERTS / (all_tok * TOPK)
    last = 0
    chunks = [(0, 0, first)] + [(1, at, n) for at, n in ((0, rest - last), (rest - last, last)) if n]
    back, scores = [], []

    def final_call(k, at, n):
        d, score = call(
            functools.partial(final_kernel, rows, scale, k * first + at, at),
            mine0,
            s,
            [(vmem, (au_mine, dh_mine, au_recv, dh_recv[k]))],
            [sds((n, 2 * rows, ff), BF16), sds((n, 1, ff), F32)],
            [],
            n * rows * ff * 40,
            n * rows * ff * 30,
            "final",
        )
        scores.append(score)
        sent = d
        back.append(flip(sent, "dp"))
        return d

    def parts_call(start, ds):
        counts = [d.shape[0] for d in ds]
        n = sum(counts)
        return call(
            functools.partial(mine_parts_kernel, rows, counts),
            mine0 + start,
            s,
            [(vmem, ds), weights],
            sds((n * rows, width), BF16),
            [wide(n), wide(n), dma((2 * n,))],
            2 * n * flop,
            2 * n * wbytes,
            "mine_parts",
            PART_COST,
        )

    given = [parts_call(0, [final_call(*chunks[0])])]
    dh_mine, given[0] = lax.optimization_barrier((dh_mine, given[0]))
    ds = []
    for chunk in chunks[1:]:
        ds.append(final_call(*chunk))
        dh_mine, ds[-1] = lax.optimization_barrier((dh_mine, ds[-1]))
    given.append(parts_call(first, ds))
    score = jnp.concatenate(scores, axis=0).reshape(half, ff)
    score_other = flip(score, "dp")
    acc_shape, zshape = (all_tok, width), (zs, tok, width)
    for k, (part, at, n) in enumerate(chunks):
        used, final = n + half * (k == 0), k == len(chunks) - 1
        given = call(
            functools.partial(combine_kernel, rows, zs, tok, half, part * first + at, n, final),
            other0,
            s,
            [(vmem, (back[k],)), weights, (vmem, (place, *given))],
            [sds(zshape, F32), sds(zshape, BF16)] if final else [sds(acc_shape, F32)],
            [wide(n), wide(n), pltpu.VMEM((n * rows, width), BF16), pltpu.VMEM((used * rows, all_tok), BF16)]
            + [dma((2 * n,))],
            2 * n * flop + 2 * used * rows * width * all_tok,
            2 * n * wbytes,
            "combine",
        )
        if k == len(chunks) - 2:
            *given, score_other = lax.optimization_barrier((*given, score_other))
            scores = jnp.concatenate(
                [jnp.where(p == 0, score, score_other), jnp.where(p == 0, score_other, score)], axis=0
            )
    keep, send = given
    summed = (keep + flip(send, "sub").astype(F32)).astype(BF16)
    total = turn(summed[0], 0).astype(F32)
    for d in range(1, zs):
        total = total + turn(summed[d], -d).astype(F32)
    return (scores, total.astype(BF16))


def solution(mesh):
    in_specs = (
        P(("dom", "expert", "dp"), "sub"),
        P(("dom", "expert", "dp"), "sub"),
        P(("dom", "expert", "dp"), None),
        P(("dom", "expert", "dp"), None),
        P(("dom", "expert", "dp"), None),
        P("expert", "dp", "sub"),
        P("expert", "dp", "sub"),
        P("expert", "sub", "dp"),
    )
    out_specs = (P(("dom", "expert"), "sub"), P(("dom", "expert", "dp"), "sub"))
    pairs = mesh.shape["dp"] == 2 and mesh.shape["sub"] == 2
    split = (LOCAL_EXPERTS // mesh.shape["expert"]) % 2 == 0
    local = stationary if pairs and split else gathered
    return jax.shard_map(local, mesh=mesh, in_specs=in_specs, out_specs=out_specs, check_vma=False)
```
